32 devices in a mesh: groups: 2 (over y), dp: 16 (over z, x, core).
Axes of the slice: x: 2, y: 2, z: 4, core: 2. Of those that a mesh axis runs over, the one named last changes fastest.
Arguments:
- acts: bfloat16 [8192, 5120], P(('groups', 'dp')), parts along dimension 0, may hold values from -6 to 6
- cotan: bfloat16 [8192, 1024], P(('groups', 'dp')), parts along dimension 0, may hold values from -4 to 4
- frozen_key_weight: bfloat16 [5120, 1024], P('dp'), may hold values from -0.078125 to 0.078125
- adapter_down_slots: bfloat16 [64, 5120, 128], P(('groups', 'dp')), parts along dimension 0, may hold values from -0.078125 to 0.078125
- adapter_up_slots: bfloat16 [64, 128, 1024], P(('groups', 'dp')), parts along dimension 0, may hold values from -0.5 to 0.5
- token_row_jobs: int32 [8192, 1], P(('groups', 'dp')), parts along dimension 0, may hold values from 0 to 31; in each aligned block of 256 rows (0 to 255, 256 to 511, ...) at most 16 rows name the same one
- slot_owner_jobs: int32 [64], P('groups'), parts along dimension 0, may hold values from 0 to 31, each once
- loss_token_count: int32 [64], P('groups'), parts along dimension 0, may hold values from 128 to 1023
Outputs:
- grad_acts: bfloat16 [8192, 5120], P(('groups', 'dp')), parts along dimension 0
- grad_a: bfloat16 [64, 5120, 128], P(('groups', 'dp')), parts along dimension 0
- grad_b: bfloat16 [64, 128, 1024], P(('groups', 'dp')), parts along dimension 0
The draws below stay inside these ranges and needn't reach their ends.
There are 2 independent parts, one for each index of `groups`. The reference program is written for one: setup_inputs(seed, part) draws one part's arguments, and reference() takes and returns one part's arrays. A program takes and returns all parts, laid end to end along the dimension named above; an argument that names none is the same for every part. Nothing has to cross between parts.
Inputs may be any that keep to these rules, and one draw needn't show every extreme that they name: `token_row_jobs`: among the rows of one device no job is named by more than 16 rows, a bound that some block reaches; every job is named by some row. `slot_owner_jobs`: each job appears once; slot s lies on index s // 2 of dp.
All inputs are finite; a program needn't handle non-finite values.
Results may differ from the reference program's by a relative error of at most 0.0059.
Values may be sent and summed in bfloat16 or wider, within the bound.
No kernel may reach another device: no remote copies, remote signals or barrier semaphores. Data moves between devices by JAX's collectives and lax.ppermute only.
A program may use at most 128 MiB of HBM per device.

```python
import math
import jax
import jax.numpy as jnp
import numpy as np
from jax import lax

MODEL_WIDTH = 5120
KEY_WIDTH = 1024
ADAPTER_RANK = 128
TOK_DEV = 256
JOB_COUNT = 32
SEQUENCE_ITEMS = 4096
MOST = 16
N_DP = 16


def with_ends(entries, rng, least, high):
    shape = entries.shape
    place = [jax.random.randint(jax.random.fold_in(rng, axis), (), 0, shape[axis]) for axis in range(len(shape))]
    entries = entries.at[tuple(place)].set(least)
    longest = shape.index(max(shape))
    place[longest] = (place[longest] + 1) % shape[longest]
    return entries.at[tuple(place)].set(high)


def block_levels(key, dims, split, least, high):
    def one(axis_at, parts):
        draws = jax.random.uniform(jax.random.fold_in(jax.random.fold_in(key, 6), axis_at), (parts,), jnp.float32, least / len(split), high / len(split))
        return jnp.repeat(jnp.exp(draws), dims[axis_at] // parts).reshape((-1,) + (1,) * (len(dims) - axis_at - 1))

    loudness = one(*split[0])
    for cut in split[1:]:
        loudness = loudness * one(*cut)
    return loudness


def deal_out(stream_key, own, number, rows, number_of, top, bound, lean):
    sequence = jax.random.permutation(stream_key, number_of)
    crowded, ordinary = load_shares(number_of, rows * top, bound, lean, True), load_shares(number_of, rows * top, bound, lean, False)
    places = jnp.arange(number_of)

    def named(tallies, rotation):
        used = int((tallies > 0).sum())
        fixed = max(1, used // 4)
        passed = fixed + (places - fixed + rotation * (used - fixed)) % max(1, number_of - fixed)
        return jnp.zeros((number_of,), jnp.int32).at[sequence[jnp.where(places < fixed, places, passed)]].set(jnp.asarray(tallies, jnp.int32))

    tallies = jnp.where(number % 4 == 0, named(crowded, number // 4), named(ordinary, number - number // 4 - 1))
    mixed = jax.random.permutation(jax.random.fold_in(own, 3), number_of)
    giver, sink = mixed[0:number_of // 2 * 2:2], mixed[1:number_of // 2 * 2:2]
    room = jnp.minimum(tallies[giver] - 1, bound - tallies[sink]) // 2
    room = jnp.where((giver == sequence[0]) | (sink == sequence[0]) | (tallies[sink] == 0), 0, jnp.maximum(room, 0))
    passed = jax.random.randint(jax.random.fold_in(own, 4), (number_of // 2,), 0, 1 << 20) % (room + 1)
    tallies = tallies.at[giver].add(-passed).at[sink].add(passed)
    members = jnp.searchsorted(jnp.cumsum(tallies), jnp.arange(rows * top), side="right").astype(jnp.int32)
    grid = members.reshape(top, rows).T
    grid = grid[jax.random.permutation(jax.random.fold_in(own, 1), rows)]
    rotation = jax.random.randint(jax.random.fold_in(own, 2), (rows, 1), 0, top)
    return jnp.take_along_axis(grid, (jnp.arange(top)[None, :] + rotation) % top, axis=1)


def load_shares(number_of, total, limit, lean, full):
    portions = [(1 << 20) // math.isqrt(rank ** lean) + 1 for rank in range(1, number_of + 1)]
    largest = limit if full else min(limit, max(-(-total // number_of), total * portions[0] // sum(portions)))
    least = 1 if total - largest >= number_of - 1 else 0
    counts, surplus = [largest] + [least] * (number_of - 1), total - largest - least * (number_of - 1)
    while surplus > 0:
        movable = [i for i in range(1, number_of) if counts[i] < largest] or [i for i in range(1, number_of) if counts[i] < limit]
        mass, remaining = sum([portions[i] for i in movable]), surplus
        for i in movable:
            addition = min(limit - counts[i], max(1, remaining * portions[i] // mass), surplus)
            counts[i] = counts[i] + addition
            surplus = surplus - addition
    return np.array(counts)


def gaussian(own_key, extent, deviation, reach, shards=(), held_as=jnp.bfloat16):
    entries = deviation * jax.random.normal(own_key, extent, jnp.float32)
    if shards:
        entries = entries * block_levels(own_key, extent, shards, -0.22, 0.18)
    return jnp.clip(entries, -reach, reach).astype(held_as)


def setup_inputs(seed: int = 0, part: int = 0) -> dict:
    seeds = jax.random.split(jax.random.key(seed), 9)
    part_splits = jax.random.split(jax.random.fold_in(seeds[8], part), 9)
    acts = gaussian(part_splits[0], (SEQUENCE_ITEMS, MODEL_WIDTH), 1.0, 6.0, ((0, 16),))
    cotan = gaussian(part_splits[1], (SEQUENCE_ITEMS, KEY_WIDTH), 0.3, 4.0, ((0, 16),))
    frozen_key_weight = gaussian(seeds[2], (MODEL_WIDTH, KEY_WIDTH), MODEL_WIDTH ** -0.5, 0.078125, ((0, 16),))
    adapter_down_slots = gaussian(part_splits[3], (JOB_COUNT, MODEL_WIDTH, ADAPTER_RANK), MODEL_WIDTH ** -0.5, 0.078125, ((0, 16),))
    adapter_up_slots = gaussian(part_splits[4], (JOB_COUNT, ADAPTER_RANK, KEY_WIDTH), ADAPTER_RANK ** -0.5, 0.5, ((0, 16),))
    token_row_jobs_keys = jax.random.split(jax.random.fold_in(part_splits[5], 1), SEQUENCE_ITEMS // TOK_DEV)
    token_row_jobs_turns = jax.random.permutation(jax.random.fold_in(part_splits[5], 3), SEQUENCE_ITEMS // TOK_DEV)
    token_row_jobs = jax.vmap(lambda own, number: deal_out(jax.random.fold_in(part_splits[5], 2), own, number, TOK_DEV, JOB_COUNT, 1, MOST, 2))(token_row_jobs_keys, token_row_jobs_turns).reshape((SEQUENCE_ITEMS, 1))
    slot_owner_jobs = jax.random.permutation(part_splits[6], JOB_COUNT).astype(jnp.int32)
    loss_token_count = with_ends(jax.random.randint(part_splits[7], (JOB_COUNT,), 128, 1024), jax.random.fold_in(part_splits[7], 1), 128, 1023).astype(jnp.int32)
    return {"acts": acts, "cotan": cotan, "frozen_key_weight": frozen_key_weight, "adapter_down_slots": adapter_down_slots, "adapter_up_slots": adapter_up_slots, "token_row_jobs": token_row_jobs, "slot_owner_jobs": slot_owner_jobs, "loss_token_count": loss_token_count}


DELTA_MULTIPLIER = 0.25


def ranks_of(row_ids):
    same = row_ids[:, None] == row_ids[None, :]
    earlier = jnp.arange(TOK_DEV)[None, :] < jnp.arange(TOK_DEV)[:, None]
    return jnp.sum(jnp.where(same & earlier, 1, 0), axis=1).astype(jnp.int32)


def reference(acts, cotan, frozen_key_weight, adapter_down_slots, adapter_up_slots, token_row_jobs, slot_owner_jobs, loss_token_count):
    ids = token_row_jobs[:, 0]
    lengths = loss_token_count.astype(jnp.float32)
    weights = jnp.mean(lengths) / lengths
    scaled = (weights[ids][:, None] * cotan.astype(jnp.float32)).astype(jnp.bfloat16)
    base_grad = lax.dot_general(scaled, frozen_key_weight, (((1,), (1,)), ((), ())), preferred_element_type=jnp.float32)
    slot_of = jnp.zeros((JOB_COUNT,), jnp.int32).at[slot_owner_jobs].set(jnp.arange(JOB_COUNT, dtype=jnp.int32))
    ranks = jax.vmap(ranks_of)(ids.reshape(N_DP, TOK_DEV)).reshape(-1)
    device = (jnp.arange(SEQUENCE_ITEMS) // TOK_DEV).astype(jnp.int32)
    per_job = N_DP * MOST
    position = slot_of[ids] * per_job + device * MOST + ranks
    sources = jnp.full((JOB_COUNT * per_job,), SEQUENCE_ITEMS, jnp.int32).at[position].set(jnp.arange(SEQUENCE_ITEMS, dtype=jnp.int32))
    acts_pad = jnp.concatenate([acts, jnp.zeros((1, MODEL_WIDTH), acts.dtype)], axis=0)
    scaled_pad = jnp.concatenate([scaled, jnp.zeros((1, KEY_WIDTH), scaled.dtype)], axis=0)

    def one_slot(carry, slot_index):
        rows = lax.dynamic_slice_in_dim(sources, (slot_index * per_job).astype(jnp.int32), per_job)
        left_operand = acts_pad[rows]
        second_factor_input = scaled_pad[rows]
        down_matrix = adapter_down_slots[slot_index]
        expansion_factor = adapter_up_slots[slot_index]
        thin_update_carry = jnp.dot(left_operand, down_matrix, preferred_element_type=jnp.float32).astype(jnp.bfloat16)
        thin_update_reverse_pass = (DELTA_MULTIPLIER * jnp.dot(second_factor_input, expansion_factor.T, preferred_element_type=jnp.float32)).astype(jnp.bfloat16)
        grad_down = jnp.dot(left_operand.T, thin_update_reverse_pass, preferred_element_type=jnp.float32).astype(jnp.bfloat16)
        expansion_factor_cotangent = (DELTA_MULTIPLIER * jnp.dot(thin_update_carry.T, second_factor_input, preferred_element_type=jnp.float32)).astype(jnp.bfloat16)
        term = jnp.dot(thin_update_reverse_pass, down_matrix.T, preferred_element_type=jnp.float32).astype(jnp.bfloat16)
        term = lax.optimization_barrier(term).astype(jnp.float32)
        return carry.at[rows].add(term), (grad_down, expansion_factor_cotangent)

    start = jnp.zeros((SEQUENCE_ITEMS + 1, MODEL_WIDTH), jnp.float32)
    adapter_grad, grads = lax.scan(one_slot, start, jnp.arange(JOB_COUNT, dtype=jnp.int32))
    grad_acts = (base_grad + adapter_grad[:SEQUENCE_ITEMS]).astype(jnp.bfloat16)
    return grad_acts, grads[0], grads[1]
```

```python
import functools

import jax
import jax.numpy as jnp
from jax import lax
from jax.experimental import pallas as pl
from jax.experimental.pallas import tpu as pltpu
from jax.sharding import PartitionSpec as P

DELTA_MULTIPLIER = 0.25
BF = jnp.bfloat16
F32 = jnp.float32
PLANES = 4
PIECES = 4
PARAMS = pltpu.CompilerParams(vmem_limit_bytes=48 * 1024 * 1024)


def whole(shape):
    zeros = (0,) * len(shape)
    return pl.BlockSpec(shape, lambda i: zeros)


def dot(a, b, ca=1, cb=0):
    return lax.dot_general(a, b, (((ca,), (cb,)), ((), ())), preferred_element_type=F32)


def route_body(count, rows_ref, *refs):
    ins, outs = refs[:count], refs[count:]
    held = ins[0][...] if count == 1 else jnp.concatenate([r[...] for r in ins], axis=0)
    moved = dot(rows_ref[...], held).astype(BF)
    at = 0
    for out in outs:
        out[...] = moved[at : at + out.shape[0]]
        at += out.shape[0]


def route(rows, ins, outs, piece=None):
    width = ins[0].shape[1]
    specs = [whole(x.shape) for x in ins]
    if piece is not None:
        at, of = piece
        width = width // of
        specs = [pl.BlockSpec((ins[0].shape[0], width), lambda i: (0, at))]
    shapes = [(n, width) for n in outs]
    return pl.pallas_call(
        functools.partial(route_body, len(ins)),
        grid=(1,),
        in_specs=[whole(rows.shape)] + specs,
        out_specs=[whole(s) for s in shapes],
        out_shape=[jax.ShapeDtypeStruct(s, BF) for s in shapes],
        compiler_params=PARAMS,
    )(rows, *ins)


def back_body(count, up_ref, *refs):
    ins, out = refs[:count], refs[count]
    for job in range(up_ref.shape[0]):
        held = jnp.concatenate([r[job] for r in ins], axis=0)
        out[job] = (DELTA_MULTIPLIER * dot(held, up_ref[job], 1, 1)).astype(BF)


def back_project(up, ins):
    local, depth = up.shape[0], up.shape[1]
    shape = (local, sum(x.shape[1] for x in ins), depth)
    return pl.pallas_call(
        functools.partial(back_body, len(ins)),
        grid=(1,),
        in_specs=[whole(up.shape)] + [whole(x.shape) for x in ins],
        out_specs=whole(shape),
        out_shape=jax.ShapeDtypeStruct(shape, BF),
        compiler_params=PARAMS,
    )(up, *ins)


def term_body(back_ref, down_ref, *outs):
    for job in range(down_ref.shape[0]):
        term = dot(back_ref[job], down_ref[job], 1, 1).astype(BF)
        at = 0
        for out in outs:
            out[job] = term[at : at + out.shape[1]]
            at += out.shape[1]


def adapter_terms(back_low, down, piece, outs):
    at, of = piece
    local, width, rank = down.shape
    width = width // of
    shapes = [(local, n, width) for n in outs]
    return pl.pallas_call(
        term_body,
        grid=(1,),
        in_specs=[
            whole(back_low.shape),
            pl.BlockSpec((local, width, rank), lambda i: (0, at, 0)),
        ],
        out_specs=[whole(s) for s in shapes],
        out_shape=[jax.ShapeDtypeStruct(s, BF) for s in shapes],
        compiler_params=PARAMS,
    )(back_low, down)


def owner_body(count, carried, back_ref, down_ref, *refs):
    ins = refs[:count]
    refs = refs[count:]
    if carried:
        low_in, _, low_ref, grad_ref = refs
    else:
        low_ref, grad_ref = refs
    for job in range(down_ref.shape[0]):
        held = jnp.concatenate([r[job] for r in ins], axis=0)
        low = dot(held, down_ref[job])
        low_ref[job] = low_in[job] + low if carried else low
        grad_ref[job] = dot(held, back_ref[job], 0, 0).astype(BF)


def owner_step(back_low, down, ins, piece, carry):
    at, of = piece
    local, width, rank = down.shape
    part = pl.BlockSpec((local, width // of, rank), lambda i: (0, at, 0))
    low_shape = (local, back_low.shape[1], rank)
    extra, extra_specs, aliases = [], [], {}
    if carry is not None:
        extra = list(carry)
        extra_specs = [whole(low_shape), pl.BlockSpec(memory_space=pl.ANY)]
        aliases = {2 + len(ins): 0, 3 + len(ins): 1}
    return pl.pallas_call(
        functools.partial(owner_body, len(ins), carry is not None),
        grid=(1,),
        in_specs=[whole(back_low.shape), part] + [whole(x.shape) for x in ins] + extra_specs,
        out_specs=[whole(low_shape), part],
        out_shape=[
            jax.ShapeDtypeStruct(low_shape, F32),
            jax.ShapeDtypeStruct(down.shape, BF),
        ],
        input_output_aliases=aliases,
        compiler_params=PARAMS,
    )(back_low, down, *ins, *extra)


def up_body(count, low_ref, *refs):
    ins, out = refs[:count], refs[count]
    for job in range(low_ref.shape[0]):
        held = jnp.concatenate([r[job] for r in ins], axis=0)
        low = low_ref[job].astype(BF)
        out[job] = (DELTA_MULTIPLIER * dot(low, held, 0, 0)).astype(BF)


def up_gradient(low, ins):
    shape = (low.shape[0], low.shape[2], ins[0].shape[2])
    return pl.pallas_call(
        functools.partial(up_body, len(ins)),
        grid=(1,),
        in_specs=[whole(low.shape)] + [whole(x.shape) for x in ins],
        out_specs=whole(shape),
        out_shape=jax.ShapeDtypeStruct(shape, BF),
        compiler_params=PARAMS,
    )(low, *ins)


def final_body(count, scaled_ref, weight_ref, rows_ref, *refs):
    ins, out = refs[:count], refs[-1]
    held = jnp.concatenate([r[...] for r in ins], axis=0)
    base = dot(scaled_ref[...], weight_ref[...], 1, 1)
    out[...] = (base + dot(rows_ref[...], held)).astype(BF)


def final_step(scaled, weight, rows, ins, piece, carry):
    at, of = piece
    width = weight.shape[0] // of
    extra = [] if carry is None else [carry]
    return pl.pallas_call(
        functools.partial(final_body, len(ins)),
        grid=(1,),
        in_specs=[
            whole(scaled.shape),
            pl.BlockSpec((width, weight.shape[1]), lambda i: (at, 0)),
            whole(rows.shape),
        ]
        + [whole(x.shape) for x in ins]
        + [pl.BlockSpec(memory_space=pl.ANY)] * len(extra),
        out_specs=pl.BlockSpec((scaled.shape[0], width), lambda i: (0, at)),
        out_shape=jax.ShapeDtypeStruct((scaled.shape[0], weight.shape[0]), BF),
        input_output_aliases={} if carry is None else {3 + len(ins): 0},
        compiler_params=PARAMS,
    )(scaled, weight, rows, *ins, *extra)


def shards(
    acts,
    cotan,
    frozen_key_weight,
    adapter_down_slots,
    adapter_up_slots,
    token_row_jobs,
    slot_owner_jobs,
    loss_token_count,
):
    devices = lax.axis_size("dp")
    parts = lax.axis_size("groups")
    tok_rows = acts.shape[0]
    local = adapter_down_slots.shape[0]
    jobs_all = slot_owner_jobs.shape[0]
    depth = 2 * tok_rows // (local * devices)
    column = devices // PLANES
    ring = column <= 4
    most = local * column * depth
    segment = PLANES * depth
    me = lax.axis_index("dp")
    plane, place = me // column, me % column

    ids = token_row_jobs[:, 0]
    lengths = loss_token_count.astype(F32)
    weights = jnp.mean(lengths) / lengths
    numbers = jnp.arange(jobs_all, dtype=jnp.int32)
    row_weight = jnp.sum(jnp.where(ids[:, None] == numbers[None, :], weights[None, :], 0.0), axis=1)
    row_slot = jnp.sum(
        jnp.where(ids[:, None] == slot_owner_jobs[None, :], numbers[None, :], 0), axis=1
    )
    scaled = (row_weight[:, None] * cotan.astype(F32)).astype(BF)

    planes = jnp.arange(PLANES, dtype=jnp.int32)
    need = jnp.max(
        jnp.sum((row_slot[:, None] // (local * column) == planes[None, :]).astype(jnp.int32), axis=0)
    )
    note = jnp.concatenate([row_slot, jnp.full((128,), need, jnp.int32)])
    notes = lax.all_to_all(
        jnp.broadcast_to(note[None, None], (parts * devices, 1, tok_rows + 128)),
        ("groups", "dp"),
        split_axis=0,
        concat_axis=0,
        tiled=True,
    )[:, 0]
    need_all = jnp.max(notes[:, tok_rows])
    mine = notes[:, :tok_rows].reshape(parts, PLANES, column, tok_rows)
    mine = lax.dynamic_index_in_dim(mine, lax.axis_index("groups"), 0, keepdims=False)
    mine = lax.dynamic_index_in_dim(mine, place, 1, keepdims=False)
    there = planes ^ plane
    slots = jnp.sum(
        jnp.where(there[:, None, None] == planes[None, :, None], mine[None], 0), axis=1
    )
    slots = jnp.concatenate([row_slot[None], slots[1:]], axis=0)
    goal = slots // (local * column)
    earlier = jnp.arange(tok_rows)[None, :] < jnp.arange(tok_rows)[:, None]
    order = jnp.sum(
        ((goal[:, :, None] == goal[:, None, :]) & earlier[None]).astype(jnp.int32), axis=2
    )
    rank = jnp.sum(
        ((slots[:, :, None] == slots[:, None, :]) & earlier[None]).astype(jnp.int32), axis=2
    )
    owner = (slots // local) % column
    if ring:
        owner = owner ^ place
    spot = (
        owner * (local * segment)
        + (slots % local) * segment
        + planes[:, None] * depth
        + rank
    )
    spot = jnp.where(goal == plane, spot, -1)
    side = goal[0] ^ plane

    def across(bufs):
        return [bufs[0]] + [
            lax.ppermute(
                bufs[s],
                "dp",
                [(d, ((d // column) ^ s) * column + d % column) for d in range(devices)],
            )
            for s in range(1, PLANES)
        ]

    blocks = [[p * column + c for c in range(column)] for p in range(PLANES)]

    def within(x):
        return lax.all_to_all(
            x, "dp", split_axis=0, concat_axis=0, tiled=True, axis_index_groups=blocks
        )

    def near(bufs):
        return [bufs[0]] + [
            lax.ppermute(bufs[s], "dp", [(d, d ^ s) for d in range(devices)])
            for s in range(1, column)
        ]

    spread_outs = [local * segment] * column if ring else [column * local * segment]
    owner_outs = [segment] * column if ring else [column * segment]

    def to_owner(bufs):
        width = bufs[0].shape[1]
        if ring:
            return [x.reshape(local, segment, width) for x in near(bufs)]
        x = within(bufs[0]).reshape(column, local, segment, width)
        return [x.transpose(1, 0, 2, 3).reshape(local, column * segment, width)]

    def from_owner(bufs):
        width = bufs[0].shape[2]
        if ring:
            return near([x.reshape(local * segment, width) for x in bufs])
        x = bufs[0].reshape(local, column, segment, width).transpose(1, 0, 2, 3)
        return [within(x.reshape(column * local * segment, width))]

    def run(size):
        total = PLANES * size
        lanes = jnp.arange(total, dtype=jnp.int32)
        code = side * size + order[0]
        out_rows = (lanes[:, None] == code[None, :]).astype(BF)
        back_rows = (code[:, None] == lanes[None, :]).astype(BF)
        kth = jnp.arange(size, dtype=jnp.int32)
        target = jnp.sum(
            jnp.where(
                (order[:, None, :] == kth[None, :, None]) & (spot[:, None, :] >= 0),
                spot[:, None, :] + 1,
                0,
            ),
            axis=2,
        ).reshape(total) - 1
        spots = jnp.arange(PLANES * most, dtype=jnp.int32)
        spread = (spots[:, None] == target[None, :]).astype(BF)
        gather = (target[:, None] == spots[None, :]).astype(BF)
        sizes = [size] * PLANES

        weight = lax.all_gather(frozen_key_weight, "dp", axis=0, tiled=True)

        def outward(x, piece=None):
            there = across(route(out_rows, [x], sizes, piece))
            return to_owner(route(spread, there, spread_outs))

        got_scaled = outward(scaled)
        back_low = back_project(adapter_up_slots, got_scaled)
        low_grad, result = None, None
        for at in range(PIECES):
            piece = (at, PIECES)
            got = outward(acts, piece)
            terms = adapter_terms(back_low, adapter_down_slots, piece, owner_outs)
            home = across(route(gather, from_owner(terms), sizes))
            low_grad = owner_step(back_low, adapter_down_slots, got, piece, low_grad)
            result = final_step(scaled, weight, back_rows, home, piece, result)
        low, grad_a = low_grad
        grad_b = up_gradient(low, got_scaled)
        return result, grad_a, grad_b

    steps = [most * 5 // 8, most * 3 // 4, most]
    which = sum((need_all > s).astype(jnp.int32) for s in steps[:-1])
    return lax.switch(which, [functools.partial(run, s) for s in steps])


def solution(mesh):
    return jax.shard_map(
        shards,
        mesh=mesh,
        in_specs=(
            P(("groups", "dp"), None),
            P(("groups", "dp"), None),
            P("dp", None),
            P(("groups", "dp"), None, None),
            P(("groups", "dp"), None, None),
            P(("groups", "dp"), None),
            P("groups"),
            P("groups"),
        ),
        out_specs=(
            P(("groups", "dp"), None),
            P(("groups", "dp"), None, None),
            P(("groups", "dp"), None, None),
        ),
        check_vma=False,
    )
```

```python
import functools

import jax
import jax.numpy as jnp
from jax import lax
from jax.experimental import pallas as pl
from jax.experimental.pallas import tpu as pltpu
from jax.sharding import PartitionSpec as P

DELTA_MULTIPLIER = 0.25
BF = jnp.bfloat16
F32 = jnp.float32
PLANES = 4
PIECES = 4
PARAMS = pltpu.CompilerParams(vmem_limit_bytes=48 * 1024 * 1024)


def whole(shape):
    zeros = (0,) * len(shape)
    return pl.BlockSpec(shape, lambda i: zeros)


def dot(a, b, ca=1, cb=0):
    return lax.dot_general(a, b, (((ca,), (cb,)), ((), ())), preferred_element_type=F32)


HERE = pl.BlockSpec(memory_space=pl.ANY)
FAR = pl.BlockSpec(memory_space=pltpu.HBM)


def route_body(count, rows_ref, *refs):
    ins, outs = refs[:count], refs[count:]
    held = ins[0][...] if count == 1 else jnp.concatenate([r[...] for r in ins], axis=0)
    moved = dot(rows_ref[...], held).astype(BF)
    at = 0
    for out in outs:
        out[...] = moved[at : at + out.shape[0]]
        at += out.shape[0]


class Line:
    def __init__(self):
        self.last = []

    def call(self, body, operands, in_specs, out_specs, out_shape, aliases=None):
        after = self.last
        first = len(operands)

        def kernel(*refs):
            return body(*refs[:first], *refs[first + len(after) :])

        out = pl.pallas_call(
            kernel,
            grid=(1,),
            in_specs=in_specs + [HERE] * len(after),
            out_specs=out_specs,
            out_shape=out_shape,
            input_output_aliases=aliases or {},
            cost_estimate=pl.CostEstimate(flops=1, bytes_accessed=1, transcendentals=0),
            compiler_params=PARAMS,
        )(*operands, *after)
        self.last = [out[0] if isinstance(out, (list, tuple)) else out]
        return out


def hold_body(ref, out):
    pass


def hold(line, x):
    last = line.last
    out = line.call(hold_body, [x], [FAR], FAR, jax.ShapeDtypeStruct(x.shape, x.dtype), {0: 0})
    line.last = last
    return out


def route(line, rows, ins, outs, piece=None):
    width = ins[0].shape[1]
    specs = [whole(x.shape) for x in ins]
    if piece is not None:
        at, of = piece
        width = width // of
        specs = [pl.BlockSpec((ins[0].shape[0], width), lambda i: (0, at))]
    shapes = [(n, width) for n in outs]
    return line.call(
        functools.partial(route_body, len(ins)),
        [rows, *ins],
        [whole(rows.shape)] + specs,
        [whole(x) for x in shapes],
        [jax.ShapeDtypeStruct(x, BF) for x in shapes],
    )


def job_rows(refs, job):
    return jnp.concatenate([ref[job] for ref in refs], axis=0)


def back_body(count, up_ref, *refs):
    out = refs[count]
    for job in range(up_ref.shape[0]):
        held = job_rows(refs[:count], job)
        out[job] = (DELTA_MULTIPLIER * dot(held, up_ref[job], 1, 1)).astype(BF)


def back_project(line, up, rows):
    local, rank = up.shape[0], up.shape[1]
    shape = (local, sum(x.shape[1] for x in rows), rank)
    return line.call(
        functools.partial(back_body, len(rows)),
        [up, *rows],
        [whole(up.shape)] + [whole(x.shape) for x in rows],
        whole(shape),
        jax.ShapeDtypeStruct(shape, BF),
    )


def term_body(back_ref, down_ref, *outs):
    for job in range(down_ref.shape[0]):
        term = dot(back_ref[job], down_ref[job], 1, 1).astype(BF)
        at = 0
        for out in outs:
            out[job] = term[at : at + out.shape[1]]
            at += out.shape[1]


def adapter_terms(line, back_low, down, piece, outs):
    at, of = piece
    local, width, rank = down.shape
    width = width // of
    shapes = [(local, n, width) for n in outs]
    return line.call(
        term_body,
        [back_low, down],
        [whole(back_low.shape), pl.BlockSpec((local, width, rank), lambda i: (0, at, 0))],
        [whole(x) for x in shapes],
        [jax.ShapeDtypeStruct(x, BF) for x in shapes],
    )


def owner_body(count, carried, back_ref, down_ref, *refs):
    ins, refs = refs[:count], refs[count:]
    if carried:
        low_in, _, low_ref, grad_ref = refs
    else:
        low_ref, grad_ref = refs
    for job in range(down_ref.shape[0]):
        held = job_rows(ins, job)
        low = dot(held, down_ref[job])
        low_ref[job] = low_in[job] + low if carried else low
        grad_ref[job] = dot(held, back_ref[job], 0, 0).astype(BF)


def owner_step(line, back_low, down, rows, piece, carry):
    at, of = piece
    local, width, rank = down.shape
    part = pl.BlockSpec((local, width // of, rank), lambda i: (0, at, 0))
    low_shape = (local, back_low.shape[1], rank)
    extra, extra_specs, aliases = [], [], {}
    if carry is not None:
        extra = list(carry)
        extra_specs = [whole(low_shape), FAR]
        aliases = {2 + len(rows): 0, 3 + len(rows): 1}
    return line.call(
        functools.partial(owner_body, len(rows), carry is not None),
        [back_low, down, *rows, *extra],
        [whole(back_low.shape), part] + [whole(x.shape) for x in rows] + extra_specs,
        [whole(low_shape), part],
        [jax.ShapeDtypeStruct(low_shape, F32), jax.ShapeDtypeStruct(down.shape, BF)],
        aliases,
    )


def up_body(count, low_ref, *refs):
    out = refs[count]
    for job in range(low_ref.shape[0]):
        low = low_ref[job].astype(BF)
        held = job_rows(refs[:count], job)
        out[job] = (DELTA_MULTIPLIER * dot(low, held, 0, 0)).astype(BF)


def up_gradient(line, low, rows):
    shape = (low.shape[0], low.shape[2], rows[0].shape[2])
    return line.call(
        functools.partial(up_body, len(rows)),
        [low, *rows],
        [whole(low.shape)] + [whole(x.shape) for x in rows],
        whole(shape),
        jax.ShapeDtypeStruct(shape, BF),
    )


def final_body(count, scaled_ref, weight_ref, rows_ref, *refs):
    ins, out = refs[:count], refs[-1]
    held = jnp.concatenate([r[...] for r in ins], axis=0)
    weight = weight_ref[...].reshape(-1, weight_ref.shape[-1])
    base = dot(scaled_ref[...], weight, 1, 1)
    out[...] = (base + dot(rows_ref[...], held)).astype(BF)


def final_step(line, scaled, weight, rows, ins, piece, carry):
    at, of = piece
    column, parts, planes, share, deep = weight.shape
    width = column * parts * planes * share // of
    extra = [] if carry is None else [carry]
    return line.call(
        functools.partial(final_body, len(ins)),
        [scaled, weight, rows, *ins, *extra],
        [
            whole(scaled.shape),
            pl.BlockSpec((column, parts, planes // of, share, deep), lambda i: (0, 0, at, 0, 0)),
            whole(rows.shape),
        ]
        + [whole(x.shape) for x in ins]
        + [FAR] * len(extra),
        pl.BlockSpec((scaled.shape[0], width), lambda i: (0, at)),
        jax.ShapeDtypeStruct((scaled.shape[0], width * of), BF),
        {} if carry is None else {3 + len(ins): 0},
    )


def shards(
    acts,
    cotan,
    frozen_key_weight,
    adapter_down_slots,
    adapter_up_slots,
    token_row_jobs,
    slot_owner_jobs,
    loss_token_count,
):
    devices = lax.axis_size("dp")
    parts = lax.axis_size("groups")
    tok_rows = acts.shape[0]
    local = adapter_down_slots.shape[0]
    jobs_all = slot_owner_jobs.shape[0]
    depth = 2 * tok_rows // (local * devices)
    column = devices // PLANES
    ring = column <= 4
    most = local * column * depth
    segment = PLANES * depth
    me = lax.axis_index("dp")
    plane, place = me // column, me % column

    ids = token_row_jobs[:, 0]
    lengths = loss_token_count.astype(F32)
    weights = jnp.mean(lengths) / lengths
    numbers = jnp.arange(jobs_all, dtype=jnp.int32)
    row_weight = jnp.sum(jnp.where(ids[:, None] == numbers[None, :], weights[None, :], 0.0), axis=1)
    row_slot = jnp.sum(
        jnp.where(ids[:, None] == slot_owner_jobs[None, :], numbers[None, :], 0), axis=1
    )
    scaled = (row_weight[:, None] * cotan.astype(F32)).astype(BF)

    planes = jnp.arange(PLANES, dtype=jnp.int32)
    need = jnp.max(
        jnp.sum((row_slot[:, None] // (local * column) == planes[None, :]).astype(jnp.int32), axis=0)
    )
    note = jnp.concatenate([row_slot, jnp.full((128,), need, jnp.int32)])
    notes = lax.all_to_all(
        jnp.broadcast_to(note[None, None], (parts * devices, 1, tok_rows + 128)),
        ("groups", "dp"),
        split_axis=0,
        concat_axis=0,
        tiled=True,
    )[:, 0]
    need_all = jnp.max(notes[:, tok_rows])
    mine = notes[:, :tok_rows].reshape(parts, PLANES, column, tok_rows)
    mine = lax.dynamic_index_in_dim(mine, lax.axis_index("groups"), 0, keepdims=False)
    mine = lax.dynamic_index_in_dim(mine, place, 1, keepdims=False)
    there = planes ^ plane
    slots = jnp.sum(
        jnp.where(there[:, None, None] == planes[None, :, None], mine[None], 0), axis=1
    )
    slots = jnp.concatenate([row_slot[None], slots[1:]], axis=0)
    goal = slots // (local * column)
    earlier = jnp.arange(tok_rows)[None, :] < jnp.arange(tok_rows)[:, None]
    order = jnp.sum(
        ((goal[:, :, None] == goal[:, None, :]) & earlier[None]).astype(jnp.int32), axis=2
    )
    rank = jnp.sum(
        ((slots[:, :, None] == slots[:, None, :]) & earlier[None]).astype(jnp.int32), axis=2
    )
    owner = (slots // local) % column
    if ring:
        owner = owner ^ place
    spot = (
        owner * (local * segment)
        + (slots % local) * segment
        + planes[:, None] * depth
        + rank
    )
    spot = jnp.where(goal == plane, spot, -1)
    own_goal = row_slot // (local * column)
    own_order = jnp.sum(
        ((own_goal[:, None] == own_goal[None, :]) & earlier).astype(jnp.int32), axis=1
    )
    side = own_goal ^ plane

    def across(bufs):
        return [bufs[0]] + [
            lax.ppermute(
                bufs[s],
                "dp",
                [(d, ((d // column) ^ s) * column + d % column) for d in range(devices)],
            )
            for s in range(1, PLANES)
        ]

    blocks = [[p * column + c for c in range(column)] for p in range(PLANES)]

    def within(x):
        return lax.all_to_all(
            x, "dp", split_axis=0, concat_axis=0, tiled=True, axis_index_groups=blocks
        )

    blocks_out = [local * segment] * column if ring else [column * local * segment]
    owner_outs = [segment] * column if ring else [column * segment]

    def near(bufs):
        if not ring:
            return [within(bufs[0])]
        return [bufs[0]] + [
            lax.ppermute(bufs[s], "dp", [(d, d ^ s) for d in range(devices)])
            for s in range(1, column)
        ]

    def at_owner(bufs):
        width = bufs[0].shape[1]
        if ring:
            return [x.reshape(local, segment, width) for x in bufs]
        x = bufs[0].reshape(column, local, segment, width).transpose(1, 0, 2, 3)
        return [x.reshape(local, column * segment, width)]

    def from_owner(bufs):
        width = bufs[0].shape[2]
        if ring:
            return [x.reshape(local * segment, width) for x in bufs]
        x = bufs[0].reshape(local, column, segment, width).transpose(1, 0, 2, 3)
        return [x.reshape(column * local * segment, width)]

    stripes = [[p * column + c for p in range(PLANES)] for c in range(column)]

    share = frozen_key_weight.shape[0] // parts
    deep = frozen_key_weight.shape[1]
    own_share = lax.dynamic_slice_in_dim(
        frozen_key_weight, lax.axis_index("groups") * share, share, 0
    )

    def shape_weight(w):
        w = w.reshape(column, parts, PLANES, share, deep)
        if share % 16 == 0:
            return w
        w = w.transpose(2, 0, 1, 3, 4)
        return w.reshape(1, 1, PLANES, column * parts * share, deep)

    def outward(size):
        lanes = jnp.arange(PLANES * size, dtype=jnp.int32)
        code = side * size + own_order
        return (lanes[:, None] == code[None, :]).astype(BF), (
            code[:, None] == lanes[None, :]
        ).astype(BF)

    def inward(size):
        kth = jnp.arange(size, dtype=jnp.int32)
        target = jnp.sum(
            jnp.where(
                (order[:, None, :] == kth[None, :, None]) & (spot[:, None, :] >= 0),
                spot[:, None, :] + 1,
                0,
            ),
            axis=2,
        ).reshape(PLANES * size) - 1
        spots = jnp.arange(PLANES * most, dtype=jnp.int32)
        return (spots[:, None] == target[None, :]).astype(BF), (
            target[:, None] == spots[None, :]
        ).astype(BF)

    scaled_z = across(route(Line(), outward(most)[0], [scaled], [most] * PLANES))
    scaled_sent = route(Line(), inward(most)[0], scaled_z, blocks_out)

    def run(size):
        out_rows, back_rows = outward(size)
        spread, gather = inward(size)
        sizes = [size] * PLANES
        line = Line()
        pieces = [(at, PIECES) for at in range(PIECES)]

        def leave(at):
            return route(line, out_rows, [acts], sizes, pieces[at])

        def spread_out(bufs):
            return route(line, spread, bufs, blocks_out)

        def term(at):
            return from_owner(
                adapter_terms(line, back_low, adapter_down_slots, pieces[at], owner_outs)
            )

        def home(came):
            return route(line, gather, came, sizes)

        def own(at, got, carry):
            return owner_step(line, back_low, adapter_down_slots, at_owner(got), pieces[at], carry)

        def final(at, carry):
            return final_step(line, scaled, weight, back_rows, terms_z[at], pieces[at], carry)

        def fly(far, close):
            far, close = across(far) if far else [], near(close)
            return far, close, far[1:] + (close[1:] if ring else close)

        acts_z, acts_o, acts_x, terms_z, terms_x = {}, {}, {}, {}, {}
        weight = lax.all_gather(
            own_share, "dp", axis=0, tiled=True, axis_index_groups=stripes
        )
        out = leave(0)
        acts_z[0], got_scaled, landed = fly(out, scaled_sent)
        out = leave(1)
        line.last += landed
        got_scaled = at_owner(got_scaled)
        back_low = back_project(line, adapter_up_slots, got_scaled)
        terms_o = term(0)

        acts_z[1], terms_x[0], landed = fly(out, terms_o)
        acts_o[0] = spread_out(acts_z[0])
        terms_o = term(1)
        line.last += landed
        back = home(terms_x[0])

        terms_z[0], terms_x[1], landed = fly(back, terms_o)
        acts_o[1] = spread_out(acts_z[1])
        out = leave(2)
        weight = lax.all_gather(hold(line, weight), "groups", axis=0, tiled=True)
        line.last += landed
        back = home(terms_x[1])

        terms_z[1], acts_x[0], landed = fly(back, acts_o[0])
        terms_o = term(2)
        line.last += landed
        carry = own(0, acts_x[0], None)

        acts_z[2], terms_x[2], landed = fly(out, terms_o)
        out = leave(3)
        weight = lax.all_gather(
            hold(line, weight), "dp", axis=0, tiled=True, axis_index_groups=blocks
        )
        line.last += landed
        back = home(terms_x[2])
        terms_o = term(3)

        terms_z[2], acts_x[1], landed = fly(back, acts_o[1])
        acts_o[2] = spread_out(acts_z[2])
        line.last += landed
        carry = own(1, acts_x[1], carry)

        acts_z[3], terms_x[3], landed = fly(out, terms_o)
        line.last += landed
        back = home(terms_x[3])
        acts_o[3] = spread_out(acts_z[3])

        terms_z[3], acts_x[2], landed = fly(back, acts_o[2])
        weight = shape_weight(weight)
        result = final(0, None)
        result = final(1, result)
        line.last += landed
        carry = own(2, acts_x[2], carry)

        _, acts_x[3], landed = fly([], acts_o[3])
        result = final(2, result)
        result = final(3, result)
        line.last += landed
        low, grad_a = own(3, acts_x[3], carry)
        grad_b = up_gradient(line, low, got_scaled)
        return result, grad_a, grad_b

    steps = [most * 5 // 8, most * 3 // 4, most]
    which = sum((need_all > s).astype(jnp.int32) for s in steps[:-1])
    return lax.switch(which, [functools.partial(run, s) for s in steps])


def solution(mesh):
    return jax.shard_map(
        shards,
        mesh=mesh,
        in_specs=(
            P(("groups", "dp"), None),
            P(("groups", "dp"), None),
            P("dp", None),
            P(("groups", "dp"), None, None),
            P(("groups", "dp"), None, None),
            P(("groups", "dp"), None),
            P("groups"),
            P("groups"),
        ),
        out_specs=(
            P(("groups", "dp"), None),
            P(("groups", "dp"), None, None),
            P(("groups", "dp"), None, None),
        ),
        check_vma=False,
    )
```

```python
import functools

import jax
import jax.numpy as jnp
from jax import lax
from jax.experimental import pallas as pl
from jax.experimental.pallas import tpu as pltpu
from jax.sharding import PartitionSpec as P

DELTA_MULTIPLIER = 0.25
BF = jnp.bfloat16
F32 = jnp.float32
PLANES = 4
PIECES = 4
PARAMS = pltpu.CompilerParams(vmem_limit_bytes=48 * 1024 * 1024)


def whole(shape):
    zeros = (0,) * len(shape)
    return pl.BlockSpec(shape, lambda i: zeros)


def dot(a, b, ca=1, cb=0):
    return lax.dot_general(a, b, (((ca,), (cb,)), ((), ())), preferred_element_type=F32)


HERE = pl.BlockSpec(memory_space=pl.ANY)
FAR = pl.BlockSpec(memory_space=pltpu.HBM)


def route_body(count, rows_ref, *refs):
    ins, outs = refs[:count], refs[count:]
    held = ins[0][...] if count == 1 else jnp.concatenate([r[...] for r in ins], axis=0)
    moved = dot(rows_ref[...], held).astype(BF)
    at = 0
    for out in outs:
        out[...] = moved[at : at + out.shape[0]]
        at += out.shape[0]


class Line:
    def __init__(self):
        self.last = []

    def call(self, body, operands, in_specs, out_specs, out_shape, pieces=1, aliases=None):
        after = self.last
        first = len(operands)

        def kernel(*refs):
            return body(*refs[:first], *refs[first + len(after) :])

        out = pl.pallas_call(
            kernel,
            grid=(pieces,),
            in_specs=in_specs + [HERE] * len(after),
            out_specs=out_specs,
            out_shape=out_shape,
            input_output_aliases=aliases or {},
            cost_estimate=pl.CostEstimate(flops=1, bytes_accessed=1, transcendentals=0),
            compiler_params=PARAMS,
        )(*operands, *after)
        self.last = [out[0] if isinstance(out, (list, tuple)) else out]
        return out


def hold_body(ref, out):
    pass


def hold(line, x):
    last = line.last
    out = line.call(hold_body, [x], [FAR], FAR, jax.ShapeDtypeStruct(x.shape, x.dtype), 1, {0: 0})
    line.last = last
    return out


def route(line, rows, ins, outs):
    width = ins[0].shape[1]
    pieces = PIECES if width % (128 * PIECES) == 0 else 1
    step = width // pieces

    def block(n):
        return pl.BlockSpec((n, step), lambda i: (0, i))

    return line.call(
        functools.partial(route_body, len(ins)),
        [rows, *ins],
        [whole(rows.shape)] + [block(x.shape[0]) for x in ins],
        [block(n) for n in outs],
        [jax.ShapeDtypeStruct((n, width), BF) for n in outs],
        pieces,
    )


def job_rows(refs, job):
    return jnp.concatenate([ref[job] for ref in refs], axis=0)


def back_body(count, up_ref, *refs):
    out = refs[count]
    for job in range(up_ref.shape[0]):
        held = job_rows(refs[:count], job)
        out[job] = (DELTA_MULTIPLIER * dot(held, up_ref[job], 1, 1)).astype(BF)


def back_project(line, up, rows):
    local, rank = up.shape[0], up.shape[1]
    shape = (local, sum(x.shape[1] for x in rows), rank)
    return line.call(
        functools.partial(back_body, len(rows)),
        [up, *rows],
        [whole(up.shape)] + [whole(x.shape) for x in rows],
        whole(shape),
        jax.ShapeDtypeStruct(shape, BF),
    )


def term_body(back_ref, down_ref, *outs):
    for job in range(down_ref.shape[0]):
        term = dot(back_ref[job], down_ref[job], 1, 1).astype(BF)
        at = 0
        for out in outs:
            out[job] = term[at : at + out.shape[1]]
            at += out.shape[1]


def adapter_terms(line, back_low, down, outs):
    local, width, rank = down.shape
    step = width // PIECES
    return line.call(
        term_body,
        [back_low, down],
        [whole(back_low.shape), pl.BlockSpec((local, step, rank), lambda i: (0, i, 0))],
        [pl.BlockSpec((local, n, step), lambda i: (0, 0, i)) for n in outs],
        [jax.ShapeDtypeStruct((local, n, width), BF) for n in outs],
        PIECES,
    )


def owner_body(count, back_ref, down_ref, *refs):
    ins, (low_ref, grad_ref) = refs[:count], refs[count:]

    @pl.when(pl.program_id(0) == 0)
    def _():
        low_ref[...] = jnp.zeros_like(low_ref)

    for job in range(down_ref.shape[0]):
        held = job_rows(ins, job)
        low_ref[job] += dot(held, down_ref[job])
        grad_ref[job] = dot(held, back_ref[job], 0, 0).astype(BF)


def owner_step(line, back_low, down, rows):
    local, width, rank = down.shape
    step = width // PIECES
    part = pl.BlockSpec((local, step, rank), lambda i: (0, i, 0))
    low_shape = (local, back_low.shape[1], rank)
    return line.call(
        functools.partial(owner_body, len(rows)),
        [back_low, down, *rows],
        [whole(back_low.shape), part]
        + [pl.BlockSpec((local, x.shape[1], step), lambda i: (0, 0, i)) for x in rows],
        [whole(low_shape), part],
        [jax.ShapeDtypeStruct(low_shape, F32), jax.ShapeDtypeStruct(down.shape, BF)],
        PIECES,
    )


def up_body(count, low_ref, *refs):
    out = refs[count]
    for job in range(low_ref.shape[0]):
        low = low_ref[job].astype(BF)
        held = job_rows(refs[:count], job)
        out[job] = (DELTA_MULTIPLIER * dot(low, held, 0, 0)).astype(BF)


def up_gradient(line, low, rows):
    shape = (low.shape[0], low.shape[2], rows[0].shape[2])
    return line.call(
        functools.partial(up_body, len(rows)),
        [low, *rows],
        [whole(low.shape)] + [whole(x.shape) for x in rows],
        whole(shape),
        jax.ShapeDtypeStruct(shape, BF),
    )


def final_body(scaled_ref, weight_ref, rows_ref, ref, out):
    cores, parts, height = weight_ref.shape[:3]
    weight = jnp.concatenate(
        [
            weight_ref[core, part, at, 0]
            for at in range(height)
            for core in range(cores)
            for part in range(parts)
        ],
        axis=0,
    )
    base = dot(scaled_ref[...], weight, 1, 1)
    out[...] = (base + dot(rows_ref[...], ref[...])).astype(BF)


def final_step(line, scaled, weight, rows, came):
    cores, parts, height, planes, share, deep = weight.shape
    step = cores * parts * height * share
    return line.call(
        final_body,
        [scaled, weight, rows, came],
        [
            whole(scaled.shape),
            pl.BlockSpec((cores, parts, height, 1, share, deep), lambda i: (0, 0, 0, i, 0, 0)),
            whole(rows.shape),
            pl.BlockSpec((came.shape[0], step), lambda i: (0, i)),
        ],
        pl.BlockSpec((scaled.shape[0], step), lambda i: (0, i)),
        jax.ShapeDtypeStruct((scaled.shape[0], step * planes), BF),
        planes,
    )


def shards(
    acts,
    cotan,
    frozen_key_weight,
    adapter_down_slots,
    adapter_up_slots,
    token_row_jobs,
    slot_owner_jobs,
    loss_token_count,
):
    devices = lax.axis_size("dp")
    parts = lax.axis_size("groups")
    tok_rows = acts.shape[0]
    local = adapter_down_slots.shape[0]
    jobs_all = slot_owner_jobs.shape[0]
    depth = 2 * tok_rows // (local * devices)
    column = devices // PLANES
    ring = column <= 4
    most = local * column * depth
    segment = PLANES * depth
    me = lax.axis_index("dp")
    plane, place = me // column, me % column

    ids = token_row_jobs[:, 0]
    lengths = loss_token_count.astype(F32)
    weights = jnp.mean(lengths) / lengths
    numbers = jnp.arange(jobs_all, dtype=jnp.int32)
    row_weight = jnp.sum(jnp.where(ids[:, None] == numbers[None, :], weights[None, :], 0.0), axis=1)
    row_slot = jnp.sum(
        jnp.where(ids[:, None] == slot_owner_jobs[None, :], numbers[None, :], 0), axis=1
    )
    scaled = (row_weight[:, None] * cotan.astype(F32)).astype(BF)

    planes = jnp.arange(PLANES, dtype=jnp.int32)
    need = jnp.max(
        jnp.sum((row_slot[:, None] // (local * column) == planes[None, :]).astype(jnp.int32), axis=0)
    )
    note = jnp.concatenate([row_slot, jnp.full((128,), need, jnp.int32)])
    notes = lax.all_to_all(
        jnp.broadcast_to(note[None, None], (parts * devices, 1, tok_rows + 128)),
        ("groups", "dp"),
        split_axis=0,
        concat_axis=0,
        tiled=True,
    )[:, 0]
    need_all = jnp.max(notes[:, tok_rows])
    mine = notes[:, :tok_rows].reshape(parts, PLANES, column, tok_rows)
    mine = lax.dynamic_index_in_dim(mine, lax.axis_index("groups"), 0, keepdims=False)
    mine = lax.dynamic_index_in_dim(mine, place, 1, keepdims=False)
    slots = mine
    goal = slots // (local * column)
    earlier = jnp.arange(tok_rows)[None, :] < jnp.arange(tok_rows)[:, None]
    order = jnp.sum(
        ((goal[:, :, None] == goal[:, None, :]) & earlier[None]).astype(jnp.int32), axis=2
    )
    rank = jnp.sum(
        ((slots[:, :, None] == slots[:, None, :]) & earlier[None]).astype(jnp.int32), axis=2
    )
    owner = (slots // local) % column
    if ring:
        owner = owner ^ place
    spot = (
        owner * (local * segment)
        + (slots % local) * segment
        + planes[:, None] * depth
        + rank
    )
    spot = jnp.where(goal == plane, spot, -1)
    own_goal = row_slot // (local * column)
    own_order = jnp.sum(
        ((own_goal[:, None] == own_goal[None, :]) & earlier).astype(jnp.int32), axis=1
    )

    def across(bufs):
        return [bufs[0]] + [
            lax.ppermute(
                bufs[s],
                "dp",
                [(d, ((d // column) ^ s) * column + d % column) for d in range(devices)],
            )
            for s in range(1, PLANES)
        ]

    blocks = [[p * column + c for c in range(column)] for p in range(PLANES)]

    def within(x):
        return lax.all_to_all(
            x, "dp", split_axis=0, concat_axis=0, tiled=True, axis_index_groups=blocks
        )

    blocks_out = [local * segment] * column if ring else [column * local * segment]
    owner_outs = [segment] * column if ring else [column * segment]

    def near(bufs):
        if not ring:
            return [within(bufs[0])]
        return [bufs[0]] + [
            lax.ppermute(bufs[s], "dp", [(d, d ^ s) for d in range(devices)])
            for s in range(1, column)
        ]

    def at_owner(bufs):
        width = bufs[0].shape[1]
        if ring:
            return [x.reshape(local, segment, width) for x in bufs]
        x = bufs[0].reshape(column, local, segment, width).transpose(1, 0, 2, 3)
        return [x.reshape(local, column * segment, width)]

    def from_owner(bufs):
        width = bufs[0].shape[2]
        if ring:
            return [x.reshape(local * segment, width) for x in bufs]
        x = bufs[0].reshape(local, column, segment, width).transpose(1, 0, 2, 3)
        return [x.reshape(column * local * segment, width)]

    stripes = [[p * column + c for p in range(PLANES)] for c in range(column)]
    pairs = [[d, d + 1] for d in range(0, devices, 2)]
    lanes_of = [
        [p * column + 2 * h + c for h in range(column // 2)]
        for p in range(PLANES)
        for c in range(2)
    ]

    def planes_swap(x):
        return lax.all_to_all(
            x, "dp", split_axis=0, concat_axis=0, tiled=True, axis_index_groups=stripes
        )

    def gather_all(x, axis, groups=None):
        return lax.all_gather(x, axis, axis=0, tiled=True, axis_index_groups=groups)

    share = frozen_key_weight.shape[0] // parts
    deep = frozen_key_weight.shape[1]
    weight = lax.dynamic_slice_in_dim(
        frozen_key_weight, lax.axis_index("groups") * share, share, 0
    )
    weight_z = gather_all(weight, "dp", stripes)

    def shape_weight(w):
        w = w.reshape(2, parts, column // 2, PLANES, share, deep)
        if share % 16 == 0:
            return w
        w = w.transpose(3, 2, 0, 1, 4, 5)
        return w.reshape(1, 1, 1, PLANES, column * parts * share, deep)

    def outward(size, side):
        lanes = jnp.arange(PLANES * size, dtype=jnp.int32)
        code = side * size + own_order
        return (lanes[:, None] == code[None, :]).astype(BF), (
            code[:, None] == lanes[None, :]
        ).astype(BF)

    def inward(size, turned=False):
        kth = jnp.arange(size, dtype=jnp.int32)
        target = jnp.sum(
            jnp.where(
                (order[:, None, :] == kth[None, :, None]) & (spot[:, None, :] >= 0),
                spot[:, None, :] + 1,
                0,
            ),
            axis=2,
        )
        if turned:
            there = (planes ^ plane)[:, None, None] == planes[None, :, None]
            target = jnp.sum(jnp.where(there, target[None], 0), axis=1)
        target = target.reshape(PLANES * size) - 1
        spots = jnp.arange(PLANES * most, dtype=jnp.int32)
        return (spots[:, None] == target[None, :]).astype(BF), (
            target[:, None] == spots[None, :]
        ).astype(BF)

    scaled_z = across(route(Line(), outward(most, own_goal ^ plane)[0], [scaled], [most] * PLANES))
    scaled_sent = route(Line(), inward(most, True)[0], scaled_z, blocks_out)

    def run(size):
        out_rows, back_rows = outward(size, own_goal)
        spread, gather = inward(size)
        line = Line()
        total = PLANES * size
        acts_z = planes_swap(route(line, out_rows, [acts], [total])[0])
        weight = gather_all(weight_z, "dp", lanes_of)
        got_scaled = at_owner(near(scaled_sent))
        back_low = back_project(line, adapter_up_slots, got_scaled)
        terms = adapter_terms(line, back_low, adapter_down_slots, owner_outs)
        terms = near(from_owner(terms))
        weight = gather_all(hold(line, weight), "groups")
        terms_z = planes_swap(route(line, gather, terms, [total])[0])
        got = at_owner(near(route(line, spread, [acts_z], blocks_out)))
        weight = gather_all(hold(line, weight), "dp", pairs)
        low, grad_a = owner_step(line, back_low, adapter_down_slots, got)
        grad_b = up_gradient(line, low, got_scaled)
        result = final_step(line, scaled, shape_weight(weight), back_rows, terms_z)
        return result, grad_a, grad_b

    steps = [most * 5 // 8, most * 3 // 4, most]
    which = sum((need_all > s).astype(jnp.int32) for s in steps[:-1])
    return lax.switch(which, [functools.partial(run, s) for s in steps])


def solution(mesh):
    return jax.shard_map(
        shards,
        mesh=mesh,
        in_specs=(
            P(("groups", "dp"), None),
            P(("groups", "dp"), None),
            P("dp", None),
            P(("groups", "dp"), None, None),
            P(("groups", "dp"), None, None),
            P(("groups", "dp"), None),
            P("groups"),
            P("groups"),
        ),
        out_specs=(
            P(("groups", "dp"), None),
            P(("groups", "dp"), None, None),
            P(("groups", "dp"), None, None),
        ),
        check_vma=False,
    )
```

```python
import functools

import jax
import jax.numpy as jnp
from jax import lax
from jax.experimental import pallas as pl
from jax.experimental.pallas import tpu as pltpu
from jax.sharding import PartitionSpec as P

DELTA_MULTIPLIER = 0.25
BF = jnp.bfloat16
F32 = jnp.float32
PLANES = 4
PIECES = 4
PARAMS = pltpu.CompilerParams(vmem_limit_bytes=48 * 1024 * 1024)


def far(shape, dtype=BF):
    return pltpu.HBM(shape, dtype)


def whole(shape):
    zeros = (0,) * len(shape)
    return pl.BlockSpec(shape, lambda i: zeros)


def dot(a, b, ca=1, cb=0):
    return lax.dot_general(a, b, (((ca,), (cb,)), ((), ())), preferred_element_type=F32)


HERE = pl.BlockSpec(memory_space=pl.ANY)
FAR = pl.BlockSpec(memory_space=pltpu.HBM)


def route_body(count, rows_ref, *refs):
    ins, outs = refs[:count], refs[count:]
    held = ins[0][...] if count == 1 else jnp.concatenate([r[...] for r in ins], axis=0)
    moved = dot(rows_ref[...], held).astype(BF)
    at = 0
    for out in outs:
        out[...] = moved[at : at + out.shape[0]]
        at += out.shape[0]


class Line:
    def __init__(self):
        self.last = []

    def call(self, body, operands, in_specs, out_specs, out_shape, pieces=1, aliases=None):
        after = self.last
        first = len(operands)

        def kernel(*refs):
            return body(*refs[:first], *refs[first + len(after) :])

        out = pl.pallas_call(
            kernel,
            grid=(pieces,),
            in_specs=in_specs + [HERE] * len(after),
            out_specs=out_specs,
            out_shape=out_shape,
            input_output_aliases=aliases or {},
            cost_estimate=pl.CostEstimate(flops=1, bytes_accessed=1, transcendentals=0),
            compiler_params=PARAMS,
        )(*operands, *after)
        self.last = [out[0] if isinstance(out, (list, tuple)) else out]
        return out


def hold_body(ref, out):
    pass


def hold(line, x):
    last = line.last
    out = line.call(hold_body, [x], [FAR], FAR, far(x.shape, x.dtype), 1, {0: 0})
    line.last = last
    return out


def route(line, rows, ins, outs, part=(0, 1, 1)):
    lowest, highest, of = part
    if of == 1 and ins[0].shape[1] % (128 * PIECES) == 0:
        highest = of = PIECES
    step = ins[0].shape[1] // of
    pieces = highest - lowest
    width = pieces * step
    return line.call(
        functools.partial(route_body, len(ins)),
        [rows, *ins],
        [whole(rows.shape)]
        + [pl.BlockSpec((x.shape[0], step), lambda i: (0, i + lowest)) for x in ins],
        [pl.BlockSpec((n, step), lambda i: (0, i)) for n in outs],
        [far((n, width)) for n in outs],
        pieces,
    )


def job_rows(refs, job):
    return jnp.concatenate([ref[job] for ref in refs], axis=0)


def back_body(count, up_ref, *refs):
    out = refs[count]
    for job in range(up_ref.shape[0]):
        held = job_rows(refs[:count], job)
        out[job] = (DELTA_MULTIPLIER * dot(held, up_ref[job], 1, 1)).astype(BF)


def back_project(line, up, rows):
    local, rank = up.shape[0], up.shape[1]
    shape = (local, sum(x.shape[1] for x in rows), rank)
    return line.call(
        functools.partial(back_body, len(rows)),
        [up, *rows],
        [whole(up.shape)] + [whole(x.shape) for x in rows],
        whole(shape),
        jax.ShapeDtypeStruct(shape, BF),
    )


def term_body(back_ref, down_ref, *outs):
    for job in range(down_ref.shape[0]):
        term = dot(back_ref[job], down_ref[job], 1, 1).astype(BF)
        at = 0
        for out in outs:
            out[job] = term[at : at + out.shape[1]]
            at += out.shape[1]


def adapter_terms(line, back_low, down, outs):
    local, width, rank = down.shape
    step = width // PIECES
    return line.call(
        term_body,
        [back_low, down],
        [whole(back_low.shape), pl.BlockSpec((local, step, rank), lambda i: (0, i, 0))],
        [pl.BlockSpec((local, n, step), lambda i: (0, 0, i)) for n in outs],
        [far((local, n, width)) for n in outs],
        PIECES,
    )


def owner_body(count, back_ref, down_ref, *refs):
    ins, (low_ref, grad_ref) = refs[:count], refs[count:]

    @pl.when(pl.program_id(0) == 0)
    def _():
        low_ref[...] = jnp.zeros_like(low_ref)

    for job in range(down_ref.shape[0]):
        held = job_rows(ins, job)
        low_ref[job] += dot(held, down_ref[job])
        grad_ref[job] = dot(held, back_ref[job], 0, 0).astype(BF)


def owner_step(line, back_low, down, rows):
    local, width, rank = down.shape
    step = width // PIECES
    part = pl.BlockSpec((local, step, rank), lambda i: (0, i, 0))
    low_shape = (local, back_low.shape[1], rank)
    return line.call(
        functools.partial(owner_body, len(rows)),
        [back_low, down, *rows],
        [whole(back_low.shape), part]
        + [pl.BlockSpec((local, x.shape[1], step), lambda i: (0, 0, i)) for x in rows],
        [whole(low_shape), part],
        [jax.ShapeDtypeStruct(low_shape, F32), jax.ShapeDtypeStruct(down.shape, BF)],
        PIECES,
    )


def up_body(count, low_ref, *refs):
    out = refs[count]
    for job in range(low_ref.shape[0]):
        low = low_ref[job].astype(BF)
        held = job_rows(refs[:count], job)
        out[job] = (DELTA_MULTIPLIER * dot(low, held, 0, 0)).astype(BF)


def up_gradient(line, low, rows):
    shape = (low.shape[0], low.shape[2], rows[0].shape[2])
    return line.call(
        functools.partial(up_body, len(rows)),
        [low, *rows],
        [whole(low.shape)] + [whole(x.shape) for x in rows],
        whole(shape),
        jax.ShapeDtypeStruct(shape, BF),
    )


def final_body(scaled_ref, weight_ref, rows_ref, main_ref, last_ref, out):
    cores, parts, height = weight_ref.shape[:3]
    weight = jnp.concatenate(
        [
            weight_ref[core, part, at, 0]
            for at in range(height)
            for core in range(cores)
            for part in range(parts)
        ],
        axis=0,
    )
    base = dot(scaled_ref[...], weight, 1, 1)
    last = pl.program_id(0) == PLANES - 1

    @pl.when(last)
    def _():
        out[...] = (base + dot(rows_ref[...], last_ref[...])).astype(BF)

    @pl.when(jnp.logical_not(last))
    def _():
        out[...] = (base + dot(rows_ref[...], main_ref[...])).astype(BF)


def final_step(line, scaled, weight, rows, main, last):
    cores, parts, height, planes, share, deep = weight.shape
    step = cores * parts * height * share
    return line.call(
        final_body,
        [scaled, weight, rows, main, last],
        [
            whole(scaled.shape),
            pl.BlockSpec((cores, parts, height, 1, share, deep), lambda i: (0, 0, 0, i, 0, 0)),
            whole(rows.shape),
            pl.BlockSpec((main.shape[0], step), lambda i: (0, jnp.minimum(i, planes - 2))),
            pl.BlockSpec((last.shape[0], step), lambda i: (0, 0)),
        ],
        pl.BlockSpec((scaled.shape[0], step), lambda i: (0, i)),
        jax.ShapeDtypeStruct((scaled.shape[0], step * planes), BF),
        planes,
    )


def shards(
    acts,
    cotan,
    frozen_key_weight,
    adapter_down_slots,
    adapter_up_slots,
    token_row_jobs,
    slot_owner_jobs,
    loss_token_count,
):
    devices = lax.axis_size("dp")
    parts = lax.axis_size("groups")
    tok_rows = acts.shape[0]
    local = adapter_down_slots.shape[0]
    jobs_all = slot_owner_jobs.shape[0]
    depth = 2 * tok_rows // (local * devices)
    column = devices // PLANES
    ring = column <= 4
    most = local * column * depth
    segment = PLANES * depth
    me = lax.axis_index("dp")
    plane, place = me // column, me % column

    first = Line()
    ids = token_row_jobs[:, 0]
    lengths = loss_token_count.astype(F32)
    weights = jnp.mean(lengths) / lengths
    numbers = jnp.arange(jobs_all, dtype=jnp.int32)
    row_weight = jnp.sum(jnp.where(ids[:, None] == numbers[None, :], weights[None, :], 0.0), axis=1)
    row_slot = jnp.sum(
        jnp.where(ids[:, None] == slot_owner_jobs[None, :], numbers[None, :], 0), axis=1
    )
    scaled = (row_weight[:, None] * cotan.astype(F32)).astype(BF)

    planes = jnp.arange(PLANES, dtype=jnp.int32)
    need = jnp.max(
        jnp.sum((row_slot[:, None] // (local * column) == planes[None, :]).astype(jnp.int32), axis=0)
    )
    note = jnp.concatenate([row_slot, jnp.full((128,), need, jnp.int32)])
    note = jnp.broadcast_to(note[None, None], (parts * devices, 1, tok_rows + 128))
    first.last = [note]
    notes = lax.all_to_all(
        note,
        ("groups", "dp"),
        split_axis=0,
        concat_axis=0,
        tiled=True,
    )[:, 0]
    need_all = jnp.max(notes[:, tok_rows])
    mine = notes[:, :tok_rows].reshape(parts, PLANES, column, tok_rows)
    mine = lax.dynamic_index_in_dim(mine, lax.axis_index("groups"), 0, keepdims=False)
    mine = lax.dynamic_index_in_dim(mine, place, 1, keepdims=False)
    slots = mine
    goal = slots // (local * column)
    earlier = jnp.arange(tok_rows)[None, :] < jnp.arange(tok_rows)[:, None]
    order = jnp.sum(
        ((goal[:, :, None] == goal[:, None, :]) & earlier[None]).astype(jnp.int32), axis=2
    )
    rank = jnp.sum(
        ((slots[:, :, None] == slots[:, None, :]) & earlier[None]).astype(jnp.int32), axis=2
    )
    owner = (slots // local) % column
    if ring:
        owner = owner ^ place
    spot = (
        owner * (local * segment)
        + (slots % local) * segment
        + planes[:, None] * depth
        + rank
    )
    spot = jnp.where(goal == plane, spot, -1)
    own_goal = row_slot // (local * column)
    own_order = jnp.sum(
        ((own_goal[:, None] == own_goal[None, :]) & earlier).astype(jnp.int32), axis=1
    )

    def across(bufs):
        return [bufs[0]] + [
            lax.ppermute(
                bufs[s],
                "dp",
                [(d, ((d // column) ^ s) * column + d % column) for d in range(devices)],
            )
            for s in range(1, PLANES)
        ]

    blocks = [[p * column + c for c in range(column)] for p in range(PLANES)]

    def within(x):
        return lax.all_to_all(
            x, "dp", split_axis=0, concat_axis=0, tiled=True, axis_index_groups=blocks
        )

    blocks_out = [local * segment] * column if ring else [column * local * segment]
    owner_outs = [segment] * column if ring else [column * segment]

    def near(bufs):
        if not ring:
            return [within(bufs[0])]
        return [bufs[0]] + [
            lax.ppermute(bufs[s], "dp", [(d, d ^ s) for d in range(devices)])
            for s in range(1, column)
        ]

    def at_owner(bufs):
        width = bufs[0].shape[1]
        if ring:
            return [x.reshape(local, segment, width) for x in bufs]
        x = bufs[0].reshape(column, local, segment, width).transpose(1, 0, 2, 3)
        return [x.reshape(local, column * segment, width)]

    def from_owner(bufs):
        width = bufs[0].shape[2]
        if ring:
            return [x.reshape(local * segment, width) for x in bufs]
        x = bufs[0].reshape(local, column, segment, width).transpose(1, 0, 2, 3)
        return [x.reshape(column * local * segment, width)]

    stripes = [[p * column + c for p in range(PLANES)] for c in range(column)]
    pairs = [[d, d + 1] for d in range(0, devices, 2)]
    lanes_of = [
        [p * column + 2 * h + c for h in range(column // 2)]
        for p in range(PLANES)
        for c in range(2)
    ]

    def planes_swap(x):
        return lax.all_to_all(
            x, "dp", split_axis=0, concat_axis=0, tiled=True, axis_index_groups=stripes
        )

    def gather_all(x, axis, groups=None):
        return lax.all_gather(x, axis, axis=0, tiled=True, axis_index_groups=groups)

    share = frozen_key_weight.shape[0] // parts
    deep = frozen_key_weight.shape[1]
    weight = lax.dynamic_slice_in_dim(
        frozen_key_weight, lax.axis_index("groups") * share, share, 0
    )
    own_share = weight
    first.last += [own_share]

    def shape_weight(w):
        w = w.reshape(2, parts, column // 2, PLANES, share, deep)
        if share % 16 == 0:
            return w
        w = w.transpose(3, 2, 0, 1, 4, 5)
        return w.reshape(1, 1, 1, PLANES, column * parts * share, deep)

    def outward(size, side):
        lanes = jnp.arange(PLANES * size, dtype=jnp.int32)
        code = side * size + own_order
        return (lanes[:, None] == code[None, :]).astype(BF), (
            code[:, None] == lanes[None, :]
        ).astype(BF)

    def inward(size, turned=False):
        kth = jnp.arange(size, dtype=jnp.int32)
        target = jnp.sum(
            jnp.where(
                (order[:, None, :] == kth[None, :, None]) & (spot[:, None, :] >= 0),
                spot[:, None, :] + 1,
                0,
            ),
            axis=2,
        )
        if turned:
            there = (planes ^ plane)[:, None, None] == planes[None, :, None]
            target = jnp.sum(jnp.where(there, target[None], 0), axis=1)
        target = target.reshape(PLANES * size) - 1
        spots = jnp.arange(PLANES * most, dtype=jnp.int32)
        return (spots[:, None] == target[None, :]).astype(BF), (
            target[:, None] == spots[None, :]
        ).astype(BF)

    def run(size, line):
        total = PLANES * size
        back_rows = outward(size, own_goal)[1]
        weight = gather_all(own_share, "dp", stripes)
        scaled_z = across(
            route(line, outward(size, own_goal ^ plane)[0], [scaled], [size] * PLANES)
        )
        leaving = route(line, outward(size, own_goal)[0], [acts], [total])[0]
        line.last += scaled_z[1:]
        acts_z = planes_swap(hold(line, leaving))
        got_scaled = at_owner(near(route(line, inward(size, True)[0], scaled_z, blocks_out)))
        weight = gather_all(hold(line, weight), "dp", lanes_of)
        spread, gather = inward(size)
        back_low = back_project(line, adapter_up_slots, got_scaled)
        terms = adapter_terms(line, back_low, adapter_down_slots, owner_outs)
        terms = near(from_owner(terms))
        main = planes_swap(route(line, gather, terms, [total], (0, PLANES - 1, PLANES))[0])
        got = route(line, spread, [acts_z], blocks_out)
        weight = gather_all(hold(line, weight), "groups")
        last = planes_swap(route(line, gather, terms, [total], (PLANES - 1, PLANES, PLANES))[0])
        got = at_owner(near(got))
        low, grad_a = owner_step(line, back_low, adapter_down_slots, got)
        grad_b = up_gradient(line, low, got_scaled)
        line.last += [main]
        weight = gather_all(hold(line, weight), "dp", pairs)
        result = final_step(line, scaled, shape_weight(weight), back_rows, main, last)
        return result, grad_a, grad_b

    size = most * 3 // 4

    def again(state):
        return (jnp.zeros_like(state[0]), *run(most, Line()))

    return lax.while_loop(
        lambda state: state[0] > 0,
        again,
        ((need_all > size).astype(jnp.int32), *run(size, first)),
    )[1:]


def solution(mesh):
    return jax.shard_map(
        shards,
        mesh=mesh,
        in_specs=(
            P(("groups", "dp"), None),
            P(("groups", "dp"), None),
            P("dp", None),
            P(("groups", "dp"), None, None),
            P(("groups", "dp"), None, None),
            P(("groups", "dp"), None),
            P("groups"),
            P("groups"),
        ),
        out_specs=(
            P(("groups", "dp"), None),
            P(("groups", "dp"), None, None),
            P(("groups", "dp"), None, None),
        ),
        check_vma=False,
    )
```

```python
import functools

import jax
import jax.numpy as jnp
from jax import lax
from jax.experimental import pallas as pl
from jax.experimental.pallas import tpu as pltpu
from jax.sharding import PartitionSpec as P

DELTA_MULTIPLIER = 0.25
BF = jnp.bfloat16
F32 = jnp.float32
PLANES = 4
PIECES = 4
PARAMS = pltpu.CompilerParams(vmem_limit_bytes=48 * 1024 * 1024)


def far(shape, dtype=BF):
    return pltpu.HBM(shape, dtype)


def whole(shape):
    zeros = (0,) * len(shape)
    return pl.BlockSpec(shape, lambda i: zeros)


def dot(a, b, ca=1, cb=0):
    return lax.dot_general(a, b, (((ca,), (cb,)), ((), ())), preferred_element_type=F32)


HERE = pl.BlockSpec(memory_space=pl.ANY)
FAR = pl.BlockSpec(memory_space=pltpu.HBM)


def route_body(count, rows_ref, *refs):
    ins, outs = refs[:count], refs[count:]
    held = ins[0][...] if count == 1 else jnp.concatenate([r[...] for r in ins], axis=0)
    moved = dot(rows_ref[...], held).astype(BF)
    at = 0
    for out in outs:
        out[...] = moved[at : at + out.shape[0]]
        at += out.shape[0]


class Line:
    def __init__(self):
        self.last = []

    def call(self, body, operands, in_specs, out_specs, out_shape, pieces=1, aliases=None):
        after = self.last
        first = len(operands)
        many = isinstance(out_shape, list)

        def kernel(*refs):
            refs[-1][...] = jnp.zeros_like(refs[-1])
            return body(*refs[:first], *refs[first + len(after) : -1])

        out = pl.pallas_call(
            kernel,
            grid=(pieces,),
            in_specs=in_specs + [HERE] * len(after),
            out_specs=(out_specs if many else [out_specs]) + [whole((8, 128))],
            out_shape=(out_shape if many else [out_shape])
            + [jax.ShapeDtypeStruct((8, 128), jnp.int32)],
            input_output_aliases=aliases or {},
            compiler_params=PARAMS,
        )(*operands, *after)
        self.last = [out[-1]]
        return out[:-1] if many else out[0]


def hold_body(ref, out):
    pass


def hold(line, x):
    last = line.last
    out = line.call(hold_body, [x], [FAR], FAR, far(x.shape, x.dtype), 1, {0: 0})
    line.last = last
    return out


def route(line, rows, ins, outs, part=(0, 1, 1)):
    lowest, highest, of = part
    if of == 1 and ins[0].shape[1] % (128 * PIECES) == 0:
        highest = of = PIECES
    step = ins[0].shape[1] // of
    pieces = highest - lowest
    width = pieces * step
    return line.call(
        functools.partial(route_body, len(ins)),
        [rows, *ins],
        [whole(rows.shape)]
        + [pl.BlockSpec((x.shape[0], step), lambda i: (0, i + lowest)) for x in ins],
        [pl.BlockSpec((n, step), lambda i: (0, i)) for n in outs],
        [far((n, width)) for n in outs],
        pieces,
    )


def job_rows(refs, job):
    return jnp.concatenate([ref[job] for ref in refs], axis=0)


def back_body(count, up_ref, *refs):
    out = refs[count]
    for job in range(up_ref.shape[0]):
        held = job_rows(refs[:count], job)
        out[job] = (DELTA_MULTIPLIER * dot(held, up_ref[job], 1, 1)).astype(BF)


def back_project(line, up, rows):
    local, rank = up.shape[0], up.shape[1]
    shape = (local, sum(x.shape[1] for x in rows), rank)
    return line.call(
        functools.partial(back_body, len(rows)),
        [up, *rows],
        [whole(up.shape)] + [whole(x.shape) for x in rows],
        whole(shape),
        jax.ShapeDtypeStruct(shape, BF),
    )


def term_body(back_ref, down_ref, *outs):
    for job in range(down_ref.shape[0]):
        term = dot(back_ref[job], down_ref[job], 1, 1).astype(BF)
        at = 0
        for out in outs:
            out[job] = term[at : at + out.shape[1]]
            at += out.shape[1]


def adapter_terms(line, back_low, down, outs):
    local, width, rank = down.shape
    step = width // PIECES
    return line.call(
        term_body,
        [back_low, down],
        [whole(back_low.shape), pl.BlockSpec((local, step, rank), lambda i: (0, i, 0))],
        [pl.BlockSpec((local, n, step), lambda i: (0, 0, i)) for n in outs],
        [far((local, n, width)) for n in outs],
        PIECES,
    )


def owner_body(count, back_ref, down_ref, *refs):
    ins, (low_ref, grad_ref) = refs[:count], refs[count:]

    @pl.when(pl.program_id(0) == 0)
    def _():
        low_ref[...] = jnp.zeros_like(low_ref)

    for job in range(down_ref.shape[0]):
        held = job_rows(ins, job)
        low_ref[job] += dot(held, down_ref[job])
        grad_ref[job] = dot(held, back_ref[job], 0, 0).astype(BF)


def owner_step(line, back_low, down, rows):
    local, width, rank = down.shape
    step = width // PIECES
    part = pl.BlockSpec((local, step, rank), lambda i: (0, i, 0))
    low_shape = (local, back_low.shape[1], rank)
    return line.call(
        functools.partial(owner_body, len(rows)),
        [back_low, down, *rows],
        [whole(back_low.shape), part]
        + [pl.BlockSpec((local, x.shape[1], step), lambda i: (0, 0, i)) for x in rows],
        [whole(low_shape), part],
        [jax.ShapeDtypeStruct(low_shape, F32), jax.ShapeDtypeStruct(down.shape, BF)],
        PIECES,
    )


def up_body(count, low_ref, *refs):
    out = refs[count]
    for job in range(low_ref.shape[0]):
        low = low_ref[job].astype(BF)
        held = job_rows(refs[:count], job)
        out[job] = (DELTA_MULTIPLIER * dot(low, held, 0, 0)).astype(BF)


def up_gradient(line, low, rows):
    shape = (low.shape[0], low.shape[2], rows[0].shape[2])
    return line.call(
        functools.partial(up_body, len(rows)),
        [low, *rows],
        [whole(low.shape)] + [whole(x.shape) for x in rows],
        whole(shape),
        jax.ShapeDtypeStruct(shape, BF),
    )


def final_body(scaled_ref, weight_ref, rows_ref, main_ref, last_ref, out):
    cores, parts, height = weight_ref.shape[:3]
    weight = jnp.concatenate(
        [
            weight_ref[core, part, at, 0]
            for at in range(height)
            for core in range(cores)
            for part in range(parts)
        ],
        axis=0,
    )
    base = dot(scaled_ref[...], weight, 1, 1)
    last = pl.program_id(0) == PLANES - 1

    @pl.when(last)
    def _():
        out[...] = (base + dot(rows_ref[...], last_ref[...])).astype(BF)

    @pl.when(jnp.logical_not(last))
    def _():
        out[...] = (base + dot(rows_ref[...], main_ref[...])).astype(BF)


def final_step(line, scaled, weight, rows, main, last):
    cores, parts, height, planes, share, deep = weight.shape
    step = cores * parts * height * share
    return line.call(
        final_body,
        [scaled, weight, rows, main, last],
        [
            whole(scaled.shape),
            pl.BlockSpec((cores, parts, height, 1, share, deep), lambda i: (0, 0, 0, i, 0, 0)),
            whole(rows.shape),
            pl.BlockSpec((main.shape[0], step), lambda i: (0, jnp.minimum(i, planes - 2))),
            pl.BlockSpec((last.shape[0], step), lambda i: (0, 0)),
        ],
        pl.BlockSpec((scaled.shape[0], step), lambda i: (0, i)),
        jax.ShapeDtypeStruct((scaled.shape[0], step * planes), BF),
        planes,
    )


def shards(
    acts,
    cotan,
    frozen_key_weight,
    adapter_down_slots,
    adapter_up_slots,
    token_row_jobs,
    slot_owner_jobs,
    loss_token_count,
):
    devices = lax.axis_size("dp")
    parts = lax.axis_size("groups")
    tok_rows = acts.shape[0]
    local = adapter_down_slots.shape[0]
    jobs_all = slot_owner_jobs.shape[0]
    depth = 2 * tok_rows // (local * devices)
    column = devices // PLANES
    ring = column <= 4
    most = local * column * depth
    segment = PLANES * depth
    me = lax.axis_index("dp")
    plane, place = me // column, me % column

    first = Line()
    ids = token_row_jobs[:, 0]
    lengths = loss_token_count.astype(F32)
    weights = jnp.mean(lengths) / lengths
    numbers = jnp.arange(jobs_all, dtype=jnp.int32)
    row_weight = jnp.sum(jnp.where(ids[:, None] == numbers[None, :], weights[None, :], 0.0), axis=1)
    row_slot = jnp.sum(
        jnp.where(ids[:, None] == slot_owner_jobs[None, :], numbers[None, :], 0), axis=1
    )
    scaled = (row_weight[:, None] * cotan.astype(F32)).astype(BF)

    planes = jnp.arange(PLANES, dtype=jnp.int32)
    need = jnp.max(
        jnp.sum((row_slot[:, None] // (local * column) == planes[None, :]).astype(jnp.int32), axis=0)
    )
    note = jnp.concatenate([row_slot, jnp.full((128,), need, jnp.int32)])
    note = jnp.broadcast_to(note[None, None], (parts * devices, 1, tok_rows + 128))
    first.last = [note]
    notes = lax.all_to_all(
        note,
        ("groups", "dp"),
        split_axis=0,
        concat_axis=0,
        tiled=True,
    )[:, 0]
    need_all = jnp.max(notes[:, tok_rows])
    mine = notes[:, :tok_rows].reshape(parts, PLANES, column, tok_rows)
    mine = lax.dynamic_index_in_dim(mine, lax.axis_index("groups"), 0, keepdims=False)
    mine = lax.dynamic_index_in_dim(mine, place, 1, keepdims=False)
    slots = mine
    goal = slots // (local * column)
    earlier = jnp.arange(tok_rows)[None, :] < jnp.arange(tok_rows)[:, None]
    order = jnp.sum(
        ((goal[:, :, None] == goal[:, None, :]) & earlier[None]).astype(jnp.int32), axis=2
    )
    rank = jnp.sum(
        ((slots[:, :, None] == slots[:, None, :]) & earlier[None]).astype(jnp.int32), axis=2
    )
    owner = (slots // local) % column
    if ring:
        owner = owner ^ place
    spot = (
        owner * (local * segment)
        + (slots % local) * segment
        + planes[:, None] * depth
        + rank
    )
    spot = jnp.where(goal == plane, spot, -1)
    own_goal = row_slot // (local * column)
    own_order = jnp.sum(
        ((own_goal[:, None] == own_goal[None, :]) & earlier).astype(jnp.int32), axis=1
    )

    def across(bufs):
        return [bufs[0]] + [
            lax.ppermute(
                bufs[s],
                "dp",
                [(d, ((d // column) ^ s) * column + d % column) for d in range(devices)],
            )
            for s in range(1, PLANES)
        ]

    blocks = [[p * column + c for c in range(column)] for p in range(PLANES)]

    def within(x):
        return lax.all_to_all(
            x, "dp", split_axis=0, concat_axis=0, tiled=True, axis_index_groups=blocks
        )

    blocks_out = [local * segment] * column if ring else [column * local * segment]
    owner_outs = [segment] * column if ring else [column * segment]

    def near(bufs):
        if not ring:
            return [within(bufs[0])]
        return [bufs[0]] + [
            lax.ppermute(bufs[s], "dp", [(d, d ^ s) for d in range(devices)])
            for s in range(1, column)
        ]

    def at_owner(bufs):
        width = bufs[0].shape[1]
        if ring:
            return [x.reshape(local, segment, width) for x in bufs]
        x = bufs[0].reshape(column, local, segment, width).transpose(1, 0, 2, 3)
        return [x.reshape(local, column * segment, width)]

    def from_owner(bufs):
        width = bufs[0].shape[2]
        if ring:
            return [x.reshape(local * segment, width) for x in bufs]
        x = bufs[0].reshape(local, column, segment, width).transpose(1, 0, 2, 3)
        return [x.reshape(column * local * segment, width)]

    stripes = [[p * column + c for p in range(PLANES)] for c in range(column)]
    pairs = [[d, d + 1] for d in range(0, devices, 2)]
    lanes_of = [
        [p * column + 2 * h + c for h in range(column // 2)]
        for p in range(PLANES)
        for c in range(2)
    ]

    def planes_swap(x):
        return lax.all_to_all(
            x, "dp", split_axis=0, concat_axis=0, tiled=True, axis_index_groups=stripes
        )

    def gather_all(x, axis, groups=None):
        return lax.all_gather(x, axis, axis=0, tiled=True, axis_index_groups=groups)

    share = frozen_key_weight.shape[0] // parts
    deep = frozen_key_weight.shape[1]
    weight = lax.dynamic_slice_in_dim(
        frozen_key_weight, lax.axis_index("groups") * share, share, 0
    )
    own_share = weight
    first.last += [own_share]

    def shape_weight(w):
        w = w.reshape(2, parts, column // 2, PLANES, share, deep)
        if share % 16 == 0:
            return w
        w = w.transpose(3, 2, 0, 1, 4, 5)
        return w.reshape(1, 1, 1, PLANES, column * parts * share, deep)

    def outward(size, side):
        lanes = jnp.arange(PLANES * size, dtype=jnp.int32)
        code = side * size + own_order
        return (lanes[:, None] == code[None, :]).astype(BF), (
            code[:, None] == lanes[None, :]
        ).astype(BF)

    def inward(size, turned=False):
        kth = jnp.arange(size, dtype=jnp.int32)
        target = jnp.sum(
            jnp.where(
                (order[:, None, :] == kth[None, :, None]) & (spot[:, None, :] >= 0),
                spot[:, None, :] + 1,
                0,
            ),
            axis=2,
        )
        if turned:
            there = (planes ^ plane)[:, None, None] == planes[None, :, None]
            target = jnp.sum(jnp.where(there, target[None], 0), axis=1)
        target = target.reshape(PLANES * size) - 1
        spots = jnp.arange(PLANES * most, dtype=jnp.int32)
        return (spots[:, None] == target[None, :]).astype(BF), (
            target[:, None] == spots[None, :]
        ).astype(BF)

    weight_z = gather_all(own_share, "dp", stripes)
    scaled_z = across(route(first, outward(most, own_goal ^ plane)[0], [scaled], [most] * PLANES))
    scaled_sent = route(first, inward(most, True)[0], scaled_z, blocks_out)

    def run(size):
        line = Line()
        total = PLANES * size
        out_rows, back_rows = outward(size, own_goal)
        spread, gather = inward(size)
        weight = gather_all(weight_z, "dp", lanes_of)
        acts_z = planes_swap(route(line, out_rows, [acts], [total])[0])
        got_scaled = at_owner(near(scaled_sent))
        back_low = back_project(line, adapter_up_slots, got_scaled)
        terms = adapter_terms(line, back_low, adapter_down_slots, owner_outs)
        terms = near(from_owner(terms))
        main = planes_swap(route(line, gather, terms, [total], (0, PLANES - 1, PLANES))[0])
        got = route(line, spread, [acts_z], blocks_out)
        weight = gather_all(hold(line, weight), "groups")
        last = planes_swap(route(line, gather, terms, [total], (PLANES - 1, PLANES, PLANES))[0])
        got = at_owner(near(got))
        low, grad_a = owner_step(line, back_low, adapter_down_slots, got)
        grad_b = up_gradient(line, low, got_scaled)
        line.last += [main]
        weight = gather_all(hold(line, weight), "dp", pairs)
        result = final_step(line, scaled, shape_weight(weight), back_rows, main, last)
        return result, grad_a, grad_b

    steps = [most * 11 // 16, most * 13 // 16, most]
    which = sum((need_all > s).astype(jnp.int32) for s in steps[:-1])
    return lax.switch(which, [functools.partial(run, s) for s in steps])


def solution(mesh):
    return jax.shard_map(
        shards,
        mesh=mesh,
        in_specs=(
            P(("groups", "dp"), None),
            P(("groups", "dp"), None),
            P("dp", None),
            P(("groups", "dp"), None, None),
            P(("groups", "dp"), None, None),
            P(("groups", "dp"), None),
            P("groups"),
            P("groups"),
        ),
        out_specs=(
            P(("groups", "dp"), None),
            P(("groups", "dp"), None, None),
            P(("groups", "dp"), None, None),
        ),
        check_vma=False,
    )
```

```python
import functools

import jax
import jax.numpy as jnp
from jax import lax
from jax.experimental import pallas as pl
from jax.experimental.pallas import tpu as pltpu
from jax.sharding import PartitionSpec as P

DELTA_MULTIPLIER = 0.25
BF = jnp.bfloat16
F32 = jnp.float32
PLANES = 4
PIECES = 4
PARAMS = pltpu.CompilerParams(vmem_limit_bytes=48 * 1024 * 1024)


def far(shape, dtype=BF):
    return pltpu.HBM(shape, dtype)


def whole(shape):
    zeros = (0,) * len(shape)
    return pl.BlockSpec(shape, lambda i: zeros)


def dot(a, b, ca=1, cb=0):
    return lax.dot_general(a, b, (((ca,), (cb,)), ((), ())), preferred_element_type=F32)


HERE = pl.BlockSpec(memory_space=pl.ANY)


def route_body(count, rows_ref, *refs):
    ins, outs = refs[:count], refs[count:]
    held = ins[0][...] if count == 1 else jnp.concatenate([r[...] for r in ins], axis=0)
    moved = dot(rows_ref[...], held).astype(BF)
    at = 0
    for out in outs:
        out[...] = moved[at : at + out.shape[0]]
        at += out.shape[0]


class Line:
    def __init__(self):
        self.last = []

    def call(self, body, operands, in_specs, out_specs, out_shape, pieces=1, scratch=()):
        after = self.last
        first = len(operands)
        many = isinstance(out_shape, list)

        def kernel(*refs):
            mark = len(refs) - 1 - len(scratch)
            refs[mark][...] = jnp.zeros_like(refs[mark])
            body(*refs[:first], *refs[first + len(after) : mark], *refs[mark + 1 :])

        out = pl.pallas_call(
            kernel,
            grid=(pieces,),
            in_specs=in_specs + [HERE] * len(after),
            out_specs=(out_specs if many else [out_specs]) + [whole((8, 128))],
            out_shape=(out_shape if many else [out_shape])
            + [jax.ShapeDtypeStruct((8, 128), jnp.int32)],
            scratch_shapes=scratch,
            compiler_params=PARAMS,
        )(*operands, *after)
        self.last = [out[-1]]
        return out[:-1] if many else out[0]


def route_body(count, rows_ref, *refs):
    ins, outs = refs[:count], refs[count:]
    held = ins[0][...] if count == 1 else jnp.concatenate([r[...] for r in ins], axis=0)
    moved = dot(rows_ref[...], held).astype(BF)
    at = 0
    for out in outs:
        out[...] = moved[at : at + out.shape[0]]
        at += out.shape[0]


class Line:
    def __init__(self):
        self.last = []

    def call(self, body, operands, in_specs, out_specs, out_shape, pieces=1, scratch=()):
        after = self.last
        first = len(operands)
        many = isinstance(out_shape, list)

        def kernel(*refs):
            mark = len(refs) - 1 - len(scratch)
            refs[mark][...] = jnp.zeros_like(refs[mark])
            body(*refs[:first], *refs[first + len(after) : mark], *refs[mark + 1 :])

        out = pl.pallas_call(
            kernel,
            grid=(pieces,),
            in_specs=in_specs + [HERE] * len(after),
            out_specs=(out_specs if many else [out_specs]) + [whole((8, 128))],
            out_shape=(out_shape if many else [out_shape])
            + [jax.ShapeDtypeStruct((8, 128), jnp.int32)],
            scratch_shapes=scratch,
            compiler_params=PARAMS,
        )(*operands, *after)
        self.last = [out[-1]]
        return out[:-1] if many else out[0]


def hold_body(ref, out):
    pass


def hold(line, x):
    last = line.last
    out = line.call(hold_body, [x], [FAR], FAR, far(x.shape, x.dtype), 1, {0: 0})
    line.last = last
    return out


def route(line, rows, ins, outs):
    width = ins[0].shape[1]
    pieces = PIECES if width % (128 * PIECES) == 0 else 1
    step = width // pieces
    return line.call(
        functools.partial(route_body, len(ins)),
        [rows, *ins],
        [whole(rows.shape)]
        + [pl.BlockSpec((x.shape[0], step), lambda i: (0, i)) for x in ins],
        [pl.BlockSpec((n, step), lambda i: (0, i)) for n in outs],
        [far((n, width)) for n in outs],
        pieces,
    )


def job_rows(refs, job):
    return jnp.concatenate([ref[job] for ref in refs], axis=0)


def back_body(count, up_ref, *refs):
    out = refs[count]
    for job in range(up_ref.shape[0]):
        held = job_rows(refs[:count], job)
        out[job] = (DELTA_MULTIPLIER * dot(held, up_ref[job], 1, 1)).astype(BF)


def back_project(line, up, rows):
    local, rank = up.shape[0], up.shape[1]
    shape = (local, sum(x.shape[1] for x in rows), rank)
    return line.call(
        functools.partial(back_body, len(rows)),
        [up, *rows],
        [whole(up.shape)] + [whole(x.shape) for x in rows],
        whole(shape),
        jax.ShapeDtypeStruct(shape, BF),
    )


def term_body(back_ref, down_ref, *outs):
    for job in range(down_ref.shape[0]):
        term = dot(back_ref[job], down_ref[job], 1, 1).astype(BF)
        at = 0
        for out in outs:
            out[job] = term[at : at + out.shape[1]]
            at += out.shape[1]


def adapter_terms(line, back_low, down, outs):
    local, width, rank = down.shape
    step = width // PIECES
    return line.call(
        term_body,
        [back_low, down],
        [whole(back_low.shape), pl.BlockSpec((local, step, rank), lambda i: (0, i, 0))],
        [pl.BlockSpec((local, n, step), lambda i: (0, 0, i)) for n in outs],
        [far((local, n, width)) for n in outs],
        PIECES,
    )


def owner_body(count, back_ref, down_ref, *refs):
    ins, (low_ref, grad_ref) = refs[:count], refs[count:]

    @pl.when(pl.program_id(0) == 0)
    def _():
        low_ref[...] = jnp.zeros_like(low_ref)

    for job in range(down_ref.shape[0]):
        held = job_rows(ins, job)
        low_ref[job] += dot(held, down_ref[job])
        grad_ref[job] = dot(held, back_ref[job], 0, 0).astype(BF)


def owner_step(line, back_low, down, rows):
    local, width, rank = down.shape
    step = width // PIECES
    part = pl.BlockSpec((local, step, rank), lambda i: (0, i, 0))
    low_shape = (local, back_low.shape[1], rank)
    return line.call(
        functools.partial(owner_body, len(rows)),
        [back_low, down, *rows],
        [whole(back_low.shape), part]
        + [pl.BlockSpec((local, x.shape[1], step), lambda i: (0, 0, i)) for x in rows],
        [whole(low_shape), part],
        [jax.ShapeDtypeStruct(low_shape, F32), jax.ShapeDtypeStruct(down.shape, BF)],
        PIECES,
    )


def up_body(count, low_ref, *refs):
    out = refs[count]
    for job in range(low_ref.shape[0]):
        low = low_ref[job].astype(BF)
        held = job_rows(refs[:count], job)
        out[job] = (DELTA_MULTIPLIER * dot(low, held, 0, 0)).astype(BF)


def up_gradient(line, low, rows):
    shape = (low.shape[0], low.shape[2], rows[0].shape[2])
    return line.call(
        functools.partial(up_body, len(rows)),
        [low, *rows],
        [whole(low.shape)] + [whole(x.shape) for x in rows],
        whole(shape),
        jax.ShapeDtypeStruct(shape, BF),
    )


def base_body(count, weight_ref, *refs):
    ins, outs = refs[:count], refs[count:]
    for x, out in zip(ins, outs):
        out[...] = dot(weight_ref[...], x[...], 1, 1).astype(BF)


def base_step(line, weight, rows):
    features, deep = weight.shape
    step, tokens = features // PLANES, rows[0].shape[0]
    return line.call(
        functools.partial(base_body, len(rows)),
        [weight, *rows],
        [pl.BlockSpec((step, deep), lambda i: (i, 0))] + [whole(x.shape) for x in rows],
        [pl.BlockSpec((step, tokens), lambda i: (i, 0)) for _ in rows],
        [far((features, tokens)) for _ in rows],
        PLANES,
    )


def final_body(count, rows_ref, came_ref, *refs):
    bases, out, held = refs[:count], refs[count], refs[count + 1]
    size = bases[0].shape[0]
    place = lax.rem(lax.axis_index("dp"), count)
    for s, ref in enumerate(bases):
        held[pl.ds(pl.multiple_of((place ^ s) * size, 16), size)] = ref[...]
    tokens = held.shape[1]
    one = (
        lax.broadcasted_iota(jnp.int32, (tokens, tokens), 0)
        == lax.broadcasted_iota(jnp.int32, (tokens, tokens), 1)
    ).astype(F32)
    base = dot(one.astype(BF), held[...], 1, 1)
    out[...] = (base + dot(rows_ref[...], came_ref[...])).astype(BF)


def final_step(line, rows, came, bases):
    tokens = rows.shape[0]
    step = came.shape[1] // PLANES
    size = step // len(bases)
    return line.call(
        functools.partial(final_body, len(bases)),
        [rows, came, *bases],
        [whole(rows.shape), pl.BlockSpec((came.shape[0], step), lambda i: (0, i))]
        + [pl.BlockSpec((size, tokens), lambda i: (i, 0)) for _ in bases],
        pl.BlockSpec((tokens, step), lambda i: (0, i)),
        jax.ShapeDtypeStruct((tokens, step * PLANES), BF),
        PLANES,
        [pltpu.VMEM((step, tokens), BF)],
    )


def shards(
    acts,
    cotan,
    frozen_key_weight,
    adapter_down_slots,
    adapter_up_slots,
    token_row_jobs,
    slot_owner_jobs,
    loss_token_count,
):
    devices = lax.axis_size("dp")
    parts = lax.axis_size("groups")
    tok_rows = acts.shape[0]
    local = adapter_down_slots.shape[0]
    jobs_all = slot_owner_jobs.shape[0]
    depth = 2 * tok_rows // (local * devices)
    column = devices // PLANES
    ring = column <= 4
    most = local * column * depth
    segment = PLANES * depth
    me = lax.axis_index("dp")
    plane, place = me // column, me % column

    first = Line()
    ids = token_row_jobs[:, 0]
    lengths = loss_token_count.astype(F32)
    weights = jnp.mean(lengths) / lengths
    numbers = jnp.arange(jobs_all, dtype=jnp.int32)
    row_weight = jnp.sum(jnp.where(ids[:, None] == numbers[None, :], weights[None, :], 0.0), axis=1)
    row_slot = jnp.sum(
        jnp.where(ids[:, None] == slot_owner_jobs[None, :], numbers[None, :], 0), axis=1
    )
    scaled = (row_weight[:, None] * cotan.astype(F32)).astype(BF)

    planes = jnp.arange(PLANES, dtype=jnp.int32)
    need = jnp.max(
        jnp.sum((row_slot[:, None] // (local * column) == planes[None, :]).astype(jnp.int32), axis=0)
    )
    note = jnp.concatenate([row_slot, jnp.full((128,), need, jnp.int32)])
    note = jnp.broadcast_to(note[None, None], (parts * devices, 1, tok_rows + 128))
    first.last = [note]
    notes = lax.all_to_all(
        note,
        ("groups", "dp"),
        split_axis=0,
        concat_axis=0,
        tiled=True,
    )[:, 0]
    need_all = jnp.max(notes[:, tok_rows])
    mine = notes[:, :tok_rows].reshape(parts, PLANES, column, tok_rows)
    mine = lax.dynamic_index_in_dim(mine, lax.axis_index("groups"), 0, keepdims=False)
    mine = lax.dynamic_index_in_dim(mine, place, 1, keepdims=False)
    slots = mine
    goal = slots // (local * column)
    earlier = jnp.arange(tok_rows)[None, :] < jnp.arange(tok_rows)[:, None]
    order = jnp.sum(
        ((goal[:, :, None] == goal[:, None, :]) & earlier[None]).astype(jnp.int32), axis=2
    )
    rank = jnp.sum(
        ((slots[:, :, None] == slots[:, None, :]) & earlier[None]).astype(jnp.int32), axis=2
    )
    owner = (slots // local) % column
    if ring:
        owner = owner ^ place
    spot = (
        owner * (local * segment)
        + (slots % local) * segment
        + planes[:, None] * depth
        + rank
    )
    spot = jnp.where(goal == plane, spot, -1)
    own_goal = row_slot // (local * column)
    own_order = jnp.sum(
        ((own_goal[:, None] == own_goal[None, :]) & earlier).astype(jnp.int32), axis=1
    )

    def across(bufs):
        return [bufs[0]] + [
            lax.ppermute(
                bufs[s],
                "dp",
                [(d, ((d // column) ^ s) * column + d % column) for d in range(devices)],
            )
            for s in range(1, PLANES)
        ]

    blocks = [[p * column + c for c in range(column)] for p in range(PLANES)]

    def within(x):
        return lax.all_to_all(
            x, "dp", split_axis=0, concat_axis=0, tiled=True, axis_index_groups=blocks
        )

    blocks_out = [local * segment] * column if ring else [column * local * segment]
    owner_outs = [segment] * column if ring else [column * segment]

    def near(bufs):
        if not ring:
            return [within(bufs[0])]
        return [bufs[0]] + [
            lax.ppermute(bufs[s], "dp", [(d, d ^ s) for d in range(devices)])
            for s in range(1, column)
        ]

    def at_owner(bufs):
        width = bufs[0].shape[1]
        if ring:
            return [x.reshape(local, segment, width) for x in bufs]
        x = bufs[0].reshape(column, local, segment, width).transpose(1, 0, 2, 3)
        return [x.reshape(local, column * segment, width)]

    def from_owner(bufs):
        width = bufs[0].shape[2]
        if ring:
            return [x.reshape(local * segment, width) for x in bufs]
        x = bufs[0].reshape(local, column, segment, width).transpose(1, 0, 2, 3)
        return [x.reshape(column * local * segment, width)]

    stripes = [[p * column + c for p in range(PLANES)] for c in range(column)]
    def planes_swap(x):
        return lax.all_to_all(
            x, "dp", split_axis=0, concat_axis=0, tiled=True, axis_index_groups=stripes
        )

    def gather_all(x, axis, groups=None):
        return lax.all_gather(x, axis, axis=0, tiled=True, axis_index_groups=groups)

    def outward(size, side):
        lanes = jnp.arange(PLANES * size, dtype=jnp.int32)
        code = side * size + own_order
        return (lanes[:, None] == code[None, :]).astype(BF), (
            code[:, None] == lanes[None, :]
        ).astype(BF)

    def inward(size, turned=False):
        kth = jnp.arange(size, dtype=jnp.int32)
        target = jnp.sum(
            jnp.where(
                (order[:, None, :] == kth[None, :, None]) & (spot[:, None, :] >= 0),
                spot[:, None, :] + 1,
                0,
            ),
            axis=2,
        )
        if turned:
            there = (planes ^ plane)[:, None, None] == planes[None, :, None]
            target = jnp.sum(jnp.where(there, target[None], 0), axis=1)
        target = target.reshape(PLANES * size) - 1
        spots = jnp.arange(PLANES * most, dtype=jnp.int32)
        return (spots[:, None] == target[None, :]).astype(BF), (
            target[:, None] == spots[None, :]
        ).astype(BF)

    scaled_z = across(route(first, outward(most, own_goal ^ plane)[0], [scaled], [most] * PLANES))
    scaled_sent = route(first, inward(most, True)[0], scaled_z, blocks_out)

    if ring:
        mates = near([scaled] * column)

    def run(size):
        line = Line()
        total = PLANES * size
        out_rows, back_rows = outward(size, own_goal)
        spread, gather = inward(size)
        if ring:
            weight = gather_all(frozen_key_weight, "dp", stripes)
        else:
            weight = gather_all(frozen_key_weight, "dp")
        acts_z = planes_swap(route(line, out_rows, [acts], [total])[0])
        got_scaled = at_owner(near(scaled_sent))
        back_low = back_project(line, adapter_up_slots, got_scaled)
        terms = adapter_terms(line, back_low, adapter_down_slots, owner_outs)
        terms = near(from_owner(terms))
        came = planes_swap(route(line, gather, terms, [total])[0])
        if ring:
            bases = near(base_step(line, weight, mates))
            line.last += bases[1:]
        else:
            bases = [dot(weight, scaled, 1, 1).astype(BF)]
        got = route(line, spread, [acts_z], blocks_out)
        got = at_owner(near(got))
        low, grad_a = owner_step(line, back_low, adapter_down_slots, got)
        grad_b = up_gradient(line, low, got_scaled)
        result = final_step(line, back_rows, came, bases)
        return result, grad_a, grad_b

    steps = [most * 11 // 16, most * 13 // 16, most]
    which = sum((need_all > s).astype(jnp.int32) for s in steps[:-1])
    return lax.switch(which, [functools.partial(run, s) for s in steps])


def solution(mesh):
    return jax.shard_map(
        shards,
        mesh=mesh,
        in_specs=(
            P(("groups", "dp"), None),
            P(("groups", "dp"), None),
            P("dp", None),
            P(("groups", "dp"), None, None),
            P(("groups", "dp"), None, None),
            P(("groups", "dp"), None),
            P("groups"),
            P("groups"),
        ),
        out_specs=(
            P(("groups", "dp"), None),
            P(("groups", "dp"), None, None),
            P(("groups", "dp"), None, None),
        ),
        check_vma=False,
    )
```

```python
import functools

import jax
import jax.numpy as jnp
from jax import lax
from jax.experimental import pallas as pl
from jax.experimental.pallas import tpu as pltpu
from jax.sharding import PartitionSpec as P

DELTA_MULTIPLIER = 0.25
BF = jnp.bfloat16
F32 = jnp.float32
PLANES = 4
PIECES = 4
PARAMS = pltpu.CompilerParams(vmem_limit_bytes=48 * 1024 * 1024)


def far(shape, dtype=BF):
    return pltpu.HBM(shape, dtype)


def whole(shape):
    zeros = (0,) * len(shape)
    return pl.BlockSpec(shape, lambda i: zeros)


def dot(a, b, ca=1, cb=0):
    return lax.dot_general(a, b, (((ca,), (cb,)), ((), ())), preferred_element_type=F32)


HERE = pl.BlockSpec(memory_space=pl.ANY)


def route_body(count, rows_ref, *refs):
    ins, outs = refs[:count], refs[count:]
    held = ins[0][...] if count == 1 else jnp.concatenate([r[...] for r in ins], axis=0)
    moved = dot(rows_ref[...], held).astype(BF)
    at = 0
    for out in outs:
        out[...] = moved[at : at + out.shape[0]]
        at += out.shape[0]


class Line:
    def __init__(self):
        self.last = []

    def call(self, body, operands, in_specs, out_specs, out_shape, pieces=1, scratch=()):
        after = self.last
        first = len(operands)
        many = isinstance(out_shape, list)

        def kernel(*refs):
            mark = len(refs) - 1 - len(scratch)
            refs[mark][...] = jnp.zeros_like(refs[mark])
            body(*refs[:first], *refs[first + len(after) : mark], *refs[mark + 1 :])

        out = pl.pallas_call(
            kernel,
            grid=(pieces,),
            in_specs=in_specs + [HERE] * len(after),
            out_specs=(out_specs if many else [out_specs]) + [whole((8, 128))],
            out_shape=(out_shape if many else [out_shape])
            + [jax.ShapeDtypeStruct((8, 128), jnp.int32)],
            scratch_shapes=scratch,
            compiler_params=PARAMS,
        )(*operands, *after)
        self.last = [out[-1]]
        return out[:-1] if many else out[0]


def route_body(count, rows_ref, *refs):
    ins, outs = refs[:count], refs[count:]
    held = ins[0][...] if count == 1 else jnp.concatenate([r[...] for r in ins], axis=0)
    moved = dot(rows_ref[...], held).astype(BF)
    at = 0
    for out in outs:
        out[...] = moved[at : at + out.shape[0]]
        at += out.shape[0]


class Line:
    def __init__(self):
        self.last = []

    def call(self, body, operands, in_specs, out_specs, out_shape, pieces=1, scratch=()):
        after = self.last
        first = len(operands)
        many = isinstance(out_shape, list)

        def kernel(*refs):
            mark = len(refs) - 1 - len(scratch)
            refs[mark][...] = jnp.zeros_like(refs[mark])
            body(*refs[:first], *refs[first + len(after) : mark], *refs[mark + 1 :])

        out = pl.pallas_call(
            kernel,
            grid=(pieces,),
            in_specs=in_specs + [HERE] * len(after),
            out_specs=(out_specs if many else [out_specs]) + [whole((8, 128))],
            out_shape=(out_shape if many else [out_shape])
            + [jax.ShapeDtypeStruct((8, 128), jnp.int32)],
            scratch_shapes=scratch,
            compiler_params=PARAMS,
        )(*operands, *after)
        self.last = [out[-1]]
        return out[:-1] if many else out[0]


def hold_body(ref, out):
    pass


def hold(line, x):
    last = line.last
    out = line.call(hold_body, [x], [FAR], FAR, far(x.shape, x.dtype), 1, {0: 0})
    line.last = last
    return out


def route(line, rows, ins, outs):
    width = ins[0].shape[1]
    pieces = PIECES if width % (128 * PIECES) == 0 else 1
    step = width // pieces
    return line.call(
        functools.partial(route_body, len(ins)),
        [rows, *ins],
        [whole(rows.shape)]
        + [pl.BlockSpec((x.shape[0], step), lambda i: (0, i)) for x in ins],
        [pl.BlockSpec((n, step), lambda i: (0, i)) for n in outs],
        [far((n, width)) for n in outs],
        pieces,
    )


def job_rows(refs, job):
    return jnp.concatenate([ref[job] for ref in refs], axis=0)


def back_body(count, up_ref, *refs):
    out = refs[count]
    for job in range(up_ref.shape[0]):
        held = job_rows(refs[:count], job)
        out[job] = (DELTA_MULTIPLIER * dot(held, up_ref[job], 1, 1)).astype(BF)


def back_project(line, up, rows):
    local, rank = up.shape[0], up.shape[1]
    shape = (local, sum(x.shape[1] for x in rows), rank)
    return line.call(
        functools.partial(back_body, len(rows)),
        [up, *rows],
        [whole(up.shape)] + [whole(x.shape) for x in rows],
        whole(shape),
        jax.ShapeDtypeStruct(shape, BF),
    )


def term_body(back_ref, down_ref, *outs):
    for job in range(down_ref.shape[0]):
        term = dot(back_ref[job], down_ref[job], 1, 1).astype(BF)
        at = 0
        for out in outs:
            out[job] = term[at : at + out.shape[1]]
            at += out.shape[1]


def adapter_terms(line, back_low, down, outs):
    local, width, rank = down.shape
    step = width // PIECES
    return line.call(
        term_body,
        [back_low, down],
        [whole(back_low.shape), pl.BlockSpec((local, step, rank), lambda i: (0, i, 0))],
        [pl.BlockSpec((local, n, step), lambda i: (0, 0, i)) for n in outs],
        [far((local, n, width)) for n in outs],
        PIECES,
    )


def owner_body(count, back_ref, down_ref, *refs):
    ins, (low_ref, grad_ref) = refs[:count], refs[count:]

    @pl.when(pl.program_id(0) == 0)
    def _():
        low_ref[...] = jnp.zeros_like(low_ref)

    for job in range(down_ref.shape[0]):
        held = job_rows(ins, job)
        low_ref[job] += dot(held, down_ref[job])
        grad_ref[job] = dot(held, back_ref[job], 0, 0).astype(BF)


def owner_step(line, back_low, down, rows):
    local, width, rank = down.shape
    step = width // PIECES
    part = pl.BlockSpec((local, step, rank), lambda i: (0, i, 0))
    low_shape = (local, back_low.shape[1], rank)
    return line.call(
        functools.partial(owner_body, len(rows)),
        [back_low, down, *rows],
        [whole(back_low.shape), part]
        + [pl.BlockSpec((local, x.shape[1], step), lambda i: (0, 0, i)) for x in rows],
        [whole(low_shape), part],
        [jax.ShapeDtypeStruct(low_shape, F32), jax.ShapeDtypeStruct(down.shape, BF)],
        PIECES,
    )


def up_body(count, low_ref, *refs):
    out = refs[count]
    for job in range(low_ref.shape[0]):
        low = low_ref[job].astype(BF)
        held = job_rows(refs[:count], job)
        out[job] = (DELTA_MULTIPLIER * dot(low, held, 0, 0)).astype(BF)


def up_gradient(line, low, rows):
    shape = (low.shape[0], low.shape[2], rows[0].shape[2])
    return line.call(
        functools.partial(up_body, len(rows)),
        [low, *rows],
        [whole(low.shape)] + [whole(x.shape) for x in rows],
        whole(shape),
        jax.ShapeDtypeStruct(shape, BF),
    )


def base_body(count, weight_ref, *refs):
    ins, outs = refs[:count], refs[count:]
    weight = jnp.concatenate([weight_ref[at, 0] for at in range(weight_ref.shape[0])], axis=0)
    for x, out in zip(ins, outs):
        out[...] = dot(weight, x[...], 1, 1).astype(BF)


def base_step(line, weight, rows):
    parts, planes, share, deep = weight.shape
    step, tokens = parts * share, rows[0].shape[0]
    return line.call(
        functools.partial(base_body, len(rows)),
        [weight, *rows],
        [pl.BlockSpec((parts, 1, share, deep), lambda i: (0, i, 0, 0))]
        + [whole(x.shape) for x in rows],
        [pl.BlockSpec((step, tokens), lambda i: (i, 0)) for _ in rows],
        [far((planes * step, tokens)) for _ in rows],
        planes,
    )


def final_body(count, rows_ref, came_ref, *refs):
    bases, out, held = refs[:count], refs[count], refs[count + 1]
    size = bases[0].shape[0]
    place = lax.rem(lax.axis_index("dp"), count)
    for s, ref in enumerate(bases):
        held[pl.ds(pl.multiple_of((place ^ s) * size, 16), size)] = ref[...]
    tokens = held.shape[1]
    one = (
        lax.broadcasted_iota(jnp.int32, (tokens, tokens), 0)
        == lax.broadcasted_iota(jnp.int32, (tokens, tokens), 1)
    ).astype(F32)
    base = dot(one.astype(BF), held[...], 1, 1)
    out[...] = (base + dot(rows_ref[...], came_ref[...])).astype(BF)


def final_step(line, rows, came, bases):
    tokens = rows.shape[0]
    step = came.shape[1] // PLANES
    size = step // len(bases)
    return line.call(
        functools.partial(final_body, len(bases)),
        [rows, came, *bases],
        [whole(rows.shape), pl.BlockSpec((came.shape[0], step), lambda i: (0, i))]
        + [pl.BlockSpec((size, tokens), lambda i: (i, 0)) for _ in bases],
        pl.BlockSpec((tokens, step), lambda i: (0, i)),
        jax.ShapeDtypeStruct((tokens, step * PLANES), BF),
        PLANES,
        [pltpu.VMEM((step, tokens), BF)],
    )


def shards(
    acts,
    cotan,
    frozen_key_weight,
    adapter_down_slots,
    adapter_up_slots,
    token_row_jobs,
    slot_owner_jobs,
    loss_token_count,
):
    devices = lax.axis_size("dp")
    parts = lax.axis_size("groups")
    tok_rows = acts.shape[0]
    local = adapter_down_slots.shape[0]
    jobs_all = slot_owner_jobs.shape[0]
    depth = 2 * tok_rows // (local * devices)
    column = devices // PLANES
    ring = column <= 4
    most = local * column * depth
    segment = PLANES * depth
    me = lax.axis_index("dp")
    plane, place = me // column, me % column

    first = Line()
    ids = token_row_jobs[:, 0]
    lengths = loss_token_count.astype(F32)
    weights = jnp.mean(lengths) / lengths
    numbers = jnp.arange(jobs_all, dtype=jnp.int32)
    row_weight = jnp.sum(jnp.where(ids[:, None] == numbers[None, :], weights[None, :], 0.0), axis=1)
    row_slot = jnp.sum(
        jnp.where(ids[:, None] == slot_owner_jobs[None, :], numbers[None, :], 0), axis=1
    )
    scaled = (row_weight[:, None] * cotan.astype(F32)).astype(BF)

    planes = jnp.arange(PLANES, dtype=jnp.int32)
    need = jnp.max(
        jnp.sum((row_slot[:, None] // (local * column) == planes[None, :]).astype(jnp.int32), axis=0)
    )
    note = jnp.concatenate([row_slot, jnp.full((128,), need, jnp.int32)])
    note = jnp.broadcast_to(note[None, None], (parts * devices, 1, tok_rows + 128))
    first.last = [note]
    notes = lax.all_to_all(
        note,
        ("groups", "dp"),
        split_axis=0,
        concat_axis=0,
        tiled=True,
    )[:, 0]
    need_all = jnp.max(notes[:, tok_rows])
    mine = notes[:, :tok_rows].reshape(parts, PLANES, column, tok_rows)
    mine = lax.dynamic_index_in_dim(mine, lax.axis_index("groups"), 0, keepdims=False)
    mine = lax.dynamic_index_in_dim(mine, place, 1, keepdims=False)
    slots = mine
    goal = slots // (local * column)
    earlier = jnp.arange(tok_rows)[None, :] < jnp.arange(tok_rows)[:, None]
    order = jnp.sum(
        ((goal[:, :, None] == goal[:, None, :]) & earlier[None]).astype(jnp.int32), axis=2
    )
    rank = jnp.sum(
        ((slots[:, :, None] == slots[:, None, :]) & earlier[None]).astype(jnp.int32), axis=2
    )
    owner = (slots // local) % column
    if ring:
        owner = owner ^ place
    spot = (
        owner * (local * segment)
        + (slots % local) * segment
        + planes[:, None] * depth
        + rank
    )
    spot = jnp.where(goal == plane, spot, -1)
    own_goal = row_slot // (local * column)
    own_order = jnp.sum(
        ((own_goal[:, None] == own_goal[None, :]) & earlier).astype(jnp.int32), axis=1
    )

    def across(bufs):
        return [bufs[0]] + [
            lax.ppermute(
                bufs[s],
                "dp",
                [(d, ((d // column) ^ s) * column + d % column) for d in range(devices)],
            )
            for s in range(1, PLANES)
        ]

    blocks = [[p * column + c for c in range(column)] for p in range(PLANES)]

    def within(x):
        return lax.all_to_all(
            x, "dp", split_axis=0, concat_axis=0, tiled=True, axis_index_groups=blocks
        )

    blocks_out = [local * segment] * column if ring else [column * local * segment]
    owner_outs = [segment] * column if ring else [column * segment]

    def near(bufs):
        if not ring:
            return [within(bufs[0])]
        return [bufs[0]] + [
            lax.ppermute(bufs[s], "dp", [(d, d ^ s) for d in range(devices)])
            for s in range(1, column)
        ]

    def at_owner(bufs):
        width = bufs[0].shape[1]
        if ring:
            return [x.reshape(local, segment, width) for x in bufs]
        x = bufs[0].reshape(column, local, segment, width).transpose(1, 0, 2, 3)
        return [x.reshape(local, column * segment, width)]

    def from_owner(bufs):
        width = bufs[0].shape[2]
        if ring:
            return [x.reshape(local * segment, width) for x in bufs]
        x = bufs[0].reshape(local, column, segment, width).transpose(1, 0, 2, 3)
        return [x.reshape(column * local * segment, width)]

    stripes = [[p * column + c for p in range(PLANES)] for c in range(column)]
    def planes_swap(x):
        return lax.all_to_all(
            x, "dp", split_axis=0, concat_axis=0, tiled=True, axis_index_groups=stripes
        )

    def gather_all(x, axis, groups=None):
        return lax.all_gather(x, axis, axis=0, tiled=True, axis_index_groups=groups)

    def outward(size, side):
        lanes = jnp.arange(PLANES * size, dtype=jnp.int32)
        code = side * size + own_order
        return (lanes[:, None] == code[None, :]).astype(BF), (
            code[:, None] == lanes[None, :]
        ).astype(BF)

    def inward(size, turned=False):
        kth = jnp.arange(size, dtype=jnp.int32)
        target = jnp.sum(
            jnp.where(
                (order[:, None, :] == kth[None, :, None]) & (spot[:, None, :] >= 0),
                spot[:, None, :] + 1,
                0,
            ),
            axis=2,
        )
        if turned:
            there = (planes ^ plane)[:, None, None] == planes[None, :, None]
            target = jnp.sum(jnp.where(there, target[None], 0), axis=1)
        target = target.reshape(PLANES * size) - 1
        spots = jnp.arange(PLANES * most, dtype=jnp.int32)
        return (spots[:, None] == target[None, :]).astype(BF), (
            target[:, None] == spots[None, :]
        ).astype(BF)

    share = frozen_key_weight.shape[0] // parts
    deep = frozen_key_weight.shape[1]
    if ring:
        weight_z = lax.dynamic_slice_in_dim(
            frozen_key_weight, lax.axis_index("groups") * share, share, 0
        )
        first.last += [weight_z]
        weight_z = gather_all(weight_z, "dp", stripes)
    rows_out = outward(most, own_goal ^ plane)[0]
    lanes = jnp.arange(tok_rows, dtype=jnp.int32)
    same_rows = (lanes[:, None] == lanes[None, :]).astype(BF)
    *scaled_z, scaled_copy = route(
        first, jnp.concatenate([rows_out, same_rows]), [scaled], [most] * PLANES + [tok_rows]
    )
    scaled_z = across(scaled_z)
    if ring:
        mates = near([scaled_copy] * column)
        first.last += [weight_z]
    scaled_sent = route(first, inward(most, True)[0], scaled_z, blocks_out)

    def run(size):
        line = Line()
        total = PLANES * size
        out_rows, back_rows = outward(size, own_goal)
        spread, gather = inward(size)
        if ring:
            weight = gather_all(weight_z, "groups").reshape(parts, PLANES, share, deep)
        else:
            weight = gather_all(frozen_key_weight, "dp")
        acts_z = planes_swap(route(line, out_rows, [acts], [total])[0])
        got_scaled = at_owner(near(scaled_sent))
        back_low = back_project(line, adapter_up_slots, got_scaled)
        terms = adapter_terms(line, back_low, adapter_down_slots, owner_outs)
        terms = near(from_owner(terms))
        if ring:
            bases = near(base_step(line, weight, mates))
        else:
            bases = [dot(weight, scaled, 1, 1).astype(BF)]
        came = planes_swap(route(line, gather, terms, [total])[0])
        if ring:
            line.last += bases[1:]
        got = route(line, spread, [acts_z], blocks_out)
        got = at_owner(near(got))
        low, grad_a = owner_step(line, back_low, adapter_down_slots, got)
        grad_b = up_gradient(line, low, got_scaled)
        result = final_step(line, back_rows, came, bases)
        return result, grad_a, grad_b

    steps = [most * 11 // 16, most * 13 // 16, most]
    which = sum((need_all > s).astype(jnp.int32) for s in steps[:-1])
    return lax.switch(which, [functools.partial(run, s) for s in steps])


def solution(mesh):
    return jax.shard_map(
        shards,
        mesh=mesh,
        in_specs=(
            P(("groups", "dp"), None),
            P(("groups", "dp"), None),
            P("dp", None),
            P(("groups", "dp"), None, None),
            P(("groups", "dp"), None, None),
            P(("groups", "dp"), None),
            P("groups"),
            P("groups"),
        ),
        out_specs=(
            P(("groups", "dp"), None),
            P(("groups", "dp"), None, None),
            P(("groups", "dp"), None, None),
        ),
        check_vma=False,
    )
```

```python
import functools

import jax
import jax.numpy as jnp
from jax import lax
from jax.experimental import pallas as pl
from jax.experimental.pallas import tpu as pltpu
from jax.sharding import PartitionSpec as P

DELTA_MULTIPLIER = 0.25
BF = jnp.bfloat16
F32 = jnp.float32
PLANES = 4
PIECES = 4
PARAMS = pltpu.CompilerParams(vmem_limit_bytes=48 * 1024 * 1024)


def far(shape, dtype=BF):
    return pltpu.HBM(shape, dtype)


def whole(shape):
    zeros = (0,) * len(shape)
    return pl.BlockSpec(shape, lambda i: zeros)


def dot(a, b, ca=1, cb=0):
    return lax.dot_general(a, b, (((ca,), (cb,)), ((), ())), preferred_element_type=F32)


HERE = pl.BlockSpec(memory_space=pl.ANY)


def note_body(ref, out):
    out[...] = ref[...]


def note_step(line, note):
    return line.call(
        note_body,
        [note],
        [whole(note.shape)],
        whole(note.shape),
        jax.ShapeDtypeStruct(note.shape, note.dtype),
    )


def route_body(count, rows_ref, *refs):
    ins, outs = refs[:count], refs[count:]
    held = ins[0][...] if count == 1 else jnp.concatenate([r[...] for r in ins], axis=0)
    moved = dot(rows_ref[...], held).astype(BF)
    at = 0
    for out in outs:
        out[...] = moved[at : at + out.shape[0]]
        at += out.shape[0]


class Line:
    def __init__(self):
        self.last = []

    def call(self, body, operands, in_specs, out_specs, out_shape, pieces=1, scratch=()):
        after = self.last
        first = len(operands)
        many = isinstance(out_shape, list)

        def kernel(*refs):
            mark = len(refs) - 1 - len(scratch)
            refs[mark][...] = jnp.zeros_like(refs[mark])
            body(*refs[:first], *refs[first + len(after) : mark], *refs[mark + 1 :])

        out = pl.pallas_call(
            kernel,
            grid=(pieces,),
            in_specs=in_specs + [HERE] * len(after),
            out_specs=(out_specs if many else [out_specs]) + [whole((8, 128))],
            out_shape=(out_shape if many else [out_shape])
            + [jax.ShapeDtypeStruct((8, 128), jnp.int32)],
            scratch_shapes=scratch,
            compiler_params=PARAMS,
        )(*operands, *after)
        self.last = [out[-1]]
        return out[:-1] if many else out[0]


def route_body(count, rows_ref, *refs):
    ins, outs = refs[:count], refs[count:]
    held = ins[0][...] if count == 1 else jnp.concatenate([r[...] for r in ins], axis=0)
    moved = dot(rows_ref[...], held).astype(BF)
    at = 0
    for out in outs:
        out[...] = moved[at : at + out.shape[0]]
        at += out.shape[0]


class Line:
    def __init__(self):
        self.last = []

    def call(self, body, operands, in_specs, out_specs, out_shape, pieces=1, scratch=()):
        after = self.last
        first = len(operands)
        many = isinstance(out_shape, list)

        def kernel(*refs):
            mark = len(refs) - 1 - len(scratch)
            refs[mark][...] = jnp.zeros_like(refs[mark])
            body(*refs[:first], *refs[first + len(after) : mark], *refs[mark + 1 :])

        out = pl.pallas_call(
            kernel,
            grid=(pieces,),
            in_specs=in_specs + [HERE] * len(after),
            out_specs=(out_specs if many else [out_specs]) + [whole((8, 128))],
            out_shape=(out_shape if many else [out_shape])
            + [jax.ShapeDtypeStruct((8, 128), jnp.int32)],
            scratch_shapes=scratch,
            compiler_params=PARAMS,
        )(*operands, *after)
        self.last = [out[-1]]
        return out[:-1] if many else out[0]


def hold_body(ref, out):
    pass


def hold(line, x):
    last = line.last
    out = line.call(hold_body, [x], [FAR], FAR, far(x.shape, x.dtype), 1, {0: 0})
    line.last = last
    return out


def route(line, rows, ins, outs):
    width = ins[0].shape[1]
    pieces = PIECES if width % (128 * PIECES) == 0 else 1
    step = width // pieces
    return line.call(
        functools.partial(route_body, len(ins)),
        [rows, *ins],
        [whole(rows.shape)]
        + [pl.BlockSpec((x.shape[0], step), lambda i: (0, i)) for x in ins],
        [pl.BlockSpec((n, step), lambda i: (0, i)) for n in outs],
        [far((n, width)) for n in outs],
        pieces,
    )


def job_rows(refs, job):
    return jnp.concatenate([ref[job] for ref in refs], axis=0)


def back_body(count, up_ref, *refs):
    out = refs[count]
    for job in range(up_ref.shape[0]):
        held = job_rows(refs[:count], job)
        out[job] = (DELTA_MULTIPLIER * dot(held, up_ref[job], 1, 1)).astype(BF)


def back_project(line, up, rows):
    local, rank = up.shape[0], up.shape[1]
    shape = (local, sum(x.shape[1] for x in rows), rank)
    return line.call(
        functools.partial(back_body, len(rows)),
        [up, *rows],
        [whole(up.shape)] + [whole(x.shape) for x in rows],
        whole(shape),
        jax.ShapeDtypeStruct(shape, BF),
    )


def term_body(back_ref, down_ref, *outs):
    for job in range(down_ref.shape[0]):
        term = dot(back_ref[job], down_ref[job], 1, 1).astype(BF)
        at = 0
        for out in outs:
            out[job] = term[at : at + out.shape[1]]
            at += out.shape[1]


def adapter_terms(line, back_low, down, outs):
    local, width, rank = down.shape
    step = width // PIECES
    return line.call(
        term_body,
        [back_low, down],
        [whole(back_low.shape), pl.BlockSpec((local, step, rank), lambda i: (0, i, 0))],
        [pl.BlockSpec((local, n, step), lambda i: (0, 0, i)) for n in outs],
        [far((local, n, width)) for n in outs],
        PIECES,
    )


def owner_body(count, back_ref, down_ref, *refs):
    ins, (low_ref, grad_ref) = refs[:count], refs[count:]

    @pl.when(pl.program_id(0) == 0)
    def _():
        low_ref[...] = jnp.zeros_like(low_ref)

    for job in range(down_ref.shape[0]):
        held = job_rows(ins, job)
        low_ref[job] += dot(held, down_ref[job])
        grad_ref[job] = dot(held, back_ref[job], 0, 0).astype(BF)


def owner_step(line, back_low, down, rows):
    local, width, rank = down.shape
    step = width // PIECES
    part = pl.BlockSpec((local, step, rank), lambda i: (0, i, 0))
    low_shape = (local, back_low.shape[1], rank)
    return line.call(
        functools.partial(owner_body, len(rows)),
        [back_low, down, *rows],
        [whole(back_low.shape), part]
        + [pl.BlockSpec((local, x.shape[1], step), lambda i: (0, 0, i)) for x in rows],
        [whole(low_shape), part],
        [jax.ShapeDtypeStruct(low_shape, F32), jax.ShapeDtypeStruct(down.shape, BF)],
        PIECES,
    )


def up_body(count, low_ref, *refs):
    out = refs[count]
    for job in range(low_ref.shape[0]):
        low = low_ref[job].astype(BF)
        held = job_rows(refs[:count], job)
        out[job] = (DELTA_MULTIPLIER * dot(low, held, 0, 0)).astype(BF)


def up_gradient(line, low, rows):
    shape = (low.shape[0], low.shape[2], rows[0].shape[2])
    return line.call(
        functools.partial(up_body, len(rows)),
        [low, *rows],
        [whole(low.shape)] + [whole(x.shape) for x in rows],
        whole(shape),
        jax.ShapeDtypeStruct(shape, BF),
    )


def base_body(count, weight_ref, *refs):
    ins, outs = refs[:count], refs[count:]
    weight = jnp.concatenate([weight_ref[at, 0] for at in range(weight_ref.shape[0])], axis=0)
    for x, out in zip(ins, outs):
        out[...] = dot(weight, x[...], 1, 1).astype(BF)


def base_step(line, weight, rows):
    parts, planes, share, deep = weight.shape
    step, tokens = parts * share, rows[0].shape[0]
    return line.call(
        functools.partial(base_body, len(rows)),
        [weight, *rows],
        [pl.BlockSpec((parts, 1, share, deep), lambda i: (0, i, 0, 0))]
        + [whole(x.shape) for x in rows],
        [pl.BlockSpec((step, tokens), lambda i: (i, 0)) for _ in rows],
        [far((planes * step, tokens)) for _ in rows],
        planes,
    )


def final_body(count, rows_ref, came_ref, *refs):
    bases, out, held = refs[:count], refs[count], refs[count + 1]
    size = bases[0].shape[0]
    place = lax.rem(lax.axis_index("dp"), count)
    for s, ref in enumerate(bases):
        held[pl.ds(pl.multiple_of((place ^ s) * size, 16), size)] = ref[...]
    tokens = held.shape[1]
    one = (
        lax.broadcasted_iota(jnp.int32, (tokens, tokens), 0)
        == lax.broadcasted_iota(jnp.int32, (tokens, tokens), 1)
    ).astype(F32)
    base = dot(one.astype(BF), held[...], 1, 1)
    out[...] = (base + dot(rows_ref[...], came_ref[...])).astype(BF)


def final_step(line, rows, came, bases):
    tokens = rows.shape[0]
    step = came.shape[1] // PLANES
    size = step // len(bases)
    return line.call(
        functools.partial(final_body, len(bases)),
        [rows, came, *bases],
        [whole(rows.shape), pl.BlockSpec((came.shape[0], step), lambda i: (0, i))]
        + [pl.BlockSpec((size, tokens), lambda i: (i, 0)) for _ in bases],
        pl.BlockSpec((tokens, step), lambda i: (0, i)),
        jax.ShapeDtypeStruct((tokens, step * PLANES), BF),
        PLANES,
        [pltpu.VMEM((step, tokens), BF)],
    )


def shards(
    acts,
    cotan,
    frozen_key_weight,
    adapter_down_slots,
    adapter_up_slots,
    token_row_jobs,
    slot_owner_jobs,
    loss_token_count,
):
    devices = lax.axis_size("dp")
    parts = lax.axis_size("groups")
    tok_rows = acts.shape[0]
    local = adapter_down_slots.shape[0]
    jobs_all = slot_owner_jobs.shape[0]
    depth = 2 * tok_rows // (local * devices)
    column = devices // PLANES
    ring = column <= 4
    most = local * column * depth
    segment = PLANES * depth
    me = lax.axis_index("dp")
    plane, place = me // column, me % column

    first = Line()
    stripes = [[p * column + c for p in range(PLANES)] for c in range(column)]
    ids = token_row_jobs[:, 0]
    lengths = loss_token_count.astype(F32)
    weights = jnp.mean(lengths) / lengths
    numbers = jnp.arange(jobs_all, dtype=jnp.int32)
    row_weight = jnp.sum(jnp.where(ids[:, None] == numbers[None, :], weights[None, :], 0.0), axis=1)
    row_slot = jnp.sum(
        jnp.where(ids[:, None] == slot_owner_jobs[None, :], numbers[None, :], 0), axis=1
    )
    scaled = (row_weight[:, None] * cotan.astype(F32)).astype(BF)

    planes = jnp.arange(PLANES, dtype=jnp.int32)
    need = jnp.max(
        jnp.sum((row_slot[:, None] // (local * column) == planes[None, :]).astype(jnp.int32), axis=0)
    )
    note = jnp.concatenate([row_slot, jnp.full((128,), need, jnp.int32)])
    share = frozen_key_weight.shape[0] // parts
    deep = frozen_key_weight.shape[1]
    own_share = lax.dynamic_slice_in_dim(
        frozen_key_weight, lax.axis_index("groups") * share, share, 0
    )
    if ring:
        weight_z = lax.all_gather(
            own_share, "dp", axis=0, tiled=True, axis_index_groups=stripes
        )
        first.last = [own_share]
        note = note_step(first, note[None])[0]
    note = jnp.broadcast_to(note[None, None], (parts * devices, 1, tok_rows + 128))
    first.last = [note]
    notes = lax.all_to_all(
        note,
        ("groups", "dp"),
        split_axis=0,
        concat_axis=0,
        tiled=True,
    )[:, 0]
    need_all = jnp.max(notes[:, tok_rows])
    mine = notes[:, :tok_rows].reshape(parts, PLANES, column, tok_rows)
    mine = lax.dynamic_index_in_dim(mine, lax.axis_index("groups"), 0, keepdims=False)
    mine = lax.dynamic_index_in_dim(mine, place, 1, keepdims=False)
    slots = mine
    goal = slots // (local * column)
    earlier = jnp.arange(tok_rows)[None, :] < jnp.arange(tok_rows)[:, None]
    order = jnp.sum(
        ((goal[:, :, None] == goal[:, None, :]) & earlier[None]).astype(jnp.int32), axis=2
    )
    rank = jnp.sum(
        ((slots[:, :, None] == slots[:, None, :]) & earlier[None]).astype(jnp.int32), axis=2
    )
    owner = (slots // local) % column
    if ring:
        owner = owner ^ place
    spot = (
        owner * (local * segment)
        + (slots % local) * segment
        + planes[:, None] * depth
        + rank
    )
    spot = jnp.where(goal == plane, spot, -1)
    own_goal = row_slot // (local * column)
    own_order = jnp.sum(
        ((own_goal[:, None] == own_goal[None, :]) & earlier).astype(jnp.int32), axis=1
    )

    def across(bufs):
        return [bufs[0]] + [
            lax.ppermute(
                bufs[s],
                "dp",
                [(d, ((d // column) ^ s) * column + d % column) for d in range(devices)],
            )
            for s in range(1, PLANES)
        ]

    blocks = [[p * column + c for c in range(column)] for p in range(PLANES)]

    def within(x):
        return lax.all_to_all(
            x, "dp", split_axis=0, concat_axis=0, tiled=True, axis_index_groups=blocks
        )

    blocks_out = [local * segment] * column if ring else [column * local * segment]
    owner_outs = [segment] * column if ring else [column * segment]

    def near(bufs):
        if not ring:
            return [within(bufs[0])]
        return [bufs[0]] + [
            lax.ppermute(bufs[s], "dp", [(d, d ^ s) for d in range(devices)])
            for s in range(1, column)
        ]

    def at_owner(bufs):
        width = bufs[0].shape[1]
        if ring:
            return [x.reshape(local, segment, width) for x in bufs]
        x = bufs[0].reshape(column, local, segment, width).transpose(1, 0, 2, 3)
        return [x.reshape(local, column * segment, width)]

    def from_owner(bufs):
        width = bufs[0].shape[2]
        if ring:
            return [x.reshape(local * segment, width) for x in bufs]
        x = bufs[0].reshape(local, column, segment, width).transpose(1, 0, 2, 3)
        return [x.reshape(column * local * segment, width)]

    def planes_swap(x):
        return lax.all_to_all(
            x, "dp", split_axis=0, concat_axis=0, tiled=True, axis_index_groups=stripes
        )

    def gather_all(x, axis, groups=None):
        return lax.all_gather(x, axis, axis=0, tiled=True, axis_index_groups=groups)

    def outward(size, side):
        lanes = jnp.arange(PLANES * size, dtype=jnp.int32)
        code = side * size + own_order
        return (lanes[:, None] == code[None, :]).astype(BF), (
            code[:, None] == lanes[None, :]
        ).astype(BF)

    def inward(size, turned=False):
        kth = jnp.arange(size, dtype=jnp.int32)
        target = jnp.sum(
            jnp.where(
                (order[:, None, :] == kth[None, :, None]) & (spot[:, None, :] >= 0),
                spot[:, None, :] + 1,
                0,
            ),
            axis=2,
        )
        if turned:
            there = (planes ^ plane)[:, None, None] == planes[None, :, None]
            target = jnp.sum(jnp.where(there, target[None], 0), axis=1)
        target = target.reshape(PLANES * size) - 1
        spots = jnp.arange(PLANES * most, dtype=jnp.int32)
        return (spots[:, None] == target[None, :]).astype(BF), (
            target[:, None] == spots[None, :]
        ).astype(BF)

    rows_out = outward(most, own_goal ^ plane)[0]
    scaled_z = across(route(first, rows_out, [scaled], [most] * PLANES))
    if ring:
        first.last += scaled_z[1:2]
        lanes = jnp.arange(tok_rows, dtype=jnp.int32)
        same_rows = (lanes[:, None] == lanes[None, :]).astype(BF)
        mates = near(route(first, same_rows, [scaled], [tok_rows]) * column)
        first.last += [weight_z]
    scaled_sent = route(first, inward(most, True)[0], scaled_z, blocks_out)

    def run(size):
        line = Line()
        total = PLANES * size
        out_rows, back_rows = outward(size, own_goal)
        spread, gather = inward(size)
        if ring:
            weight = gather_all(weight_z, "groups").reshape(parts, PLANES, share, deep)
        else:
            weight = gather_all(frozen_key_weight, "dp")
        acts_z = planes_swap(route(line, out_rows, [acts], [total])[0])
        got_scaled = at_owner(near(scaled_sent))
        back_low = back_project(line, adapter_up_slots, got_scaled)
        terms = adapter_terms(line, back_low, adapter_down_slots, owner_outs)
        terms = near(from_owner(terms))
        if ring:
            bases = near(base_step(line, weight, mates))
        else:
            bases = [dot(weight, scaled, 1, 1).astype(BF)]
        came = planes_swap(route(line, gather, terms, [total])[0])
        got = route(line, spread, [acts_z], blocks_out)
        got = at_owner(near(got))
        low, grad_a = owner_step(line, back_low, adapter_down_slots, got)
        grad_b = up_gradient(line, low, got_scaled)
        result = final_step(line, back_rows, came, bases)
        return result, grad_a, grad_b

    steps = [most * 11 // 16, most * 13 // 16, most]
    which = sum((need_all > s).astype(jnp.int32) for s in steps[:-1])
    return lax.switch(which, [functools.partial(run, s) for s in steps])


def solution(mesh):
    return jax.shard_map(
        shards,
        mesh=mesh,
        in_specs=(
            P(("groups", "dp"), None),
            P(("groups", "dp"), None),
            P("dp", None),
            P(("groups", "dp"), None, None),
            P(("groups", "dp"), None, None),
            P(("groups", "dp"), None),
            P("groups"),
            P("groups"),
        ),
        out_specs=(
            P(("groups", "dp"), None),
            P(("groups", "dp"), None, None),
            P(("groups", "dp"), None, None),
        ),
        check_vma=False,
    )
```

```python
import functools

import jax
import jax.numpy as jnp
from jax import lax
from jax.experimental import pallas as pl
from jax.experimental.pallas import tpu as pltpu
from jax.sharding import PartitionSpec as P

DELTA_MULTIPLIER = 0.25
BF = jnp.bfloat16
F32 = jnp.float32
PLANES = 4
PIECES = 4
PARAMS = pltpu.CompilerParams(vmem_limit_bytes=48 * 1024 * 1024)


def far(shape, dtype=BF):
    return pltpu.HBM(shape, dtype)


def whole(shape):
    zeros = (0,) * len(shape)
    return pl.BlockSpec(shape, lambda i: zeros)


def dot(a, b, ca=1, cb=0):
    return lax.dot_general(a, b, (((ca,), (cb,)), ((), ())), preferred_element_type=F32)


HERE = pl.BlockSpec(memory_space=pl.ANY)


def note_body(ref, out):
    out[...] = ref[...]


def note_step(line, note):
    return line.call(
        note_body,
        [note],
        [whole(note.shape)],
        whole(note.shape),
        jax.ShapeDtypeStruct(note.shape, note.dtype),
    )


def route_body(count, rows_ref, *refs):
    ins, outs = refs[:count], refs[count:]
    held = ins[0][...] if count == 1 else jnp.concatenate([r[...] for r in ins], axis=0)
    moved = dot(rows_ref[...], held).astype(BF)
    at = 0
    for out in outs:
        out[...] = moved[at : at + out.shape[0]]
        at += out.shape[0]


class Line:
    def __init__(self):
        self.last = []

    def call(self, body, operands, in_specs, out_specs, out_shape, pieces=1, scratch=()):
        after = self.last
        first = len(operands)
        many = isinstance(out_shape, list)

        def kernel(*refs):
            mark = len(refs) - 1 - len(scratch)
            refs[mark][...] = jnp.zeros_like(refs[mark])
            body(*refs[:first], *refs[first + len(after) : mark], *refs[mark + 1 :])

        out = pl.pallas_call(
            kernel,
            grid=(pieces,),
            in_specs=in_specs + [HERE] * len(after),
            out_specs=(out_specs if many else [out_specs]) + [whole((8, 128))],
            out_shape=(out_shape if many else [out_shape])
            + [jax.ShapeDtypeStruct((8, 128), jnp.int32)],
            scratch_shapes=scratch,
            compiler_params=PARAMS,
        )(*operands, *after)
        self.last = [out[-1]]
        return out[:-1] if many else out[0]


def route_body(count, rows_ref, *refs):
    ins, outs = refs[:count], refs[count:]
    held = ins[0][...] if count == 1 else jnp.concatenate([r[...] for r in ins], axis=0)
    moved = dot(rows_ref[...], held).astype(BF)
    at = 0
    for out in outs:
        out[...] = moved[at : at + out.shape[0]]
        at += out.shape[0]


class Line:
    def __init__(self):
        self.last = []

    def call(self, body, operands, in_specs, out_specs, out_shape, pieces=1, scratch=()):
        after = self.last
        first = len(operands)
        many = isinstance(out_shape, list)

        def kernel(*refs):
            mark = len(refs) - 1 - len(scratch)
            refs[mark][...] = jnp.zeros_like(refs[mark])
            body(*refs[:first], *refs[first + len(after) : mark], *refs[mark + 1 :])

        out = pl.pallas_call(
            kernel,
            grid=(pieces,),
            in_specs=in_specs + [HERE] * len(after),
            out_specs=(out_specs if many else [out_specs]) + [whole((8, 128))],
            out_shape=(out_shape if many else [out_shape])
            + [jax.ShapeDtypeStruct((8, 128), jnp.int32)],
            scratch_shapes=scratch,
            compiler_params=PARAMS,
        )(*operands, *after)
        self.last = [out[-1]]
        return out[:-1] if many else out[0]


def hold_body(ref, out):
    pass


def hold(line, x):
    last = line.last
    out = line.call(hold_body, [x], [FAR], FAR, far(x.shape, x.dtype), 1, {0: 0})
    line.last = last
    return out


def route(line, rows, ins, outs):
    width = ins[0].shape[1]
    pieces = PIECES if width % (128 * PIECES) == 0 else 1
    step = width // pieces
    return line.call(
        functools.partial(route_body, len(ins)),
        [rows, *ins],
        [whole(rows.shape)]
        + [pl.BlockSpec((x.shape[0], step), lambda i: (0, i)) for x in ins],
        [pl.BlockSpec((n, step), lambda i: (0, i)) for n in outs],
        [far((n, width)) for n in outs],
        pieces,
    )


def job_rows(refs, job):
    return jnp.concatenate([ref[job] for ref in refs], axis=0)


def back_body(count, up_ref, *refs):
    out = refs[count]
    for job in range(up_ref.shape[0]):
        held = job_rows(refs[:count], job)
        out[job] = (DELTA_MULTIPLIER * dot(held, up_ref[job], 1, 1)).astype(BF)


def back_project(line, up, rows):
    local, rank = up.shape[0], up.shape[1]
    shape = (local, sum(x.shape[1] for x in rows), rank)
    return line.call(
        functools.partial(back_body, len(rows)),
        [up, *rows],
        [whole(up.shape)] + [whole(x.shape) for x in rows],
        whole(shape),
        jax.ShapeDtypeStruct(shape, BF),
    )


def term_body(back_ref, down_ref, *outs):
    for job in range(down_ref.shape[0]):
        term = dot(back_ref[job], down_ref[job], 1, 1).astype(BF)
        at = 0
        for out in outs:
            out[job] = term[at : at + out.shape[1]]
            at += out.shape[1]


def adapter_terms(line, back_low, down, outs):
    local, width, rank = down.shape
    step = width // PIECES
    return line.call(
        term_body,
        [back_low, down],
        [whole(back_low.shape), pl.BlockSpec((local, step, rank), lambda i: (0, i, 0))],
        [pl.BlockSpec((local, n, step), lambda i: (0, 0, i)) for n in outs],
        [far((local, n, width)) for n in outs],
        PIECES,
    )


def owner_body(count, back_ref, down_ref, *refs):
    ins, (low_ref, grad_ref) = refs[:count], refs[count:]

    @pl.when(pl.program_id(0) == 0)
    def _():
        low_ref[...] = jnp.zeros_like(low_ref)

    for job in range(down_ref.shape[0]):
        held = job_rows(ins, job)
        low_ref[job] += dot(held, down_ref[job])
        grad_ref[job] = dot(held, back_ref[job], 0, 0).astype(BF)


def owner_step(line, back_low, down, rows):
    local, width, rank = down.shape
    step = width // PIECES
    part = pl.BlockSpec((local, step, rank), lambda i: (0, i, 0))
    low_shape = (local, back_low.shape[1], rank)
    return line.call(
        functools.partial(owner_body, len(rows)),
        [back_low, down, *rows],
        [whole(back_low.shape), part]
        + [pl.BlockSpec((local, x.shape[1], step), lambda i: (0, 0, i)) for x in rows],
        [whole(low_shape), part],
        [jax.ShapeDtypeStruct(low_shape, F32), jax.ShapeDtypeStruct(down.shape, BF)],
        PIECES,
    )


def up_body(count, low_ref, *refs):
    out = refs[count]
    for job in range(low_ref.shape[0]):
        low = low_ref[job].astype(BF)
        held = job_rows(refs[:count], job)
        out[job] = (DELTA_MULTIPLIER * dot(low, held, 0, 0)).astype(BF)


def up_gradient(line, low, rows):
    shape = (low.shape[0], low.shape[2], rows[0].shape[2])
    return line.call(
        functools.partial(up_body, len(rows)),
        [low, *rows],
        [whole(low.shape)] + [whole(x.shape) for x in rows],
        whole(shape),
        jax.ShapeDtypeStruct(shape, BF),
    )


def base_body(count, weight_ref, *refs):
    ins, outs = refs[:count], refs[count:]
    weight = jnp.concatenate([weight_ref[at, 0] for at in range(weight_ref.shape[0])], axis=0)
    for x, out in zip(ins, outs):
        out[...] = dot(weight, x[...], 1, 1).astype(BF)


def base_step(line, weight, rows):
    parts, planes, share, deep = weight.shape
    step, tokens = parts * share, rows[0].shape[0]
    return line.call(
        functools.partial(base_body, len(rows)),
        [weight, *rows],
        [pl.BlockSpec((parts, 1, share, deep), lambda i: (0, i, 0, 0))]
        + [whole(x.shape) for x in rows],
        [pl.BlockSpec((step, tokens), lambda i: (i, 0)) for _ in rows],
        [far((planes * step, tokens)) for _ in rows],
        planes,
    )


def final_body(count, rows_ref, came_ref, *refs):
    bases, out, held = refs[:count], refs[count], refs[count + 1]
    size = bases[0].shape[0]
    place = lax.rem(lax.axis_index("dp"), count)
    for s, ref in enumerate(bases):
        held[pl.ds(pl.multiple_of((place ^ s) * size, 16), size)] = ref[...]
    tokens = held.shape[1]
    one = (
        lax.broadcasted_iota(jnp.int32, (tokens, tokens), 0)
        == lax.broadcasted_iota(jnp.int32, (tokens, tokens), 1)
    ).astype(F32)
    base = dot(one.astype(BF), held[...], 1, 1)
    out[...] = (base + dot(rows_ref[...], came_ref[...])).astype(BF)


def final_step(line, rows, came, bases):
    tokens = rows.shape[0]
    step = came.shape[1] // PLANES
    size = step // len(bases)
    return line.call(
        functools.partial(final_body, len(bases)),
        [rows, came, *bases],
        [whole(rows.shape), pl.BlockSpec((came.shape[0], step), lambda i: (0, i))]
        + [pl.BlockSpec((size, tokens), lambda i: (i, 0)) for _ in bases],
        pl.BlockSpec((tokens, step), lambda i: (0, i)),
        jax.ShapeDtypeStruct((tokens, step * PLANES), BF),
        PLANES,
        [pltpu.VMEM((step, tokens), BF)],
    )


def shards(
    acts,
    cotan,
    frozen_key_weight,
    adapter_down_slots,
    adapter_up_slots,
    token_row_jobs,
    slot_owner_jobs,
    loss_token_count,
):
    devices = lax.axis_size("dp")
    parts = lax.axis_size("groups")
    tok_rows = acts.shape[0]
    local = adapter_down_slots.shape[0]
    jobs_all = slot_owner_jobs.shape[0]
    depth = 2 * tok_rows // (local * devices)
    column = devices // PLANES
    ring = column <= 4
    most = local * column * depth
    segment = PLANES * depth
    me = lax.axis_index("dp")
    plane, place = me // column, me % column

    first = Line()
    stripes = [[p * column + c for p in range(PLANES)] for c in range(column)]
    ids = token_row_jobs[:, 0]
    lengths = loss_token_count.astype(F32)
    weights = jnp.mean(lengths) / lengths
    numbers = jnp.arange(jobs_all, dtype=jnp.int32)
    row_weight = jnp.sum(jnp.where(ids[:, None] == numbers[None, :], weights[None, :], 0.0), axis=1)
    row_slot = jnp.sum(
        jnp.where(ids[:, None] == slot_owner_jobs[None, :], numbers[None, :], 0), axis=1
    )
    scaled = (row_weight[:, None] * cotan.astype(F32)).astype(BF)

    planes = jnp.arange(PLANES, dtype=jnp.int32)
    need = jnp.max(
        jnp.sum((row_slot[:, None] // (local * column) == planes[None, :]).astype(jnp.int32), axis=0)
    )
    note = jnp.concatenate([row_slot, jnp.full((128,), need, jnp.int32)])
    share = frozen_key_weight.shape[0] // parts
    deep = frozen_key_weight.shape[1]
    own_share = lax.dynamic_slice_in_dim(
        frozen_key_weight, lax.axis_index("groups") * share, share, 0
    )
    if ring:
        weight_z = lax.all_gather(
            own_share, "dp", axis=0, tiled=True, axis_index_groups=stripes
        )
        first.last = [own_share]
        note = note_step(first, note[None])[0]
    note = jnp.broadcast_to(note[None, None], (parts * devices, 1, tok_rows + 128))
    first.last = [note]
    notes = lax.all_to_all(
        note,
        ("groups", "dp"),
        split_axis=0,
        concat_axis=0,
        tiled=True,
    )[:, 0]
    need_all = jnp.max(notes[:, tok_rows])
    mine = notes[:, :tok_rows].reshape(parts, PLANES, column, tok_rows)
    mine = lax.dynamic_index_in_dim(mine, lax.axis_index("groups"), 0, keepdims=False)
    mine = lax.dynamic_index_in_dim(mine, place, 1, keepdims=False)
    slots = mine
    goal = slots // (local * column)
    earlier = jnp.arange(tok_rows)[None, :] < jnp.arange(tok_rows)[:, None]
    order = jnp.sum(
        ((goal[:, :, None] == goal[:, None, :]) & earlier[None]).astype(jnp.int32), axis=2
    )
    rank = jnp.sum(
        ((slots[:, :, None] == slots[:, None, :]) & earlier[None]).astype(jnp.int32), axis=2
    )
    owner = (slots // local) % column
    if ring:
        owner = owner ^ place
    spot = (
        owner * (local * segment)
        + (slots % local) * segment
        + planes[:, None] * depth
        + rank
    )
    spot = jnp.where(goal == plane, spot, -1)
    own_goal = row_slot // (local * column)
    own_order = jnp.sum(
        ((own_goal[:, None] == own_goal[None, :]) & earlier).astype(jnp.int32), axis=1
    )

    def across(bufs):
        return [bufs[0]] + [
            lax.ppermute(
                bufs[s],
                "dp",
                [(d, ((d // column) ^ s) * column + d % column) for d in range(devices)],
            )
            for s in range(1, PLANES)
        ]

    blocks = [[p * column + c for c in range(column)] for p in range(PLANES)]

    def within(x):
        return lax.all_to_all(
            x, "dp", split_axis=0, concat_axis=0, tiled=True, axis_index_groups=blocks
        )

    blocks_out = [local * segment] * column if ring else [column * local * segment]
    owner_outs = [segment] * column if ring else [column * segment]

    def near(bufs):
        if not ring:
            return [within(bufs[0])]
        return [bufs[0]] + [
            lax.ppermute(bufs[s], "dp", [(d, d ^ s) for d in range(devices)])
            for s in range(1, column)
        ]

    def at_owner(bufs):
        width = bufs[0].shape[1]
        if ring:
            return [x.reshape(local, segment, width) for x in bufs]
        x = bufs[0].reshape(column, local, segment, width).transpose(1, 0, 2, 3)
        return [x.reshape(local, column * segment, width)]

    def from_owner(bufs):
        width = bufs[0].shape[2]
        if ring:
            return [x.reshape(local * segment, width) for x in bufs]
        x = bufs[0].reshape(local, column, segment, width).transpose(1, 0, 2, 3)
        return [x.reshape(column * local * segment, width)]

    def planes_swap(x):
        return lax.all_to_all(
            x, "dp", split_axis=0, concat_axis=0, tiled=True, axis_index_groups=stripes
        )

    def gather_all(x, axis, groups=None):
        return lax.all_gather(x, axis, axis=0, tiled=True, axis_index_groups=groups)

    def outward(size, side):
        lanes = jnp.arange(PLANES * size, dtype=jnp.int32)
        code = side * size + own_order
        return (lanes[:, None] == code[None, :]).astype(BF), (
            code[:, None] == lanes[None, :]
        ).astype(BF)

    def inward(size, turned=False):
        kth = jnp.arange(size, dtype=jnp.int32)
        target = jnp.sum(
            jnp.where(
                (order[:, None, :] == kth[None, :, None]) & (spot[:, None, :] >= 0),
                spot[:, None, :] + 1,
                0,
            ),
            axis=2,
        )
        if turned:
            there = (planes ^ plane)[:, None, None] == planes[None, :, None]
            target = jnp.sum(jnp.where(there, target[None], 0), axis=1)
        target = target.reshape(PLANES * size) - 1
        spots = jnp.arange(PLANES * most, dtype=jnp.int32)
        return (spots[:, None] == target[None, :]).astype(BF), (
            target[:, None] == spots[None, :]
        ).astype(BF)

    rows_out = outward(most, own_goal ^ plane)[0]
    scaled_z = across(route(first, rows_out, [scaled], [most] * PLANES))
    if ring:
        lanes = jnp.arange(tok_rows, dtype=jnp.int32)
        same_rows = (lanes[:, None] == lanes[None, :]).astype(BF)
        early = route(first, same_rows, [scaled], [tok_rows])
        first.last += scaled_z[1:2]
        late = route(first, same_rows, [scaled], [tok_rows])
        mates = near(list(early) * (column - 1) + list(late))
    scaled_sent = route(first, inward(most, True)[0], scaled_z, blocks_out)

    def run(size):
        line = Line()
        total = PLANES * size
        out_rows, back_rows = outward(size, own_goal)
        spread, gather = inward(size)
        if ring:
            weight = gather_all(weight_z, "groups").reshape(parts, PLANES, share, deep)
        else:
            weight = gather_all(frozen_key_weight, "dp")
        acts_z = planes_swap(route(line, out_rows, [acts], [total])[0])
        got_scaled = at_owner(near(scaled_sent))
        back_low = back_project(line, adapter_up_slots, got_scaled)
        terms = adapter_terms(line, back_low, adapter_down_slots, owner_outs)
        terms = near(from_owner(terms))
        if ring:
            bases = near(base_step(line, weight, mates))
        else:
            bases = [dot(weight, scaled, 1, 1).astype(BF)]
        came = planes_swap(route(line, gather, terms, [total])[0])
        got = route(line, spread, [acts_z], blocks_out)
        got = at_owner(near(got))
        low, grad_a = owner_step(line, back_low, adapter_down_slots, got)
        grad_b = up_gradient(line, low, got_scaled)
        result = final_step(line, back_rows, came, bases)
        return result, grad_a, grad_b

    steps = [most * 11 // 16, most * 13 // 16, most]
    which = sum((need_all > s).astype(jnp.int32) for s in steps[:-1])
    return lax.switch(which, [functools.partial(run, s) for s in steps])


def solution(mesh):
    return jax.shard_map(
        shards,
        mesh=mesh,
        in_specs=(
            P(("groups", "dp"), None),
            P(("groups", "dp"), None),
            P("dp", None),
            P(("groups", "dp"), None, None),
            P(("groups", "dp"), None, None),
            P(("groups", "dp"), None),
            P("groups"),
            P("groups"),
        ),
        out_specs=(
            P(("groups", "dp"), None),
            P(("groups", "dp"), None, None),
            P(("groups", "dp"), None, None),
        ),
        check_vma=False,
    )
```

```python
import functools

import jax
import jax.numpy as jnp
from jax import lax
from jax.experimental import pallas as pl
from jax.experimental.pallas import tpu as pltpu
from jax.sharding import PartitionSpec as P

DELTA_MULTIPLIER = 0.25
BF = jnp.bfloat16
F32 = jnp.float32
PLANES = 4
PIECES = 4
PARAMS = pltpu.CompilerParams(vmem_limit_bytes=48 * 1024 * 1024)


def far(shape, dtype=BF):
    return pltpu.HBM(shape, dtype)


def whole(shape):
    zeros = (0,) * len(shape)
    return pl.BlockSpec(shape, lambda i: zeros)


def dot(a, b, ca=1, cb=0):
    return lax.dot_general(a, b, (((ca,), (cb,)), ((), ())), preferred_element_type=F32)


HERE = pl.BlockSpec(memory_space=pl.ANY)


def note_body(ref, out):
    out[...] = ref[...]


def note_step(line, note):
    return line.call(
        note_body,
        [note],
        [whole(note.shape)],
        whole(note.shape),
        jax.ShapeDtypeStruct(note.shape, note.dtype),
    )


def route_body(count, rows_ref, *refs):
    ins, outs = refs[:count], refs[count:]
    held = ins[0][...] if count == 1 else jnp.concatenate([r[...] for r in ins], axis=0)
    moved = dot(rows_ref[...], held).astype(BF)
    at = 0
    for out in outs:
        out[...] = moved[at : at + out.shape[0]]
        at += out.shape[0]


class Line:
    def __init__(self):
        self.last = []

    def call(self, body, operands, in_specs, out_specs, out_shape, pieces=1, scratch=()):
        after = self.last
        first = len(operands)
        many = isinstance(out_shape, list)

        def kernel(*refs):
            mark = len(refs) - 1 - len(scratch)
            refs[mark][...] = jnp.zeros_like(refs[mark])
            body(*refs[:first], *refs[first + len(after) : mark], *refs[mark + 1 :])

        out = pl.pallas_call(
            kernel,
            grid=(pieces,),
            in_specs=in_specs + [HERE] * len(after),
            out_specs=(out_specs if many else [out_specs]) + [whole((8, 128))],
            out_shape=(out_shape if many else [out_shape])
            + [jax.ShapeDtypeStruct((8, 128), jnp.int32)],
            scratch_shapes=scratch,
            compiler_params=PARAMS,
        )(*operands, *after)
        self.last = [out[-1]]
        return out[:-1] if many else out[0]


def route_body(count, rows_ref, *refs):
    ins, outs = refs[:count], refs[count:]
    held = ins[0][...] if count == 1 else jnp.concatenate([r[...] for r in ins], axis=0)
    moved = dot(rows_ref[...], held).astype(BF)
    at = 0
    for out in outs:
        out[...] = moved[at : at + out.shape[0]]
        at += out.shape[0]


class Line:
    def __init__(self):
        self.last = []

    def call(self, body, operands, in_specs, out_specs, out_shape, pieces=1, scratch=()):
        after = self.last
        first = len(operands)
        many = isinstance(out_shape, list)

        def kernel(*refs):
            mark = len(refs) - 1 - len(scratch)
            refs[mark][...] = jnp.zeros_like(refs[mark])
            body(*refs[:first], *refs[first + len(after) : mark], *refs[mark + 1 :])

        out = pl.pallas_call(
            kernel,
            grid=(pieces,),
            in_specs=in_specs + [HERE] * len(after),
            out_specs=(out_specs if many else [out_specs]) + [whole((8, 128))],
            out_shape=(out_shape if many else [out_shape])
            + [jax.ShapeDtypeStruct((8, 128), jnp.int32)],
            scratch_shapes=scratch,
            compiler_params=PARAMS,
        )(*operands, *after)
        self.last = [out[-1]]
        return out[:-1] if many else out[0]


def hold_body(ref, out):
    pass


def hold(line, x):
    last = line.last
    out = line.call(hold_body, [x], [FAR], FAR, far(x.shape, x.dtype), 1, {0: 0})
    line.last = last
    return out


def route(line, rows, ins, outs):
    width = ins[0].shape[1]
    pieces = PIECES if width % (128 * PIECES) == 0 else 1
    step = width // pieces
    return line.call(
        functools.partial(route_body, len(ins)),
        [rows, *ins],
        [whole(rows.shape)]
        + [pl.BlockSpec((x.shape[0], step), lambda i: (0, i)) for x in ins],
        [pl.BlockSpec((n, step), lambda i: (0, i)) for n in outs],
        [far((n, width)) for n in outs],
        pieces,
    )


def job_rows(refs, job):
    return jnp.concatenate([ref[job] for ref in refs], axis=0)


def back_body(count, up_ref, *refs):
    out = refs[count]
    for job in range(up_ref.shape[0]):
        held = job_rows(refs[:count], job)
        out[job] = (DELTA_MULTIPLIER * dot(held, up_ref[job], 1, 1)).astype(BF)


def back_project(line, up, rows):
    local, rank = up.shape[0], up.shape[1]
    shape = (local, sum(x.shape[1] for x in rows), rank)
    return line.call(
        functools.partial(back_body, len(rows)),
        [up, *rows],
        [whole(up.shape)] + [whole(x.shape) for x in rows],
        whole(shape),
        jax.ShapeDtypeStruct(shape, BF),
    )


def term_body(back_ref, down_ref, *outs):
    for job in range(down_ref.shape[0]):
        term = dot(back_ref[job], down_ref[job], 1, 1).astype(BF)
        at = 0
        for out in outs:
            out[job] = term[at : at + out.shape[1]]
            at += out.shape[1]


def adapter_terms(line, back_low, down, outs):
    local, width, rank = down.shape
    step = width // PIECES
    return line.call(
        term_body,
        [back_low, down],
        [whole(back_low.shape), pl.BlockSpec((local, step, rank), lambda i: (0, i, 0))],
        [pl.BlockSpec((local, n, step), lambda i: (0, 0, i)) for n in outs],
        [far((local, n, width)) for n in outs],
        PIECES,
    )


def owner_body(count, back_ref, down_ref, *refs):
    ins, (low_ref, grad_ref) = refs[:count], refs[count:]

    @pl.when(pl.program_id(0) == 0)
    def _():
        low_ref[...] = jnp.zeros_like(low_ref)

    for job in range(down_ref.shape[0]):
        held = job_rows(ins, job)
        low_ref[job] += dot(held, down_ref[job])
        grad_ref[job] = dot(held, back_ref[job], 0, 0).astype(BF)


def owner_step(line, back_low, down, rows):
    local, width, rank = down.shape
    step = width // PIECES
    part = pl.BlockSpec((local, step, rank), lambda i: (0, i, 0))
    low_shape = (local, back_low.shape[1], rank)
    return line.call(
        functools.partial(owner_body, len(rows)),
        [back_low, down, *rows],
        [whole(back_low.shape), part]
        + [pl.BlockSpec((local, x.shape[1], step), lambda i: (0, 0, i)) for x in rows],
        [whole(low_shape), part],
        [jax.ShapeDtypeStruct(low_shape, F32), jax.ShapeDtypeStruct(down.shape, BF)],
        PIECES,
    )


def up_body(count, low_ref, *refs):
    out = refs[count]
    for job in range(low_ref.shape[0]):
        low = low_ref[job].astype(BF)
        held = job_rows(refs[:count], job)
        out[job] = (DELTA_MULTIPLIER * dot(low, held, 0, 0)).astype(BF)


def up_gradient(line, low, rows):
    shape = (low.shape[0], low.shape[2], rows[0].shape[2])
    return line.call(
        functools.partial(up_body, len(rows)),
        [low, *rows],
        [whole(low.shape)] + [whole(x.shape) for x in rows],
        whole(shape),
        jax.ShapeDtypeStruct(shape, BF),
    )


def base_body(count, weight_ref, *refs):
    ins, outs = refs[:count], refs[count:]
    weight = jnp.concatenate([weight_ref[at, 0] for at in range(weight_ref.shape[0])], axis=0)
    for x, out in zip(ins, outs):
        out[...] = dot(weight, x[...], 1, 1).astype(BF)


def base_step(line, weight, rows):
    parts, planes, share, deep = weight.shape
    step, tokens = parts * share, rows[0].shape[0]
    return line.call(
        functools.partial(base_body, len(rows)),
        [weight, *rows],
        [pl.BlockSpec((parts, 1, share, deep), lambda i: (0, i, 0, 0))]
        + [whole(x.shape) for x in rows],
        [pl.BlockSpec((step, tokens), lambda i: (i, 0)) for _ in rows],
        [far((planes * step, tokens)) for _ in rows],
        planes,
    )


def final_body(count, rows_ref, came_ref, *refs):
    bases, out, held = refs[:count], refs[count], refs[count + 1]
    size = bases[0].shape[0]
    place = lax.rem(lax.axis_index("dp"), count)
    for s, ref in enumerate(bases):
        held[pl.ds(pl.multiple_of((place ^ s) * size, 16), size)] = ref[...]
    tokens = held.shape[1]
    one = (
        lax.broadcasted_iota(jnp.int32, (tokens, tokens), 0)
        == lax.broadcasted_iota(jnp.int32, (tokens, tokens), 1)
    ).astype(F32)
    base = dot(one.astype(BF), held[...], 1, 1)
    out[...] = (base + dot(rows_ref[...], came_ref[...])).astype(BF)


def final_step(line, rows, came, bases):
    tokens = rows.shape[0]
    step = came.shape[1] // PLANES
    size = step // len(bases)
    return line.call(
        functools.partial(final_body, len(bases)),
        [rows, came, *bases],
        [whole(rows.shape), pl.BlockSpec((came.shape[0], step), lambda i: (0, i))]
        + [pl.BlockSpec((size, tokens), lambda i: (i, 0)) for _ in bases],
        pl.BlockSpec((tokens, step), lambda i: (0, i)),
        jax.ShapeDtypeStruct((tokens, step * PLANES), BF),
        PLANES,
        [pltpu.VMEM((step, tokens), BF)],
    )


def shards(
    acts,
    cotan,
    frozen_key_weight,
    adapter_down_slots,
    adapter_up_slots,
    token_row_jobs,
    slot_owner_jobs,
    loss_token_count,
):
    devices = lax.axis_size("dp")
    parts = lax.axis_size("groups")
    tok_rows = acts.shape[0]
    local = adapter_down_slots.shape[0]
    jobs_all = slot_owner_jobs.shape[0]
    depth = 2 * tok_rows // (local * devices)
    column = devices // PLANES
    ring = column <= 4
    most = local * column * depth
    segment = PLANES * depth
    me = lax.axis_index("dp")
    plane, place = me // column, me % column

    first = Line()
    stripes = [[p * column + c for p in range(PLANES)] for c in range(column)]
    ids = token_row_jobs[:, 0]
    lengths = loss_token_count.astype(F32)
    weights = jnp.mean(lengths) / lengths
    numbers = jnp.arange(jobs_all, dtype=jnp.int32)
    row_weight = jnp.sum(jnp.where(ids[:, None] == numbers[None, :], weights[None, :], 0.0), axis=1)
    row_slot = jnp.sum(
        jnp.where(ids[:, None] == slot_owner_jobs[None, :], numbers[None, :], 0), axis=1
    )
    scaled = (row_weight[:, None] * cotan.astype(F32)).astype(BF)

    planes = jnp.arange(PLANES, dtype=jnp.int32)
    need = jnp.max(
        jnp.sum((row_slot[:, None] // (local * column) == planes[None, :]).astype(jnp.int32), axis=0)
    )
    note = jnp.concatenate([row_slot, jnp.full((128,), need, jnp.int32)])
    share = frozen_key_weight.shape[0] // parts
    deep = frozen_key_weight.shape[1]
    own_share = lax.dynamic_slice_in_dim(
        frozen_key_weight, lax.axis_index("groups") * share, share, 0
    )
    if ring:
        weight_z = lax.all_gather(
            own_share, "dp", axis=0, tiled=True, axis_index_groups=stripes
        )
        first.last = [own_share]
        note = note_step(first, note[None])[0]
    note = jnp.broadcast_to(note[None, None], (parts * devices, 1, tok_rows + 128))
    first.last = [note]
    notes = lax.all_to_all(
        note,
        ("groups", "dp"),
        split_axis=0,
        concat_axis=0,
        tiled=True,
    )[:, 0]
    need_all = jnp.max(notes[:, tok_rows])
    mine = notes[:, :tok_rows].reshape(parts, PLANES, column, tok_rows)
    mine = lax.dynamic_index_in_dim(mine, lax.axis_index("groups"), 0, keepdims=False)
    mine = lax.dynamic_index_in_dim(mine, place, 1, keepdims=False)
    slots = mine
    goal = slots // (local * column)
    earlier = jnp.arange(tok_rows)[None, :] < jnp.arange(tok_rows)[:, None]
    order = jnp.sum(
        ((goal[:, :, None] == goal[:, None, :]) & earlier[None]).astype(jnp.int32), axis=2
    )
    rank = jnp.sum(
        ((slots[:, :, None] == slots[:, None, :]) & earlier[None]).astype(jnp.int32), axis=2
    )
    owner = (slots // local) % column
    if ring:
        owner = owner ^ place
    spot = (
        owner * (local * segment)
        + (slots % local) * segment
        + planes[:, None] * depth
        + rank
    )
    spot = jnp.where(goal == plane, spot, -1)
    own_goal = row_slot // (local * column)
    own_order = jnp.sum(
        ((own_goal[:, None] == own_goal[None, :]) & earlier).astype(jnp.int32), axis=1
    )

    def across(bufs):
        return [bufs[0]] + [
            lax.ppermute(
                bufs[s],
                "dp",
                [(d, ((d // column) ^ s) * column + d % column) for d in range(devices)],
            )
            for s in range(1, PLANES)
        ]

    blocks = [[p * column + c for c in range(column)] for p in range(PLANES)]

    def within(x):
        return lax.all_to_all(
            x, "dp", split_axis=0, concat_axis=0, tiled=True, axis_index_groups=blocks
        )

    blocks_out = [local * segment] * column if ring else [column * local * segment]
    owner_outs = [segment] * column if ring else [column * segment]

    def near(bufs):
        if not ring:
            return [within(bufs[0])]
        return [bufs[0]] + [
            lax.ppermute(bufs[s], "dp", [(d, d ^ s) for d in range(devices)])
            for s in range(1, column)
        ]

    def at_owner(bufs):
        width = bufs[0].shape[1]
        if ring:
            return [x.reshape(local, segment, width) for x in bufs]
        x = bufs[0].reshape(column, local, segment, width).transpose(1, 0, 2, 3)
        return [x.reshape(local, column * segment, width)]

    def from_owner(bufs):
        width = bufs[0].shape[2]
        if ring:
            return [x.reshape(local * segment, width) for x in bufs]
        x = bufs[0].reshape(local, column, segment, width).transpose(1, 0, 2, 3)
        return [x.reshape(column * local * segment, width)]

    def planes_swap(x):
        return lax.all_to_all(
            x, "dp", split_axis=0, concat_axis=0, tiled=True, axis_index_groups=stripes
        )

    def gather_all(x, axis, groups=None):
        return lax.all_gather(x, axis, axis=0, tiled=True, axis_index_groups=groups)

    def outward(size, side):
        lanes = jnp.arange(PLANES * size, dtype=jnp.int32)
        code = side * size + own_order
        return (lanes[:, None] == code[None, :]).astype(BF), (
            code[:, None] == lanes[None, :]
        ).astype(BF)

    def inward(size, turned=False):
        kth = jnp.arange(size, dtype=jnp.int32)
        target = jnp.sum(
            jnp.where(
                (order[:, None, :] == kth[None, :, None]) & (spot[:, None, :] >= 0),
                spot[:, None, :] + 1,
                0,
            ),
            axis=2,
        )
        if turned:
            there = (planes ^ plane)[:, None, None] == planes[None, :, None]
            target = jnp.sum(jnp.where(there, target[None], 0), axis=1)
        target = target.reshape(PLANES * size) - 1
        spots = jnp.arange(PLANES * most, dtype=jnp.int32)
        return (spots[:, None] == target[None, :]).astype(BF), (
            target[:, None] == spots[None, :]
        ).astype(BF)

    rows_out = outward(most, own_goal ^ plane)[0]
    scaled_z = across(route(first, rows_out, [scaled], [most] * PLANES))
    if ring:
        lanes = jnp.arange(tok_rows, dtype=jnp.int32)
        same_rows = (lanes[:, None] == lanes[None, :]).astype(BF)
        early = route(first, same_rows, [scaled], [tok_rows])
        first.last += scaled_z[1:2]
        late = route(first, same_rows, [scaled], [tok_rows])
        mates = near(list(early) * (column - 1) + list(late))
    steps = [most * 11 // 16, most * 13 // 16, most]
    total = PLANES * steps[0]
    usual = route(first, outward(steps[0], own_goal)[0], [acts], [total])[0]
    if ring:
        first.last += [weight_z]
    scaled_sent = route(first, inward(most, True)[0], scaled_z, blocks_out)

    def run(size):
        line = Line()
        total = PLANES * size
        out_rows, back_rows = outward(size, own_goal)
        spread, gather = inward(size)
        if ring:
            weight = gather_all(weight_z, "groups").reshape(parts, PLANES, share, deep)
        else:
            weight = gather_all(frozen_key_weight, "dp")
        leaving = usual if size == steps[0] else route(line, out_rows, [acts], [total])[0]
        acts_z = planes_swap(leaving)
        got_scaled = at_owner(near(scaled_sent))
        back_low = back_project(line, adapter_up_slots, got_scaled)
        terms = adapter_terms(line, back_low, adapter_down_slots, owner_outs)
        terms = near(from_owner(terms))
        if ring:
            bases = near(base_step(line, weight, mates))
        else:
            bases = [dot(weight, scaled, 1, 1).astype(BF)]
        came = planes_swap(route(line, gather, terms, [total])[0])
        got = route(line, spread, [acts_z], blocks_out)
        got = at_owner(near(got))
        low, grad_a = owner_step(line, back_low, adapter_down_slots, got)
        grad_b = up_gradient(line, low, got_scaled)
        result = final_step(line, back_rows, came, bases)
        return result, grad_a, grad_b

    which = sum((need_all > s).astype(jnp.int32) for s in steps[:-1])
    return lax.switch(which, [functools.partial(run, s) for s in steps])


def solution(mesh):
    return jax.shard_map(
        shards,
        mesh=mesh,
        in_specs=(
            P(("groups", "dp"), None),
            P(("groups", "dp"), None),
            P("dp", None),
            P(("groups", "dp"), None, None),
            P(("groups", "dp"), None, None),
            P(("groups", "dp"), None),
            P("groups"),
            P("groups"),
        ),
        out_specs=(
            P(("groups", "dp"), None),
            P(("groups", "dp"), None, None),
            P(("groups", "dp"), None, None),
        ),
        check_vma=False,
    )
```

```python
import functools

import jax
import jax.numpy as jnp
from jax import lax
from jax.experimental import pallas as pl
from jax.experimental.pallas import tpu as pltpu
from jax.sharding import PartitionSpec as P

DELTA_MULTIPLIER = 0.25
BF = jnp.bfloat16
F32 = jnp.float32
PLANES = 4
PIECES = 4
PARAMS = pltpu.CompilerParams(vmem_limit_bytes=48 * 1024 * 1024)


def far(shape, dtype=BF):
    return pltpu.HBM(shape, dtype)


def whole(shape):
    zeros = (0,) * len(shape)
    return pl.BlockSpec(shape, lambda i: zeros)


def dot(a, b, ca=1, cb=0):
    return lax.dot_general(a, b, (((ca,), (cb,)), ((), ())), preferred_element_type=F32)


HERE = pl.BlockSpec(memory_space=pl.ANY)


def note_body(ref, out):
    out[...] = ref[...]


def note_step(line, note):
    return line.call(
        note_body,
        [note],
        [whole(note.shape)],
        whole(note.shape),
        jax.ShapeDtypeStruct(note.shape, note.dtype),
    )


def route_body(count, rows_ref, *refs):
    ins, outs = refs[:count], refs[count:]
    held = ins[0][...] if count == 1 else jnp.concatenate([r[...] for r in ins], axis=0)
    moved = dot(rows_ref[...], held).astype(BF)
    at = 0
    for out in outs:
        out[...] = moved[at : at + out.shape[0]]
        at += out.shape[0]


class Line:
    def __init__(self):
        self.last = []

    def call(self, body, operands, in_specs, out_specs, out_shape, pieces=1, scratch=()):
        after = self.last
        first = len(operands)
        many = isinstance(out_shape, list)

        def kernel(*refs):
            mark = len(refs) - 1 - len(scratch)
            refs[mark][...] = jnp.zeros_like(refs[mark])
            body(*refs[:first], *refs[first + len(after) : mark], *refs[mark + 1 :])

        out = pl.pallas_call(
            kernel,
            grid=(pieces,),
            in_specs=in_specs + [HERE] * len(after),
            out_specs=(out_specs if many else [out_specs]) + [whole((8, 128))],
            out_shape=(out_shape if many else [out_shape])
            + [jax.ShapeDtypeStruct((8, 128), jnp.int32)],
            scratch_shapes=scratch,
            compiler_params=PARAMS,
        )(*operands, *after)
        self.last = [out[-1]]
        return out[:-1] if many else out[0]


def route_body(count, rows_ref, *refs):
    ins, outs = refs[:count], refs[count:]
    held = ins[0][...] if count == 1 else jnp.concatenate([r[...] for r in ins], axis=0)
    moved = dot(rows_ref[...], held).astype(BF)
    at = 0
    for out in outs:
        out[...] = moved[at : at + out.shape[0]]
        at += out.shape[0]


class Line:
    def __init__(self):
        self.last = []

    def call(self, body, operands, in_specs, out_specs, out_shape, pieces=1, scratch=()):
        after = self.last
        first = len(operands)
        many = isinstance(out_shape, list)

        def kernel(*refs):
            mark = len(refs) - 1 - len(scratch)
            refs[mark][...] = jnp.zeros_like(refs[mark])
            body(*refs[:first], *refs[first + len(after) : mark], *refs[mark + 1 :])

        out = pl.pallas_call(
            kernel,
            grid=(pieces,),
            in_specs=in_specs + [HERE] * len(after),
            out_specs=(out_specs if many else [out_specs]) + [whole((8, 128))],
            out_shape=(out_shape if many else [out_shape])
            + [jax.ShapeDtypeStruct((8, 128), jnp.int32)],
            scratch_shapes=scratch,
            compiler_params=PARAMS,
        )(*operands, *after)
        self.last = [out[-1]]
        return out[:-1] if many else out[0]


def hold_body(ref, out):
    pass


def hold(line, x):
    last = line.last
    out = line.call(hold_body, [x], [FAR], FAR, far(x.shape, x.dtype), 1, {0: 0})
    line.last = last
    return out


def route(line, rows, ins, outs):
    width = ins[0].shape[1]
    pieces = PIECES if width % (128 * PIECES) == 0 else 1
    step = width // pieces
    return line.call(
        functools.partial(route_body, len(ins)),
        [rows, *ins],
        [whole(rows.shape)]
        + [pl.BlockSpec((x.shape[0], step), lambda i: (0, i)) for x in ins],
        [pl.BlockSpec((n, step), lambda i: (0, i)) for n in outs],
        [far((n, width)) for n in outs],
        pieces,
    )


def job_rows(refs, job):
    return jnp.concatenate([ref[job] for ref in refs], axis=0)


def back_body(count, up_ref, *refs):
    out = refs[count]
    for job in range(up_ref.shape[0]):
        held = job_rows(refs[:count], job)
        out[job] = (DELTA_MULTIPLIER * dot(held, up_ref[job], 1, 1)).astype(BF)


def back_project(line, up, rows):
    local, rank = up.shape[0], up.shape[1]
    shape = (local, sum(x.shape[1] for x in rows), rank)
    return line.call(
        functools.partial(back_body, len(rows)),
        [up, *rows],
        [whole(up.shape)] + [whole(x.shape) for x in rows],
        whole(shape),
        jax.ShapeDtypeStruct(shape, BF),
    )


def term_body(back_ref, down_ref, *outs):
    for job in range(down_ref.shape[0]):
        term = dot(back_ref[job], down_ref[job], 1, 1).astype(BF)
        at = 0
        for out in outs:
            out[job] = term[at : at + out.shape[1]]
            at += out.shape[1]


def adapter_terms(line, back_low, down, outs):
    local, width, rank = down.shape
    step = width // PIECES
    return line.call(
        term_body,
        [back_low, down],
        [whole(back_low.shape), pl.BlockSpec((local, step, rank), lambda i: (0, i, 0))],
        [pl.BlockSpec((local, n, step), lambda i: (0, 0, i)) for n in outs],
        [far((local, n, width)) for n in outs],
        PIECES,
    )


def owner_body(count, back_ref, down_ref, *refs):
    ins, (low_ref, grad_ref) = refs[:count], refs[count:]

    @pl.when(pl.program_id(0) == 0)
    def _():
        low_ref[...] = jnp.zeros_like(low_ref)

    for job in range(down_ref.shape[0]):
        held = job_rows(ins, job)
        low_ref[job] += dot(held, down_ref[job])
        grad_ref[job] = dot(held, back_ref[job], 0, 0).astype(BF)


def owner_step(line, back_low, down, rows):
    local, width, rank = down.shape
    step = width // PIECES
    part = pl.BlockSpec((local, step, rank), lambda i: (0, i, 0))
    low_shape = (local, back_low.shape[1], rank)
    return line.call(
        functools.partial(owner_body, len(rows)),
        [back_low, down, *rows],
        [whole(back_low.shape), part]
        + [pl.BlockSpec((local, x.shape[1], step), lambda i: (0, 0, i)) for x in rows],
        [whole(low_shape), part],
        [jax.ShapeDtypeStruct(low_shape, F32), jax.ShapeDtypeStruct(down.shape, BF)],
        PIECES,
    )


def up_body(count, low_ref, *refs):
    out = refs[count]
    for job in range(low_ref.shape[0]):
        low = low_ref[job].astype(BF)
        held = job_rows(refs[:count], job)
        out[job] = (DELTA_MULTIPLIER * dot(low, held, 0, 0)).astype(BF)


def up_gradient(line, low, rows):
    shape = (low.shape[0], low.shape[2], rows[0].shape[2])
    return line.call(
        functools.partial(up_body, len(rows)),
        [low, *rows],
        [whole(low.shape)] + [whole(x.shape) for x in rows],
        whole(shape),
        jax.ShapeDtypeStruct(shape, BF),
    )


def base_body(count, weight_ref, *refs):
    ins, outs = refs[:count], refs[count:]
    weight = jnp.concatenate([weight_ref[at, 0] for at in range(weight_ref.shape[0])], axis=0)
    for x, out in zip(ins, outs):
        out[...] = dot(weight, x[...], 1, 1).astype(BF)


def base_step(line, weight, rows):
    parts, planes, share, deep = weight.shape
    step, tokens = parts * share, rows[0].shape[0]
    return line.call(
        functools.partial(base_body, len(rows)),
        [weight, *rows],
        [pl.BlockSpec((parts, 1, share, deep), lambda i: (0, i, 0, 0))]
        + [whole(x.shape) for x in rows],
        [pl.BlockSpec((step, tokens), lambda i: (i, 0)) for _ in rows],
        [far((planes * step, tokens)) for _ in rows],
        planes,
    )


def final_body(count, rows_ref, came_ref, *refs):
    bases, out, held = refs[:count], refs[count], refs[count + 1]
    size = bases[0].shape[0]
    place = lax.rem(lax.axis_index("dp"), count)
    for s, ref in enumerate(bases):
        held[pl.ds(pl.multiple_of((place ^ s) * size, 16), size)] = ref[...]
    tokens = held.shape[1]
    one = (
        lax.broadcasted_iota(jnp.int32, (tokens, tokens), 0)
        == lax.broadcasted_iota(jnp.int32, (tokens, tokens), 1)
    ).astype(F32)
    base = dot(one.astype(BF), held[...], 1, 1)
    out[...] = (base + dot(rows_ref[...], came_ref[...])).astype(BF)


def final_step(line, rows, came, bases):
    tokens = rows.shape[0]
    step = came.shape[1] // PLANES
    size = step // len(bases)
    return line.call(
        functools.partial(final_body, len(bases)),
        [rows, came, *bases],
        [whole(rows.shape), pl.BlockSpec((came.shape[0], step), lambda i: (0, i))]
        + [pl.BlockSpec((size, tokens), lambda i: (i, 0)) for _ in bases],
        pl.BlockSpec((tokens, step), lambda i: (0, i)),
        jax.ShapeDtypeStruct((tokens, step * PLANES), BF),
        PLANES,
        [pltpu.VMEM((step, tokens), BF)],
    )


def shards(
    acts,
    cotan,
    frozen_key_weight,
    adapter_down_slots,
    adapter_up_slots,
    token_row_jobs,
    slot_owner_jobs,
    loss_token_count,
):
    devices = lax.axis_size("dp")
    parts = lax.axis_size("groups")
    tok_rows = acts.shape[0]
    local = adapter_down_slots.shape[0]
    jobs_all = slot_owner_jobs.shape[0]
    depth = 2 * tok_rows // (local * devices)
    column = devices // PLANES
    ring = column <= 4
    most = local * column * depth
    segment = PLANES * depth
    me = lax.axis_index("dp")
    plane, place = me // column, me % column

    first = Line()
    stripes = [[p * column + c for p in range(PLANES)] for c in range(column)]
    ids = token_row_jobs[:, 0]
    lengths = loss_token_count.astype(F32)
    weights = jnp.mean(lengths) / lengths
    numbers = jnp.arange(jobs_all, dtype=jnp.int32)
    row_weight = jnp.sum(jnp.where(ids[:, None] == numbers[None, :], weights[None, :], 0.0), axis=1)
    row_slot = jnp.sum(
        jnp.where(ids[:, None] == slot_owner_jobs[None, :], numbers[None, :], 0), axis=1
    )
    scaled = (row_weight[:, None] * cotan.astype(F32)).astype(BF)

    planes = jnp.arange(PLANES, dtype=jnp.int32)
    need = jnp.max(
        jnp.sum((row_slot[:, None] // (local * column) == planes[None, :]).astype(jnp.int32), axis=0)
    )
    note = jnp.concatenate([row_slot, jnp.full((128,), need, jnp.int32)])
    share = frozen_key_weight.shape[0] // parts
    deep = frozen_key_weight.shape[1]
    own_share = lax.dynamic_slice_in_dim(
        frozen_key_weight, lax.axis_index("groups") * share, share, 0
    )
    if ring:
        weight_z = lax.all_gather(
            own_share, "dp", axis=0, tiled=True, axis_index_groups=stripes
        )
        first.last = [own_share]
        note = note_step(first, note[None])[0]
    note = jnp.broadcast_to(note[None, None], (parts * devices, 1, tok_rows + 128))
    first.last = [note]
    notes = lax.all_to_all(
        note,
        ("groups", "dp"),
        split_axis=0,
        concat_axis=0,
        tiled=True,
    )[:, 0]
    need_all = jnp.max(notes[:, tok_rows])
    mine = notes[:, :tok_rows].reshape(parts, PLANES, column, tok_rows)
    mine = lax.dynamic_index_in_dim(mine, lax.axis_index("groups"), 0, keepdims=False)
    mine = lax.dynamic_index_in_dim(mine, place, 1, keepdims=False)
    slots = mine
    goal = slots // (local * column)
    earlier = jnp.arange(tok_rows)[None, :] < jnp.arange(tok_rows)[:, None]
    order = jnp.sum(
        ((goal[:, :, None] == goal[:, None, :]) & earlier[None]).astype(jnp.int32), axis=2
    )
    rank = jnp.sum(
        ((slots[:, :, None] == slots[:, None, :]) & earlier[None]).astype(jnp.int32), axis=2
    )
    owner = (slots // local) % column
    if ring:
        owner = owner ^ place
    spot = (
        owner * (local * segment)
        + (slots % local) * segment
        + planes[:, None] * depth
        + rank
    )
    spot = jnp.where(goal == plane, spot, -1)
    own_goal = row_slot // (local * column)
    own_order = jnp.sum(
        ((own_goal[:, None] == own_goal[None, :]) & earlier).astype(jnp.int32), axis=1
    )

    def across(bufs):
        return [bufs[0]] + [
            lax.ppermute(
                bufs[s],
                "dp",
                [(d, ((d // column) ^ s) * column + d % column) for d in range(devices)],
            )
            for s in range(1, PLANES)
        ]

    blocks = [[p * column + c for c in range(column)] for p in range(PLANES)]

    def within(x):
        return lax.all_to_all(
            x, "dp", split_axis=0, concat_axis=0, tiled=True, axis_index_groups=blocks
        )

    blocks_out = [local * segment] * column if ring else [column * local * segment]
    owner_outs = [segment] * column if ring else [column * segment]

    def near(bufs):
        if not ring:
            return [within(bufs[0])]
        return [bufs[0]] + [
            lax.ppermute(bufs[s], "dp", [(d, d ^ s) for d in range(devices)])
            for s in range(1, column)
        ]

    def at_owner(bufs):
        width = bufs[0].shape[1]
        if ring:
            return [x.reshape(local, segment, width) for x in bufs]
        x = bufs[0].reshape(column, local, segment, width).transpose(1, 0, 2, 3)
        return [x.reshape(local, column * segment, width)]

    def from_owner(bufs):
        width = bufs[0].shape[2]
        if ring:
            return [x.reshape(local * segment, width) for x in bufs]
        x = bufs[0].reshape(local, column, segment, width).transpose(1, 0, 2, 3)
        return [x.reshape(column * local * segment, width)]

    def planes_swap(x):
        return lax.all_to_all(
            x, "dp", split_axis=0, concat_axis=0, tiled=True, axis_index_groups=stripes
        )

    def gather_all(x, axis, groups=None):
        return lax.all_gather(x, axis, axis=0, tiled=True, axis_index_groups=groups)

    def outward(size, side):
        lanes = jnp.arange(PLANES * size, dtype=jnp.int32)
        code = side * size + own_order
        return (lanes[:, None] == code[None, :]).astype(BF), (
            code[:, None] == lanes[None, :]
        ).astype(BF)

    def inward(size, turned=False):
        kth = jnp.arange(size, dtype=jnp.int32)
        target = jnp.sum(
            jnp.where(
                (order[:, None, :] == kth[None, :, None]) & (spot[:, None, :] >= 0),
                spot[:, None, :] + 1,
                0,
            ),
            axis=2,
        )
        if turned:
            there = (planes ^ plane)[:, None, None] == planes[None, :, None]
            target = jnp.sum(jnp.where(there, target[None], 0), axis=1)
        target = target.reshape(PLANES * size) - 1
        spots = jnp.arange(PLANES * most, dtype=jnp.int32)
        return (spots[:, None] == target[None, :]).astype(BF), (
            target[:, None] == spots[None, :]
        ).astype(BF)

    rows_out = outward(most, own_goal ^ plane)[0]
    scaled_z = across(route(first, rows_out, [scaled], [most] * PLANES))
    if ring:
        lanes = jnp.arange(tok_rows, dtype=jnp.int32)
        same_rows = (lanes[:, None] == lanes[None, :]).astype(BF)
        early = route(first, same_rows, [scaled], [tok_rows])[0]
        mates = [
            early,
            *(lax.ppermute(early, "dp", [(d, d ^ s) for d in range(devices)]) for s in range(1, 3)),
        ]
        first.last += mates[1:2]
        late = route(first, same_rows, [scaled], [tok_rows])[0]
        mates += [
            lax.ppermute(late, "dp", [(d, d ^ s) for d in range(devices)])
            for s in range(3, column)
        ]
        mates = mates[:column]
    steps = [most * 11 // 16, most * 13 // 16, most]
    total = PLANES * steps[0]
    usual = route(first, outward(steps[0], own_goal)[0], [acts], [total])[0]
    if ring:
        first.last += [weight_z]
    scaled_sent = route(first, inward(most, True)[0], scaled_z, blocks_out)

    def run(size):
        line = Line()
        total = PLANES * size
        out_rows, back_rows = outward(size, own_goal)
        spread, gather = inward(size)
        if ring:
            weight = gather_all(weight_z, "groups").reshape(parts, PLANES, share, deep)
        else:
            weight = gather_all(frozen_key_weight, "dp")
        leaving = usual if size == steps[0] else route(line, out_rows, [acts], [total])[0]
        acts_z = planes_swap(leaving)
        got_scaled = at_owner(near(scaled_sent))
        back_low = back_project(line, adapter_up_slots, got_scaled)
        terms = adapter_terms(line, back_low, adapter_down_slots, owner_outs)
        terms = near(from_owner(terms))
        if ring:
            bases = near(base_step(line, weight, mates))
        else:
            bases = [dot(weight, scaled, 1, 1).astype(BF)]
        got = route(line, spread, [acts_z], blocks_out)
        came = planes_swap(route(line, gather, terms, [total])[0])
        got = at_owner(near(got))
        low, grad_a = owner_step(line, back_low, adapter_down_slots, got)
        grad_b = up_gradient(line, low, got_scaled)
        result = final_step(line, back_rows, came, bases)
        return result, grad_a, grad_b

    which = sum((need_all > s).astype(jnp.int32) for s in steps[:-1])
    return lax.switch(which, [functools.partial(run, s) for s in steps])


def solution(mesh):
    return jax.shard_map(
        shards,
        mesh=mesh,
        in_specs=(
            P(("groups", "dp"), None),
            P(("groups", "dp"), None),
            P("dp", None),
            P(("groups", "dp"), None, None),
            P(("groups", "dp"), None, None),
            P(("groups", "dp"), None),
            P("groups"),
            P("groups"),
        ),
        out_specs=(
            P(("groups", "dp"), None),
            P(("groups", "dp"), None, None),
            P(("groups", "dp"), None, None),
        ),
        check_vma=False,
    )
```

```python
import functools

import jax
import jax.numpy as jnp
from jax import lax
from jax.experimental import pallas as pl
from jax.experimental.pallas import tpu as pltpu
from jax.sharding import PartitionSpec as P

DELTA_MULTIPLIER = 0.25
BF = jnp.bfloat16
F32 = jnp.float32
PLANES = 4
PIECES = 4
PARAMS = pltpu.CompilerParams(vmem_limit_bytes=48 * 1024 * 1024)


def far(shape, dtype=BF):
    return pltpu.HBM(shape, dtype)


def whole(shape):
    zeros = (0,) * len(shape)
    return pl.BlockSpec(shape, lambda i: zeros)


def dot(a, b, ca=1, cb=0):
    return lax.dot_general(a, b, (((ca,), (cb,)), ((), ())), preferred_element_type=F32)


HERE = pl.BlockSpec(memory_space=pl.ANY)


def note_body(ref, out):
    out[...] = ref[...]


def note_step(line, note):
    return line.call(
        note_body,
        [note],
        [whole(note.shape)],
        whole(note.shape),
        jax.ShapeDtypeStruct(note.shape, note.dtype),
    )


def route_body(count, rows_ref, *refs):
    ins, outs = refs[:count], refs[count:]
    held = ins[0][...] if count == 1 else jnp.concatenate([r[...] for r in ins], axis=0)
    moved = dot(rows_ref[...], held).astype(BF)
    at = 0
    for out in outs:
        out[...] = moved[at : at + out.shape[0]]
        at += out.shape[0]


class Line:
    def __init__(self):
        self.last = []

    def call(self, body, operands, in_specs, out_specs, out_shape, pieces=1, scratch=()):
        after = self.last
        first = len(operands)
        many = isinstance(out_shape, list)

        def kernel(*refs):
            mark = len(refs) - 1 - len(scratch)
            refs[mark][...] = jnp.zeros_like(refs[mark])
            body(*refs[:first], *refs[first + len(after) : mark], *refs[mark + 1 :])

        out = pl.pallas_call(
            kernel,
            grid=(pieces,),
            in_specs=in_specs + [HERE] * len(after),
            out_specs=(out_specs if many else [out_specs]) + [whole((8, 128))],
            out_shape=(out_shape if many else [out_shape])
            + [jax.ShapeDtypeStruct((8, 128), jnp.int32)],
            scratch_shapes=scratch,
            compiler_params=PARAMS,
        )(*operands, *after)
        self.last = [out[-1]]
        return out[:-1] if many else out[0]


def route_body(count, rows_ref, *refs):
    ins, outs = refs[:count], refs[count:]
    held = ins[0][...] if count == 1 else jnp.concatenate([r[...] for r in ins], axis=0)
    moved = dot(rows_ref[...], held).astype(BF)
    at = 0
    for out in outs:
        out[...] = moved[at : at + out.shape[0]]
        at += out.shape[0]


class Line:
    def __init__(self):
        self.last = []

    def call(self, body, operands, in_specs, out_specs, out_shape, pieces=1, scratch=()):
        after = self.last
        first = len(operands)
        many = isinstance(out_shape, list)

        def kernel(*refs):
            mark = len(refs) - 1 - len(scratch)
            refs[mark][...] = jnp.zeros_like(refs[mark])
            body(*refs[:first], *refs[first + len(after) : mark], *refs[mark + 1 :])

        out = pl.pallas_call(
            kernel,
            grid=(pieces,),
            in_specs=in_specs + [HERE] * len(after),
            out_specs=(out_specs if many else [out_specs]) + [whole((8, 128))],
            out_shape=(out_shape if many else [out_shape])
            + [jax.ShapeDtypeStruct((8, 128), jnp.int32)],
            scratch_shapes=scratch,
            compiler_params=PARAMS,
        )(*operands, *after)
        self.last = [out[-1]]
        return out[:-1] if many else out[0]


def hold_body(ref, out):
    pass


def hold(line, x):
    last = line.last
    out = line.call(hold_body, [x], [FAR], FAR, far(x.shape, x.dtype), 1, {0: 0})
    line.last = last
    return out


def route(line, rows, ins, outs):
    width = ins[0].shape[1]
    pieces = PIECES if width % (128 * PIECES) == 0 else 1
    step = width // pieces
    return line.call(
        functools.partial(route_body, len(ins)),
        [rows, *ins],
        [whole(rows.shape)]
        + [pl.BlockSpec((x.shape[0], step), lambda i: (0, i)) for x in ins],
        [pl.BlockSpec((n, step), lambda i: (0, i)) for n in outs],
        [far((n, width)) for n in outs],
        pieces,
    )


def job_rows(refs, job):
    return jnp.concatenate([ref[job] for ref in refs], axis=0)


def back_body(count, up_ref, *refs):
    out = refs[count]
    for job in range(up_ref.shape[0]):
        held = job_rows(refs[:count], job)
        out[job] = (DELTA_MULTIPLIER * dot(held, up_ref[job], 1, 1)).astype(BF)


def back_project(line, up, rows):
    local, rank = up.shape[0], up.shape[1]
    shape = (local, sum(x.shape[1] for x in rows), rank)
    return line.call(
        functools.partial(back_body, len(rows)),
        [up, *rows],
        [whole(up.shape)] + [whole(x.shape) for x in rows],
        whole(shape),
        jax.ShapeDtypeStruct(shape, BF),
    )


def term_body(back_ref, down_ref, *outs):
    for job in range(down_ref.shape[0]):
        term = dot(back_ref[job], down_ref[job], 1, 1).astype(BF)
        at = 0
        for out in outs:
            out[job] = term[at : at + out.shape[1]]
            at += out.shape[1]


def adapter_terms(line, back_low, down, outs):
    local, width, rank = down.shape
    step = width // PIECES
    return line.call(
        term_body,
        [back_low, down],
        [whole(back_low.shape), pl.BlockSpec((local, step, rank), lambda i: (0, i, 0))],
        [pl.BlockSpec((local, n, step), lambda i: (0, 0, i)) for n in outs],
        [far((local, n, width)) for n in outs],
        PIECES,
    )


def owner_body(count, back_ref, down_ref, *refs):
    ins, (low_ref, grad_ref) = refs[:count], refs[count:]

    @pl.when(pl.program_id(0) == 0)
    def _():
        low_ref[...] = jnp.zeros_like(low_ref)

    for job in range(down_ref.shape[0]):
        held = job_rows(ins, job)
        low_ref[job] += dot(held, down_ref[job])
        grad_ref[job] = dot(held, back_ref[job], 0, 0).astype(BF)


def owner_step(line, back_low, down, rows):
    local, width, rank = down.shape
    step = width // PIECES
    part = pl.BlockSpec((local, step, rank), lambda i: (0, i, 0))
    low_shape = (local, back_low.shape[1], rank)
    return line.call(
        functools.partial(owner_body, len(rows)),
        [back_low, down, *rows],
        [whole(back_low.shape), part]
        + [pl.BlockSpec((local, x.shape[1], step), lambda i: (0, 0, i)) for x in rows],
        [whole(low_shape), part],
        [jax.ShapeDtypeStruct(low_shape, F32), jax.ShapeDtypeStruct(down.shape, BF)],
        PIECES,
    )


def up_body(count, low_ref, *refs):
    out = refs[count]
    for job in range(low_ref.shape[0]):
        low = low_ref[job].astype(BF)
        held = job_rows(refs[:count], job)
        out[job] = (DELTA_MULTIPLIER * dot(low, held, 0, 0)).astype(BF)


def up_gradient(line, low, rows):
    shape = (low.shape[0], low.shape[2], rows[0].shape[2])
    return line.call(
        functools.partial(up_body, len(rows)),
        [low, *rows],
        [whole(low.shape)] + [whole(x.shape) for x in rows],
        whole(shape),
        jax.ShapeDtypeStruct(shape, BF),
    )


def base_body(count, mine_ref, other_ref, *refs):
    ins, outs = refs[:count], refs[count:]
    lower = lax.axis_index("groups") == 0
    mine, other = mine_ref[0], other_ref[0]
    weight = jnp.concatenate(
        [jnp.where(lower, mine, other), jnp.where(lower, other, mine)], axis=0
    )
    for x, out in zip(ins, outs):
        out[...] = dot(weight, x[...], 1, 1).astype(BF)


def base_step(line, weight, rows):
    planes, share, deep = weight[0].shape
    step, tokens = 2 * share, rows[0].shape[0]
    half = pl.BlockSpec((1, share, deep), lambda i: (i, 0, 0))
    return line.call(
        functools.partial(base_body, len(rows)),
        [*weight, *rows],
        [half, half] + [whole(x.shape) for x in rows],
        [pl.BlockSpec((step, tokens), lambda i: (i, 0)) for _ in rows],
        [far((planes * step, tokens)) for _ in rows],
        planes,
    )


def final_body(count, rows_ref, came_ref, *refs):
    bases, out, held = refs[:count], refs[count], refs[count + 1]
    size = bases[0].shape[0]
    place = lax.rem(lax.axis_index("dp"), count)
    for s, ref in enumerate(bases):
        held[pl.ds(pl.multiple_of((place ^ s) * size, 16), size)] = ref[...]
    tokens = held.shape[1]
    one = (
        lax.broadcasted_iota(jnp.int32, (tokens, tokens), 0)
        == lax.broadcasted_iota(jnp.int32, (tokens, tokens), 1)
    ).astype(F32)
    base = dot(one.astype(BF), held[...], 1, 1)
    out[...] = (base + dot(rows_ref[...], came_ref[...])).astype(BF)


def final_step(line, rows, came, bases):
    tokens = rows.shape[0]
    step = came.shape[1] // PLANES
    size = step // len(bases)
    return line.call(
        functools.partial(final_body, len(bases)),
        [rows, came, *bases],
        [whole(rows.shape), pl.BlockSpec((came.shape[0], step), lambda i: (0, i))]
        + [pl.BlockSpec((size, tokens), lambda i: (i, 0)) for _ in bases],
        pl.BlockSpec((tokens, step), lambda i: (0, i)),
        jax.ShapeDtypeStruct((tokens, step * PLANES), BF),
        PLANES,
        [pltpu.VMEM((step, tokens), BF)],
    )


def shards(
    acts,
    cotan,
    frozen_key_weight,
    adapter_down_slots,
    adapter_up_slots,
    token_row_jobs,
    slot_owner_jobs,
    loss_token_count,
):
    devices = lax.axis_size("dp")
    parts = lax.axis_size("groups")
    tok_rows = acts.shape[0]
    local = adapter_down_slots.shape[0]
    jobs_all = slot_owner_jobs.shape[0]
    depth = 2 * tok_rows // (local * devices)
    column = devices // PLANES
    ring = column <= 4 and parts == 2
    most = local * column * depth
    segment = PLANES * depth
    me = lax.axis_index("dp")
    plane, place = me // column, me % column

    first = Line()
    stripes = [[p * column + c for p in range(PLANES)] for c in range(column)]
    ids = token_row_jobs[:, 0]
    lengths = loss_token_count.astype(F32)
    weights = jnp.mean(lengths) / lengths
    numbers = jnp.arange(jobs_all, dtype=jnp.int32)
    row_weight = jnp.sum(jnp.where(ids[:, None] == numbers[None, :], weights[None, :], 0.0), axis=1)
    row_slot = jnp.sum(
        jnp.where(ids[:, None] == slot_owner_jobs[None, :], numbers[None, :], 0), axis=1
    )
    scaled = (row_weight[:, None] * cotan.astype(F32)).astype(BF)

    planes = jnp.arange(PLANES, dtype=jnp.int32)
    need = jnp.max(
        jnp.sum((row_slot[:, None] // (local * column) == planes[None, :]).astype(jnp.int32), axis=0)
    )
    note = jnp.concatenate([row_slot, jnp.full((128,), need, jnp.int32)])
    share = frozen_key_weight.shape[0] // parts
    deep = frozen_key_weight.shape[1]
    own_share = lax.dynamic_slice_in_dim(
        frozen_key_weight, lax.axis_index("groups") * share, share, 0
    )
    if ring:
        shares = [own_share] + [
            lax.ppermute(
                own_share,
                "dp",
                [(d, ((d // column) ^ s) * column + d % column) for d in range(devices)],
            )
            for s in range(1, PLANES)
        ]
        first.last = shares[1:]
        note = note_step(first, note[None])[0]
        shares = jnp.stack(shares)
        turn = jnp.arange(PLANES, dtype=jnp.int32) ^ plane
        weight_z = shares[0][None]
        for s in range(1, PLANES):
            weight_z = jnp.where((turn == s)[:, None, None], shares[s][None], weight_z)
    note = jnp.broadcast_to(note[None, None], (parts * devices, 1, tok_rows + 128))
    first.last = [note]
    notes = lax.all_to_all(
        note,
        ("groups", "dp"),
        split_axis=0,
        concat_axis=0,
        tiled=True,
    )[:, 0]
    need_all = jnp.max(notes[:, tok_rows])
    mine = notes[:, :tok_rows].reshape(parts, PLANES, column, tok_rows)
    mine = lax.dynamic_index_in_dim(mine, lax.axis_index("groups"), 0, keepdims=False)
    mine = lax.dynamic_index_in_dim(mine, place, 1, keepdims=False)
    slots = mine
    goal = slots // (local * column)
    earlier = jnp.arange(tok_rows)[None, :] < jnp.arange(tok_rows)[:, None]
    order = jnp.sum(
        ((goal[:, :, None] == goal[:, None, :]) & earlier[None]).astype(jnp.int32), axis=2
    )
    rank = jnp.sum(
        ((slots[:, :, None] == slots[:, None, :]) & earlier[None]).astype(jnp.int32), axis=2
    )
    owner = (slots // local) % column
    if ring:
        owner = owner ^ place
    spot = (
        owner * (local * segment)
        + (slots % local) * segment
        + planes[:, None] * depth
        + rank
    )
    spot = jnp.where(goal == plane, spot, -1)
    own_goal = row_slot // (local * column)
    own_order = jnp.sum(
        ((own_goal[:, None] == own_goal[None, :]) & earlier).astype(jnp.int32), axis=1
    )

    def across(bufs):
        return [bufs[0]] + [
            lax.ppermute(
                bufs[s],
                "dp",
                [(d, ((d // column) ^ s) * column + d % column) for d in range(devices)],
            )
            for s in range(1, PLANES)
        ]

    blocks = [[p * column + c for c in range(column)] for p in range(PLANES)]

    def within(x):
        return lax.all_to_all(
            x, "dp", split_axis=0, concat_axis=0, tiled=True, axis_index_groups=blocks
        )

    blocks_out = [local * segment] * column if ring else [column * local * segment]
    owner_outs = [segment] * column if ring else [column * segment]

    def near(bufs):
        if not ring:
            return [within(bufs[0])]
        return [bufs[0]] + [
            lax.ppermute(bufs[s], "dp", [(d, d ^ s) for d in range(devices)])
            for s in range(1, column)
        ]

    def at_owner(bufs):
        width = bufs[0].shape[1]
        if ring:
            return [x.reshape(local, segment, width) for x in bufs]
        x = bufs[0].reshape(column, local, segment, width).transpose(1, 0, 2, 3)
        return [x.reshape(local, column * segment, width)]

    def from_owner(bufs):
        width = bufs[0].shape[2]
        if ring:
            return [x.reshape(local * segment, width) for x in bufs]
        x = bufs[0].reshape(local, column, segment, width).transpose(1, 0, 2, 3)
        return [x.reshape(column * local * segment, width)]

    def planes_swap(x):
        return lax.all_to_all(
            x, "dp", split_axis=0, concat_axis=0, tiled=True, axis_index_groups=stripes
        )

    def gather_all(x, axis, groups=None):
        return lax.all_gather(x, axis, axis=0, tiled=True, axis_index_groups=groups)

    def outward(size, side):
        lanes = jnp.arange(PLANES * size, dtype=jnp.int32)
        code = side * size + own_order
        return (lanes[:, None] == code[None, :]).astype(BF), (
            code[:, None] == lanes[None, :]
        ).astype(BF)

    def inward(size, turned=False):
        kth = jnp.arange(size, dtype=jnp.int32)
        target = jnp.sum(
            jnp.where(
                (order[:, None, :] == kth[None, :, None]) & (spot[:, None, :] >= 0),
                spot[:, None, :] + 1,
                0,
            ),
            axis=2,
        )
        if turned:
            there = (planes ^ plane)[:, None, None] == planes[None, :, None]
            target = jnp.sum(jnp.where(there, target[None], 0), axis=1)
        target = target.reshape(PLANES * size) - 1
        spots = jnp.arange(PLANES * most, dtype=jnp.int32)
        return (spots[:, None] == target[None, :]).astype(BF), (
            target[:, None] == spots[None, :]
        ).astype(BF)

    rows_out = outward(most, own_goal ^ plane)[0]
    scaled_z = across(route(first, rows_out, [scaled], [most] * PLANES))
    if ring:
        lanes = jnp.arange(tok_rows, dtype=jnp.int32)
        same_rows = (lanes[:, None] == lanes[None, :]).astype(BF)
        early = route(first, same_rows, [scaled], [tok_rows])[0]
        mates = [
            early,
            *(lax.ppermute(early, "dp", [(d, d ^ s) for d in range(devices)]) for s in range(1, 3)),
        ]
        first.last += mates[1:2]
        late = route(first, same_rows, [scaled], [tok_rows])[0]
        mates += [
            lax.ppermute(late, "dp", [(d, d ^ s) for d in range(devices)])
            for s in range(3, column)
        ]
        mates = mates[:column]
    steps = [most * 11 // 16, most * 13 // 16, most]
    total = PLANES * steps[0]
    usual = route(first, outward(steps[0], own_goal)[0], [acts], [total])[0]
    scaled_sent = route(first, inward(most, True)[0], scaled_z, blocks_out)

    def run(size):
        line = Line()
        total = PLANES * size
        out_rows, back_rows = outward(size, own_goal)
        spread, gather = inward(size)
        if ring:
            weight = weight_z, lax.ppermute(weight_z, "groups", [(0, 1), (1, 0)])
        else:
            weight = gather_all(frozen_key_weight, "dp")
        leaving = usual if size == steps[0] else route(line, out_rows, [acts], [total])[0]
        acts_z = planes_swap(leaving)
        got_scaled = at_owner(near(scaled_sent))
        back_low = back_project(line, adapter_up_slots, got_scaled)
        terms = adapter_terms(line, back_low, adapter_down_slots, owner_outs)
        terms = near(from_owner(terms))
        if ring:
            bases = near(base_step(line, weight, mates))
        else:
            bases = [dot(weight, scaled, 1, 1).astype(BF)]
        got = route(line, spread, [acts_z], blocks_out)
        came = planes_swap(route(line, gather, terms, [total])[0])
        got = at_owner(near(got))
        low, grad_a = owner_step(line, back_low, adapter_down_slots, got)
        grad_b = up_gradient(line, low, got_scaled)
        result = final_step(line, back_rows, came, bases)
        return result, grad_a, grad_b

    which = sum((need_all > s).astype(jnp.int32) for s in steps[:-1])
    return lax.switch(which, [functools.partial(run, s) for s in steps])


def solution(mesh):
    return jax.shard_map(
        shards,
        mesh=mesh,
        in_specs=(
            P(("groups", "dp"), None),
            P(("groups", "dp"), None),
            P("dp", None),
            P(("groups", "dp"), None, None),
            P(("groups", "dp"), None, None),
            P(("groups", "dp"), None),
            P("groups"),
            P("groups"),
        ),
        out_specs=(
            P(("groups", "dp"), None),
            P(("groups", "dp"), None, None),
            P(("groups", "dp"), None, None),
        ),
        check_vma=False,
    )
```

```python
import functools

import jax
import jax.numpy as jnp
from jax import lax
from jax.experimental import pallas as pl
from jax.experimental.pallas import tpu as pltpu
from jax.sharding import PartitionSpec as P

DELTA_MULTIPLIER = 0.25
BF = jnp.bfloat16
F32 = jnp.float32
PLANES = 4
PIECES = 4
PARAMS = pltpu.CompilerParams(vmem_limit_bytes=48 * 1024 * 1024)


def far(shape, dtype=BF):
    return pltpu.HBM(shape, dtype)


def whole(shape):
    zeros = (0,) * len(shape)
    return pl.BlockSpec(shape, lambda i: zeros)


def dot(a, b, ca=1, cb=0):
    return lax.dot_general(a, b, (((ca,), (cb,)), ((), ())), preferred_element_type=F32)


HERE = pl.BlockSpec(memory_space=pl.ANY)


def note_body(ref, out):
    out[...] = ref[...]


def note_step(line, note):
    return line.call(
        note_body,
        [note],
        [whole(note.shape)],
        whole(note.shape),
        jax.ShapeDtypeStruct(note.shape, note.dtype),
    )


def route_body(count, rows_ref, *refs):
    ins, outs = refs[:count], refs[count:]
    held = ins[0][...] if count == 1 else jnp.concatenate([r[...] for r in ins], axis=0)
    moved = dot(rows_ref[...], held).astype(BF)
    at = 0
    for out in outs:
        out[...] = moved[at : at + out.shape[0]]
        at += out.shape[0]


class Line:
    def __init__(self):
        self.last = []

    def call(self, body, operands, in_specs, out_specs, out_shape, pieces=1, scratch=()):
        after = self.last
        first = len(operands)
        many = isinstance(out_shape, list)

        def kernel(*refs):
            mark = len(refs) - 1 - len(scratch)
            refs[mark][...] = jnp.zeros_like(refs[mark])
            body(*refs[:first], *refs[first + len(after) : mark], *refs[mark + 1 :])

        out = pl.pallas_call(
            kernel,
            grid=(pieces,),
            in_specs=in_specs + [HERE] * len(after),
            out_specs=(out_specs if many else [out_specs]) + [whole((8, 128))],
            out_shape=(out_shape if many else [out_shape])
            + [jax.ShapeDtypeStruct((8, 128), jnp.int32)],
            scratch_shapes=scratch,
            compiler_params=PARAMS,
        )(*operands, *after)
        self.last = [out[-1]]
        return out[:-1] if many else out[0]


def route_body(count, rows_ref, *refs):
    ins, outs = refs[:count], refs[count:]
    held = ins[0][...] if count == 1 else jnp.concatenate([r[...] for r in ins], axis=0)
    moved = dot(rows_ref[...], held).astype(BF)
    at = 0
    for out in outs:
        out[...] = moved[at : at + out.shape[0]]
        at += out.shape[0]


class Line:
    def __init__(self):
        self.last = []

    def call(self, body, operands, in_specs, out_specs, out_shape, pieces=1, scratch=()):
        after = self.last
        first = len(operands)
        many = isinstance(out_shape, list)

        def kernel(*refs):
            mark = len(refs) - 1 - len(scratch)
            refs[mark][...] = jnp.zeros_like(refs[mark])
            body(*refs[:first], *refs[first + len(after) : mark], *refs[mark + 1 :])

        out = pl.pallas_call(
            kernel,
            grid=(pieces,),
            in_specs=in_specs + [HERE] * len(after),
            out_specs=(out_specs if many else [out_specs]) + [whole((8, 128))],
            out_shape=(out_shape if many else [out_shape])
            + [jax.ShapeDtypeStruct((8, 128), jnp.int32)],
            scratch_shapes=scratch,
            compiler_params=PARAMS,
        )(*operands, *after)
        self.last = [out[-1]]
        return out[:-1] if many else out[0]


def hold_body(ref, out):
    pass


def hold(line, x):
    last = line.last
    out = line.call(hold_body, [x], [FAR], FAR, far(x.shape, x.dtype), 1, {0: 0})
    line.last = last
    return out


def route(line, rows, ins, outs):
    width = ins[0].shape[1]
    pieces = PIECES if width % (128 * PIECES) == 0 else 1
    step = width // pieces
    return line.call(
        functools.partial(route_body, len(ins)),
        [rows, *ins],
        [whole(rows.shape)]
        + [pl.BlockSpec((x.shape[0], step), lambda i: (0, i)) for x in ins],
        [pl.BlockSpec((n, step), lambda i: (0, i)) for n in outs],
        [far((n, width)) for n in outs],
        pieces,
    )


def job_rows(refs, job):
    return jnp.concatenate([ref[job] for ref in refs], axis=0)


def back_body(count, up_ref, *refs):
    out = refs[count]
    for job in range(up_ref.shape[0]):
        held = job_rows(refs[:count], job)
        out[job] = (DELTA_MULTIPLIER * dot(held, up_ref[job], 1, 1)).astype(BF)


def back_project(line, up, rows):
    local, rank = up.shape[0], up.shape[1]
    shape = (local, sum(x.shape[1] for x in rows), rank)
    return line.call(
        functools.partial(back_body, len(rows)),
        [up, *rows],
        [whole(up.shape)] + [whole(x.shape) for x in rows],
        whole(shape),
        jax.ShapeDtypeStruct(shape, BF),
    )


def term_body(back_ref, down_ref, *outs):
    for job in range(down_ref.shape[0]):
        term = dot(back_ref[job], down_ref[job], 1, 1).astype(BF)
        at = 0
        for out in outs:
            out[job] = term[at : at + out.shape[1]]
            at += out.shape[1]


def adapter_terms(line, back_low, down, outs):
    local, width, rank = down.shape
    step = width // PIECES
    return line.call(
        term_body,
        [back_low, down],
        [whole(back_low.shape), pl.BlockSpec((local, step, rank), lambda i: (0, i, 0))],
        [pl.BlockSpec((local, n, step), lambda i: (0, 0, i)) for n in outs],
        [far((local, n, width)) for n in outs],
        PIECES,
    )


def owner_body(count, back_ref, down_ref, *refs):
    ins, (low_ref, grad_ref) = refs[:count], refs[count:]

    @pl.when(pl.program_id(0) == 0)
    def _():
        low_ref[...] = jnp.zeros_like(low_ref)

    for job in range(down_ref.shape[0]):
        held = job_rows(ins, job)
        low_ref[job] += dot(held, down_ref[job])
        grad_ref[job] = dot(held, back_ref[job], 0, 0).astype(BF)


def owner_step(line, back_low, down, rows):
    local, width, rank = down.shape
    step = width // PIECES
    part = pl.BlockSpec((local, step, rank), lambda i: (0, i, 0))
    low_shape = (local, back_low.shape[1], rank)
    return line.call(
        functools.partial(owner_body, len(rows)),
        [back_low, down, *rows],
        [whole(back_low.shape), part]
        + [pl.BlockSpec((local, x.shape[1], step), lambda i: (0, 0, i)) for x in rows],
        [whole(low_shape), part],
        [jax.ShapeDtypeStruct(low_shape, F32), jax.ShapeDtypeStruct(down.shape, BF)],
        PIECES,
    )


def up_body(count, low_ref, *refs):
    out = refs[count]
    for job in range(low_ref.shape[0]):
        low = low_ref[job].astype(BF)
        held = job_rows(refs[:count], job)
        out[job] = (DELTA_MULTIPLIER * dot(low, held, 0, 0)).astype(BF)


def up_gradient(line, low, rows):
    shape = (low.shape[0], low.shape[2], rows[0].shape[2])
    return line.call(
        functools.partial(up_body, len(rows)),
        [low, *rows],
        [whole(low.shape)] + [whole(x.shape) for x in rows],
        whole(shape),
        jax.ShapeDtypeStruct(shape, BF),
    )


def base_body(count, mine_ref, other_ref, *refs):
    ins, outs = refs[:count], refs[count:]
    lower = lax.axis_index("groups") == 0
    mine, other = mine_ref[0], other_ref[0]
    weight = jnp.concatenate(
        [jnp.where(lower, mine, other), jnp.where(lower, other, mine)], axis=0
    )
    for x, out in zip(ins, outs):
        out[...] = dot(weight, x[...], 1, 1).astype(BF)


def base_step(line, weight, rows):
    planes, share, deep = weight[0].shape
    step, tokens = 2 * share, rows[0].shape[0]
    half = pl.BlockSpec((1, share, deep), lambda i: (i, 0, 0))
    return line.call(
        functools.partial(base_body, len(rows)),
        [*weight, *rows],
        [half, half] + [whole(x.shape) for x in rows],
        [pl.BlockSpec((step, tokens), lambda i: (i, 0)) for _ in rows],
        [far((planes * step, tokens)) for _ in rows],
        planes,
    )


def final_body(count, rows_ref, came_ref, *refs):
    bases, out, held = refs[:count], refs[count], refs[count + 1]
    size = bases[0].shape[0]
    place = lax.rem(lax.axis_index("dp"), count)
    for s, ref in enumerate(bases):
        held[pl.ds(pl.multiple_of((place ^ s) * size, 16), size)] = ref[...]
    tokens = held.shape[1]
    one = (
        lax.broadcasted_iota(jnp.int32, (tokens, tokens), 0)
        == lax.broadcasted_iota(jnp.int32, (tokens, tokens), 1)
    ).astype(F32)
    base = dot(one.astype(BF), held[...], 1, 1)
    out[...] = (base + dot(rows_ref[...], came_ref[...])).astype(BF)


def final_step(line, rows, came, bases):
    tokens = rows.shape[0]
    step = came.shape[1] // PLANES
    size = step // len(bases)
    return line.call(
        functools.partial(final_body, len(bases)),
        [rows, came, *bases],
        [whole(rows.shape), pl.BlockSpec((came.shape[0], step), lambda i: (0, i))]
        + [pl.BlockSpec((size, tokens), lambda i: (i, 0)) for _ in bases],
        pl.BlockSpec((tokens, step), lambda i: (0, i)),
        jax.ShapeDtypeStruct((tokens, step * PLANES), BF),
        PLANES,
        [pltpu.VMEM((step, tokens), BF)],
    )


def shards(
    acts,
    cotan,
    frozen_key_weight,
    adapter_down_slots,
    adapter_up_slots,
    token_row_jobs,
    slot_owner_jobs,
    loss_token_count,
):
    devices = lax.axis_size("dp")
    parts = lax.axis_size("groups")
    tok_rows = acts.shape[0]
    local = adapter_down_slots.shape[0]
    jobs_all = slot_owner_jobs.shape[0]
    depth = 2 * tok_rows // (local * devices)
    column = devices // PLANES
    ring = column <= 4 and parts == 2
    most = local * column * depth
    segment = PLANES * depth
    me = lax.axis_index("dp")
    plane, place = me // column, me % column

    first = Line()
    stripes = [[p * column + c for p in range(PLANES)] for c in range(column)]
    ids = token_row_jobs[:, 0]
    lengths = loss_token_count.astype(F32)
    weights = jnp.mean(lengths) / lengths
    numbers = jnp.arange(jobs_all, dtype=jnp.int32)
    row_weight = jnp.sum(jnp.where(ids[:, None] == numbers[None, :], weights[None, :], 0.0), axis=1)
    row_slot = jnp.sum(
        jnp.where(ids[:, None] == slot_owner_jobs[None, :], numbers[None, :], 0), axis=1
    )
    scaled = (row_weight[:, None] * cotan.astype(F32)).astype(BF)

    planes = jnp.arange(PLANES, dtype=jnp.int32)
    need = jnp.max(
        jnp.sum((row_slot[:, None] // (local * column) == planes[None, :]).astype(jnp.int32), axis=0)
    )
    note = jnp.concatenate([row_slot, jnp.full((128,), need, jnp.int32)])
    share = frozen_key_weight.shape[0] // parts
    deep = frozen_key_weight.shape[1]
    own_share = lax.dynamic_slice_in_dim(
        frozen_key_weight, lax.axis_index("groups") * share, share, 0
    )
    if ring:
        shares = [own_share] + [
            lax.ppermute(
                own_share,
                "dp",
                [(d, ((d // column) ^ s) * column + d % column) for d in range(devices)],
            )
            for s in range(1, PLANES)
        ]
        first.last = [own_share]
        note = note_step(first, note[None])[0]
        near_share, far_shares = shares[1:2], shares[2:]
        shares = jnp.stack(shares)
        turn = jnp.arange(PLANES, dtype=jnp.int32) ^ plane
        weight_z = shares[0][None]
        for s in range(1, PLANES):
            weight_z = jnp.where((turn == s)[:, None, None], shares[s][None], weight_z)
    note = jnp.broadcast_to(note[None, None], (parts * devices, 1, tok_rows + 128))
    first.last = [note]
    notes = lax.all_to_all(
        note,
        ("groups", "dp"),
        split_axis=0,
        concat_axis=0,
        tiled=True,
    )[:, 0]
    need_all = jnp.max(notes[:, tok_rows])
    mine = notes[:, :tok_rows].reshape(parts, PLANES, column, tok_rows)
    mine = lax.dynamic_index_in_dim(mine, lax.axis_index("groups"), 0, keepdims=False)
    mine = lax.dynamic_index_in_dim(mine, place, 1, keepdims=False)
    slots = mine
    goal = slots // (local * column)
    earlier = jnp.arange(tok_rows)[None, :] < jnp.arange(tok_rows)[:, None]
    order = jnp.sum(
        ((goal[:, :, None] == goal[:, None, :]) & earlier[None]).astype(jnp.int32), axis=2
    )
    rank = jnp.sum(
        ((slots[:, :, None] == slots[:, None, :]) & earlier[None]).astype(jnp.int32), axis=2
    )
    owner = (slots // local) % column
    if ring:
        owner = owner ^ place
    spot = (
        owner * (local * segment)
        + (slots % local) * segment
        + planes[:, None] * depth
        + rank
    )
    spot = jnp.where(goal == plane, spot, -1)
    own_goal = row_slot // (local * column)
    own_order = jnp.sum(
        ((own_goal[:, None] == own_goal[None, :]) & earlier).astype(jnp.int32), axis=1
    )

    def across(bufs):
        return [bufs[0]] + [
            lax.ppermute(
                bufs[s],
                "dp",
                [(d, ((d // column) ^ s) * column + d % column) for d in range(devices)],
            )
            for s in range(1, PLANES)
        ]

    blocks = [[p * column + c for c in range(column)] for p in range(PLANES)]

    def within(x):
        return lax.all_to_all(
            x, "dp", split_axis=0, concat_axis=0, tiled=True, axis_index_groups=blocks
        )

    blocks_out = [local * segment] * column if ring else [column * local * segment]
    owner_outs = [segment] * column if ring else [column * segment]

    def near(bufs):
        if not ring:
            return [within(bufs[0])]
        return [bufs[0]] + [
            lax.ppermute(bufs[s], "dp", [(d, d ^ s) for d in range(devices)])
            for s in range(1, column)
        ]

    def at_owner(bufs):
        width = bufs[0].shape[1]
        if ring:
            return [x.reshape(local, segment, width) for x in bufs]
        x = bufs[0].reshape(column, local, segment, width).transpose(1, 0, 2, 3)
        return [x.reshape(local, column * segment, width)]

    def from_owner(bufs):
        width = bufs[0].shape[2]
        if ring:
            return [x.reshape(local * segment, width) for x in bufs]
        x = bufs[0].reshape(local, column, segment, width).transpose(1, 0, 2, 3)
        return [x.reshape(column * local * segment, width)]

    def planes_swap(x):
        return lax.all_to_all(
            x, "dp", split_axis=0, concat_axis=0, tiled=True, axis_index_groups=stripes
        )

    def gather_all(x, axis, groups=None):
        return lax.all_gather(x, axis, axis=0, tiled=True, axis_index_groups=groups)

    def outward(size, side):
        lanes = jnp.arange(PLANES * size, dtype=jnp.int32)
        code = side * size + own_order
        return (lanes[:, None] == code[None, :]).astype(BF), (
            code[:, None] == lanes[None, :]
        ).astype(BF)

    def inward(size, turned=False):
        kth = jnp.arange(size, dtype=jnp.int32)
        target = jnp.sum(
            jnp.where(
                (order[:, None, :] == kth[None, :, None]) & (spot[:, None, :] >= 0),
                spot[:, None, :] + 1,
                0,
            ),
            axis=2,
        )
        if turned:
            there = (planes ^ plane)[:, None, None] == planes[None, :, None]
            target = jnp.sum(jnp.where(there, target[None], 0), axis=1)
        target = target.reshape(PLANES * size) - 1
        spots = jnp.arange(PLANES * most, dtype=jnp.int32)
        return (spots[:, None] == target[None, :]).astype(BF), (
            target[:, None] == spots[None, :]
        ).astype(BF)

    rows_out = outward(most, own_goal ^ plane)[0]
    if ring:
        lanes = jnp.arange(tok_rows, dtype=jnp.int32)
        same_rows = (lanes[:, None] == lanes[None, :]).astype(BF)
        first.last += near_share
        early = route(first, same_rows, [scaled], [tok_rows])[0]
        mates = [
            early,
            *(lax.ppermute(early, "dp", [(d, d ^ s) for d in range(devices)]) for s in range(1, 3)),
        ]
        first.last += mates[1:2]
        late = route(first, same_rows, [scaled], [tok_rows])[0]
        mates += [
            lax.ppermute(late, "dp", [(d, d ^ s) for d in range(devices)])
            for s in range(3, column)
        ]
        mates = mates[:column]
        first.last += far_shares
    scaled_z = across(route(first, rows_out, [scaled], [most] * PLANES))
    steps = [most * 11 // 16, most * 13 // 16, most]
    total = PLANES * steps[0]
    usual = route(first, outward(steps[0], own_goal)[0], [acts], [total])[0]
    scaled_sent = route(first, inward(most, True)[0], scaled_z, blocks_out)

    def run(size):
        line = Line()
        total = PLANES * size
        out_rows, back_rows = outward(size, own_goal)
        spread, gather = inward(size)
        if ring:
            weight = weight_z, lax.ppermute(weight_z, "groups", [(0, 1), (1, 0)])
        else:
            weight = gather_all(frozen_key_weight, "dp")
        leaving = usual if size == steps[0] else route(line, out_rows, [acts], [total])[0]
        acts_z = planes_swap(leaving)
        got_scaled = at_owner(near(scaled_sent))
        back_low = back_project(line, adapter_up_slots, got_scaled)
        terms = adapter_terms(line, back_low, adapter_down_slots, owner_outs)
        terms = near(from_owner(terms))
        if ring:
            bases = near(base_step(line, weight, mates))
        else:
            bases = [dot(weight, scaled, 1, 1).astype(BF)]
        got = route(line, spread, [acts_z], blocks_out)
        came = planes_swap(route(line, gather, terms, [total])[0])
        got = at_owner(near(got))
        low, grad_a = owner_step(line, back_low, adapter_down_slots, got)
        grad_b = up_gradient(line, low, got_scaled)
        result = final_step(line, back_rows, came, bases)
        return result, grad_a, grad_b

    which = sum((need_all > s).astype(jnp.int32) for s in steps[:-1])
    return lax.switch(which, [functools.partial(run, s) for s in steps])


def solution(mesh):
    return jax.shard_map(
        shards,
        mesh=mesh,
        in_specs=(
            P(("groups", "dp"), None),
            P(("groups", "dp"), None),
            P("dp", None),
            P(("groups", "dp"), None, None),
            P(("groups", "dp"), None, None),
            P(("groups", "dp"), None),
            P("groups"),
            P("groups"),
        ),
        out_specs=(
            P(("groups", "dp"), None),
            P(("groups", "dp"), None, None),
            P(("groups", "dp"), None, None),
        ),
        check_vma=False,
    )
```

```python
import functools

import jax
import jax.numpy as jnp
from jax import lax
from jax.experimental import pallas as pl
from jax.experimental.pallas import tpu as pltpu
from jax.sharding import PartitionSpec as P

DELTA_MULTIPLIER = 0.25
BF = jnp.bfloat16
F32 = jnp.float32
PLANES = 4
PIECES = 4
PARAMS = pltpu.CompilerParams(vmem_limit_bytes=48 * 1024 * 1024)


def far(shape, dtype=BF):
    return pltpu.HBM(shape, dtype)


def whole(shape):
    zeros = (0,) * len(shape)
    return pl.BlockSpec(shape, lambda i: zeros)


def dot(a, b, ca=1, cb=0):
    return lax.dot_general(a, b, (((ca,), (cb,)), ((), ())), preferred_element_type=F32)


HERE = pl.BlockSpec(memory_space=pl.ANY)


def note_body(ref, out):
    out[...] = ref[...]


def note_step(line, note):
    return line.call(
        note_body,
        [note],
        [whole(note.shape)],
        whole(note.shape),
        jax.ShapeDtypeStruct(note.shape, note.dtype),
    )


def route_body(count, rows_ref, *refs):
    ins, outs = refs[:count], refs[count:]
    held = ins[0][...] if count == 1 else jnp.concatenate([r[...] for r in ins], axis=0)
    moved = dot(rows_ref[...], held).astype(BF)
    at = 0
    for out in outs:
        out[...] = moved[at : at + out.shape[0]]
        at += out.shape[0]


class Line:
    def __init__(self):
        self.last = []

    def call(self, body, operands, in_specs, out_specs, out_shape, pieces=1, scratch=()):
        after = self.last
        first = len(operands)
        many = isinstance(out_shape, list)

        def kernel(*refs):
            mark = len(refs) - 1 - len(scratch)
            refs[mark][...] = jnp.zeros_like(refs[mark])
            body(*refs[:first], *refs[first + len(after) : mark], *refs[mark + 1 :])

        out = pl.pallas_call(
            kernel,
            grid=(pieces,),
            in_specs=in_specs + [HERE] * len(after),
            out_specs=(out_specs if many else [out_specs]) + [whole((8, 128))],
            out_shape=(out_shape if many else [out_shape])
            + [jax.ShapeDtypeStruct((8, 128), jnp.int32)],
            scratch_shapes=scratch,
            compiler_params=PARAMS,
        )(*operands, *after)
        self.last = [out[-1]]
        return out[:-1] if many else out[0]


def route_body(count, rows_ref, *refs):
    ins, outs = refs[:count], refs[count:]
    held = ins[0][...] if count == 1 else jnp.concatenate([r[...] for r in ins], axis=0)
    moved = dot(rows_ref[...], held).astype(BF)
    at = 0
    for out in outs:
        out[...] = moved[at : at + out.shape[0]]
        at += out.shape[0]


class Line:
    def __init__(self):
        self.last = []

    def call(self, body, operands, in_specs, out_specs, out_shape, pieces=1, scratch=()):
        after = self.last
        first = len(operands)
        many = isinstance(out_shape, list)

        def kernel(*refs):
            mark = len(refs) - 1 - len(scratch)
            refs[mark][...] = jnp.zeros_like(refs[mark])
            body(*refs[:first], *refs[first + len(after) : mark], *refs[mark + 1 :])

        out = pl.pallas_call(
            kernel,
            grid=(pieces,),
            in_specs=in_specs + [HERE] * len(after),
            out_specs=(out_specs if many else [out_specs]) + [whole((8, 128))],
            out_shape=(out_shape if many else [out_shape])
            + [jax.ShapeDtypeStruct((8, 128), jnp.int32)],
            scratch_shapes=scratch,
            compiler_params=PARAMS,
        )(*operands, *after)
        self.last = [out[-1]]
        return out[:-1] if many else out[0]


def hold_body(ref, out):
    pass


def hold(line, x):
    last = line.last
    out = line.call(hold_body, [x], [FAR], FAR, far(x.shape, x.dtype), 1, {0: 0})
    line.last = last
    return out


def route(line, rows, ins, outs):
    width = ins[0].shape[1]
    pieces = PIECES if width % (128 * PIECES) == 0 else 1
    step = width // pieces
    return line.call(
        functools.partial(route_body, len(ins)),
        [rows, *ins],
        [whole(rows.shape)]
        + [pl.BlockSpec((x.shape[0], step), lambda i: (0, i)) for x in ins],
        [pl.BlockSpec((n, step), lambda i: (0, i)) for n in outs],
        [far((n, width)) for n in outs],
        pieces,
    )


def job_rows(refs, job):
    return jnp.concatenate([ref[job] for ref in refs], axis=0)


def back_body(count, up_ref, *refs):
    out = refs[count]
    for job in range(up_ref.shape[0]):
        held = job_rows(refs[:count], job)
        out[job] = (DELTA_MULTIPLIER * dot(held, up_ref[job], 1, 1)).astype(BF)


def back_project(line, up, rows):
    local, rank = up.shape[0], up.shape[1]
    shape = (local, sum(x.shape[1] for x in rows), rank)
    return line.call(
        functools.partial(back_body, len(rows)),
        [up, *rows],
        [whole(up.shape)] + [whole(x.shape) for x in rows],
        whole(shape),
        jax.ShapeDtypeStruct(shape, BF),
    )


def term_body(back_ref, down_ref, *outs):
    for job in range(down_ref.shape[0]):
        term = dot(back_ref[job], down_ref[job], 1, 1).astype(BF)
        at = 0
        for out in outs:
            out[job] = term[at : at + out.shape[1]]
            at += out.shape[1]


def adapter_terms(line, back_low, down, outs):
    local, width, rank = down.shape
    step = width // PIECES
    return line.call(
        term_body,
        [back_low, down],
        [whole(back_low.shape), pl.BlockSpec((local, step, rank), lambda i: (0, i, 0))],
        [pl.BlockSpec((local, n, step), lambda i: (0, 0, i)) for n in outs],
        [far((local, n, width)) for n in outs],
        PIECES,
    )


def owner_body(count, back_ref, down_ref, *refs):
    ins, (low_ref, grad_ref) = refs[:count], refs[count:]

    @pl.when(pl.program_id(0) == 0)
    def _():
        low_ref[...] = jnp.zeros_like(low_ref)

    for job in range(down_ref.shape[0]):
        held = job_rows(ins, job)
        low_ref[job] += dot(held, down_ref[job])
        grad_ref[job] = dot(held, back_ref[job], 0, 0).astype(BF)


def owner_step(line, back_low, down, rows):
    local, width, rank = down.shape
    step = width // PIECES
    part = pl.BlockSpec((local, step, rank), lambda i: (0, i, 0))
    low_shape = (local, back_low.shape[1], rank)
    return line.call(
        functools.partial(owner_body, len(rows)),
        [back_low, down, *rows],
        [whole(back_low.shape), part]
        + [pl.BlockSpec((local, x.shape[1], step), lambda i: (0, 0, i)) for x in rows],
        [whole(low_shape), part],
        [jax.ShapeDtypeStruct(low_shape, F32), jax.ShapeDtypeStruct(down.shape, BF)],
        PIECES,
    )


def up_body(count, low_ref, *refs):
    out = refs[count]
    for job in range(low_ref.shape[0]):
        low = low_ref[job].astype(BF)
        held = job_rows(refs[:count], job)
        out[job] = (DELTA_MULTIPLIER * dot(low, held, 0, 0)).astype(BF)


def up_gradient(line, low, rows):
    shape = (low.shape[0], low.shape[2], rows[0].shape[2])
    return line.call(
        functools.partial(up_body, len(rows)),
        [low, *rows],
        [whole(low.shape)] + [whole(x.shape) for x in rows],
        whole(shape),
        jax.ShapeDtypeStruct(shape, BF),
    )


def base_body(count, mine_ref, other_ref, *refs):
    ins, outs = refs[:count], refs[count:]
    lower = lax.axis_index("groups") == 0
    mine, other = mine_ref[0], other_ref[0]
    weight = jnp.concatenate(
        [jnp.where(lower, mine, other), jnp.where(lower, other, mine)], axis=0
    )
    for x, out in zip(ins, outs):
        out[...] = dot(weight, x[...], 1, 1).astype(BF)


def base_step(line, weight, rows):
    planes, share, deep = weight[0].shape
    step, tokens = 2 * share, rows[0].shape[0]
    half = pl.BlockSpec((1, share, deep), lambda i: (i, 0, 0))
    return line.call(
        functools.partial(base_body, len(rows)),
        [*weight, *rows],
        [half, half] + [whole(x.shape) for x in rows],
        [pl.BlockSpec((step, tokens), lambda i: (i, 0)) for _ in rows],
        [far((planes * step, tokens)) for _ in rows],
        planes,
    )


def final_body(count, rows_ref, came_ref, *refs):
    bases, out, held = refs[:count], refs[count], refs[count + 1]
    size = bases[0].shape[0]
    place = lax.rem(lax.axis_index("dp"), count)
    for s, ref in enumerate(bases):
        held[pl.ds(pl.multiple_of((place ^ s) * size, 16), size)] = ref[...]
    tokens = held.shape[1]
    one = (
        lax.broadcasted_iota(jnp.int32, (tokens, tokens), 0)
        == lax.broadcasted_iota(jnp.int32, (tokens, tokens), 1)
    ).astype(F32)
    base = dot(one.astype(BF), held[...], 1, 1)
    out[...] = (base + dot(rows_ref[...], came_ref[...])).astype(BF)


def final_step(line, rows, came, bases):
    tokens = rows.shape[0]
    step = came.shape[1] // PLANES
    size = step // len(bases)
    return line.call(
        functools.partial(final_body, len(bases)),
        [rows, came, *bases],
        [whole(rows.shape), pl.BlockSpec((came.shape[0], step), lambda i: (0, i))]
        + [pl.BlockSpec((size, tokens), lambda i: (i, 0)) for _ in bases],
        pl.BlockSpec((tokens, step), lambda i: (0, i)),
        jax.ShapeDtypeStruct((tokens, step * PLANES), BF),
        PLANES,
        [pltpu.VMEM((step, tokens), BF)],
    )


def shards(
    acts,
    cotan,
    frozen_key_weight,
    adapter_down_slots,
    adapter_up_slots,
    token_row_jobs,
    slot_owner_jobs,
    loss_token_count,
):
    devices = lax.axis_size("dp")
    parts = lax.axis_size("groups")
    tok_rows = acts.shape[0]
    local = adapter_down_slots.shape[0]
    jobs_all = slot_owner_jobs.shape[0]
    depth = 2 * tok_rows // (local * devices)
    column = devices // PLANES
    ring = column <= 4 and parts == 2
    most = local * column * depth
    segment = PLANES * depth
    me = lax.axis_index("dp")
    plane, place = me // column, me % column

    first = Line()
    stripes = [[p * column + c for p in range(PLANES)] for c in range(column)]
    ids = token_row_jobs[:, 0]
    lengths = loss_token_count.astype(F32)
    weights = jnp.mean(lengths) / lengths
    numbers = jnp.arange(jobs_all, dtype=jnp.int32)
    row_weight = jnp.sum(jnp.where(ids[:, None] == numbers[None, :], weights[None, :], 0.0), axis=1)
    row_slot = jnp.sum(
        jnp.where(ids[:, None] == slot_owner_jobs[None, :], numbers[None, :], 0), axis=1
    )
    scaled = (row_weight[:, None] * cotan.astype(F32)).astype(BF)

    planes = jnp.arange(PLANES, dtype=jnp.int32)
    need = jnp.max(
        jnp.sum((row_slot[:, None] // (local * column) == planes[None, :]).astype(jnp.int32), axis=0)
    )
    note = jnp.concatenate([row_slot, jnp.full((128,), need, jnp.int32)])
    share = frozen_key_weight.shape[0] // parts
    deep = frozen_key_weight.shape[1]
    own_share = lax.dynamic_slice_in_dim(
        frozen_key_weight, lax.axis_index("groups") * share, share, 0
    )
    if ring:
        shares = [own_share] + [
            lax.ppermute(
                own_share,
                "dp",
                [(d, ((d // column) ^ s) * column + d % column) for d in range(devices)],
            )
            for s in range(1, PLANES)
        ]
        first.last = [own_share]
        near_share, far_shares = shares[1:2], shares[2:]
        shares = jnp.stack(shares)
        turn = jnp.arange(PLANES, dtype=jnp.int32) ^ plane
        weight_z = shares[0][None]
        for s in range(1, PLANES):
            weight_z = jnp.where((turn == s)[:, None, None], shares[s][None], weight_z)
    earlier = jnp.arange(tok_rows)[None, :] < jnp.arange(tok_rows)[:, None]
    own_goal = row_slot // (local * column)
    own_order = jnp.sum(
        ((own_goal[:, None] == own_goal[None, :]) & earlier).astype(jnp.int32), axis=1
    )

    def across(bufs):
        return [bufs[0]] + [
            lax.ppermute(
                bufs[s],
                "dp",
                [(d, ((d // column) ^ s) * column + d % column) for d in range(devices)],
            )
            for s in range(1, PLANES)
        ]

    blocks = [[p * column + c for c in range(column)] for p in range(PLANES)]

    def within(x):
        return lax.all_to_all(
            x, "dp", split_axis=0, concat_axis=0, tiled=True, axis_index_groups=blocks
        )

    blocks_out = [local * segment] * column if ring else [column * local * segment]
    owner_outs = [segment] * column if ring else [column * segment]

    def near(bufs):
        if not ring:
            return [within(bufs[0])]
        return [bufs[0]] + [
            lax.ppermute(bufs[s], "dp", [(d, d ^ s) for d in range(devices)])
            for s in range(1, column)
        ]

    def at_owner(bufs):
        width = bufs[0].shape[1]
        if ring:
            return [x.reshape(local, segment, width) for x in bufs]
        x = bufs[0].reshape(column, local, segment, width).transpose(1, 0, 2, 3)
        return [x.reshape(local, column * segment, width)]

    def from_owner(bufs):
        width = bufs[0].shape[2]
        if ring:
            return [x.reshape(local * segment, width) for x in bufs]
        x = bufs[0].reshape(local, column, segment, width).transpose(1, 0, 2, 3)
        return [x.reshape(column * local * segment, width)]

    def planes_swap(x):
        return lax.all_to_all(
            x, "dp", split_axis=0, concat_axis=0, tiled=True, axis_index_groups=stripes
        )

    def gather_all(x, axis, groups=None):
        return lax.all_gather(x, axis, axis=0, tiled=True, axis_index_groups=groups)

    def outward(size, side):
        lanes = jnp.arange(PLANES * size, dtype=jnp.int32)
        code = side * size + own_order
        return (lanes[:, None] == code[None, :]).astype(BF), (
            code[:, None] == lanes[None, :]
        ).astype(BF)

    def inward(size, turned=False):
        kth = jnp.arange(size, dtype=jnp.int32)
        target = jnp.sum(
            jnp.where(
                (order[:, None, :] == kth[None, :, None]) & (spot[:, None, :] >= 0),
                spot[:, None, :] + 1,
                0,
            ),
            axis=2,
        )
        if turned:
            there = (planes ^ plane)[:, None, None] == planes[None, :, None]
            target = jnp.sum(jnp.where(there, target[None], 0), axis=1)
        target = target.reshape(PLANES * size) - 1
        spots = jnp.arange(PLANES * most, dtype=jnp.int32)
        return (spots[:, None] == target[None, :]).astype(BF), (
            target[:, None] == spots[None, :]
        ).astype(BF)

    rows_out = outward(most, own_goal ^ plane)[0]
    if ring:
        lanes = jnp.arange(tok_rows, dtype=jnp.int32)
        same_rows = (lanes[:, None] == lanes[None, :]).astype(BF)
        first.last += near_share
        early = route(first, same_rows, [scaled], [tok_rows])[0]
        mates = [
            early,
            *(lax.ppermute(early, "dp", [(d, d ^ s) for d in range(devices)]) for s in range(1, 3)),
        ]
        first.last += mates[1:2]
        late = route(first, same_rows, [scaled], [tok_rows])[0]
        mates += [
            lax.ppermute(late, "dp", [(d, d ^ s) for d in range(devices)])
            for s in range(3, column)
        ]
        mates = mates[:column]
        first.last += far_shares
    scaled_z = across(route(first, rows_out, [scaled], [most] * PLANES))
    if ring:
        note = note_step(first, note[None])[0]
    note = jnp.broadcast_to(note[None, None], (parts * devices, 1, tok_rows + 128))
    notes = lax.all_to_all(
        note,
        ("groups", "dp"),
        split_axis=0,
        concat_axis=0,
        tiled=True,
    )[:, 0]
    need_all = jnp.max(notes[:, tok_rows])
    mine = notes[:, :tok_rows].reshape(parts, PLANES, column, tok_rows)
    mine = lax.dynamic_index_in_dim(mine, lax.axis_index("groups"), 0, keepdims=False)
    mine = lax.dynamic_index_in_dim(mine, place, 1, keepdims=False)
    slots = mine
    goal = slots // (local * column)
    order = jnp.sum(
        ((goal[:, :, None] == goal[:, None, :]) & earlier[None]).astype(jnp.int32), axis=2
    )
    rank = jnp.sum(
        ((slots[:, :, None] == slots[:, None, :]) & earlier[None]).astype(jnp.int32), axis=2
    )
    owner = (slots // local) % column
    if ring:
        owner = owner ^ place
    spot = (
        owner * (local * segment)
        + (slots % local) * segment
        + planes[:, None] * depth
        + rank
    )
    spot = jnp.where(goal == plane, spot, -1)
    steps = [most * 11 // 16, most * 13 // 16, most]
    total = PLANES * steps[0]
    usual = route(first, outward(steps[0], own_goal)[0], [acts], [total])[0]
    scaled_sent = route(first, inward(most, True)[0], scaled_z, blocks_out)

    def run(size):
        line = Line()
        total = PLANES * size
        out_rows, back_rows = outward(size, own_goal)
        spread, gather = inward(size)
        if ring:
            weight = weight_z, lax.ppermute(weight_z, "groups", [(0, 1), (1, 0)])
        else:
            weight = gather_all(frozen_key_weight, "dp")
        leaving = usual if size == steps[0] else route(line, out_rows, [acts], [total])[0]
        acts_z = planes_swap(leaving)
        got_scaled = at_owner(near(scaled_sent))
        back_low = back_project(line, adapter_up_slots, got_scaled)
        terms = adapter_terms(line, back_low, adapter_down_slots, owner_outs)
        terms = near(from_owner(terms))
        if ring:
            bases = near(base_step(line, weight, mates))
        else:
            bases = [dot(weight, scaled, 1, 1).astype(BF)]
        got = route(line, spread, [acts_z], blocks_out)
        came = planes_swap(route(line, gather, terms, [total])[0])
        got = at_owner(near(got))
        low, grad_a = owner_step(line, back_low, adapter_down_slots, got)
        grad_b = up_gradient(line, low, got_scaled)
        result = final_step(line, back_rows, came, bases)
        return result, grad_a, grad_b

    which = sum((need_all > s).astype(jnp.int32) for s in steps[:-1])
    return lax.switch(which, [functools.partial(run, s) for s in steps])


def solution(mesh):
    return jax.shard_map(
        shards,
        mesh=mesh,
        in_specs=(
            P(("groups", "dp"), None),
            P(("groups", "dp"), None),
            P("dp", None),
            P(("groups", "dp"), None, None),
            P(("groups", "dp"), None, None),
            P(("groups", "dp"), None),
            P("groups"),
            P("groups"),
        ),
        out_specs=(
            P(("groups", "dp"), None),
            P(("groups", "dp"), None, None),
            P(("groups", "dp"), None, None),
        ),
        check_vma=False,
    )
```

```python
import functools

import jax
import jax.numpy as jnp
from jax import lax
from jax.experimental import pallas as pl
from jax.experimental.pallas import tpu as pltpu
from jax.sharding import PartitionSpec as P

DELTA_MULTIPLIER = 0.25
BF = jnp.bfloat16
F32 = jnp.float32
PLANES = 4
PIECES = 4
PARAMS = pltpu.CompilerParams(vmem_limit_bytes=48 * 1024 * 1024)


def far(shape, dtype=BF):
    return pltpu.HBM(shape, dtype)


def whole(shape):
    zeros = (0,) * len(shape)
    return pl.BlockSpec(shape, lambda i: zeros)


def dot(a, b, ca=1, cb=0):
    return lax.dot_general(a, b, (((ca,), (cb,)), ((), ())), preferred_element_type=F32)


HERE = pl.BlockSpec(memory_space=pl.ANY)


def note_body(ref, out):
    out[...] = ref[...]


def note_step(line, note):
    return line.call(
        note_body,
        [note],
        [whole(note.shape)],
        whole(note.shape),
        jax.ShapeDtypeStruct(note.shape, note.dtype),
    )


def route_body(count, rows_ref, *refs):
    ins, outs = refs[:count], refs[count:]
    held = ins[0][...] if count == 1 else jnp.concatenate([r[...] for r in ins], axis=0)
    moved = dot(rows_ref[...], held).astype(BF)
    at = 0
    for out in outs:
        out[...] = moved[at : at + out.shape[0]]
        at += out.shape[0]


class Line:
    def __init__(self):
        self.last = []

    def call(self, body, operands, in_specs, out_specs, out_shape, pieces=1, scratch=()):
        after = self.last
        first = len(operands)
        many = isinstance(out_shape, list)

        def kernel(*refs):
            mark = len(refs) - 1 - len(scratch)
            refs[mark][...] = jnp.zeros_like(refs[mark])
            body(*refs[:first], *refs[first + len(after) : mark], *refs[mark + 1 :])

        out = pl.pallas_call(
            kernel,
            grid=(pieces,),
            in_specs=in_specs + [HERE] * len(after),
            out_specs=(out_specs if many else [out_specs]) + [whole((8, 128))],
            out_shape=(out_shape if many else [out_shape])
            + [jax.ShapeDtypeStruct((8, 128), jnp.int32)],
            scratch_shapes=scratch,
            compiler_params=PARAMS,
        )(*operands, *after)
        self.last = [out[-1]]
        return out[:-1] if many else out[0]


def route_body(count, rows_ref, *refs):
    ins, outs = refs[:count], refs[count:]
    held = ins[0][...] if count == 1 else jnp.concatenate([r[...] for r in ins], axis=0)
    moved = dot(rows_ref[...], held).astype(BF)
    at = 0
    for out in outs:
        out[...] = moved[at : at + out.shape[0]]
        at += out.shape[0]


class Line:
    def __init__(self):
        self.last = []

    def call(self, body, operands, in_specs, out_specs, out_shape, pieces=1, scratch=()):
        after = self.last
        first = len(operands)
        many = isinstance(out_shape, list)

        def kernel(*refs):
            mark = len(refs) - 1 - len(scratch)
            refs[mark][...] = jnp.zeros_like(refs[mark])
            body(*refs[:first], *refs[first + len(after) : mark], *refs[mark + 1 :])

        out = pl.pallas_call(
            kernel,
            grid=(pieces,),
            in_specs=in_specs + [HERE] * len(after),
            out_specs=(out_specs if many else [out_specs]) + [whole((8, 128))],
            out_shape=(out_shape if many else [out_shape])
            + [jax.ShapeDtypeStruct((8, 128), jnp.int32)],
            scratch_shapes=scratch,
            compiler_params=PARAMS,
        )(*operands, *after)
        self.last = [out[-1]]
        return out[:-1] if many else out[0]


def hold_body(ref, out):
    pass


def hold(line, x):
    last = line.last
    out = line.call(hold_body, [x], [FAR], FAR, far(x.shape, x.dtype), 1, {0: 0})
    line.last = last
    return out


def route(line, rows, ins, outs):
    width = ins[0].shape[1]
    pieces = PIECES if width % (128 * PIECES) == 0 else 1
    step = width // pieces
    return line.call(
        functools.partial(route_body, len(ins)),
        [rows, *ins],
        [whole(rows.shape)]
        + [pl.BlockSpec((x.shape[0], step), lambda i: (0, i)) for x in ins],
        [pl.BlockSpec((n, step), lambda i: (0, i)) for n in outs],
        [far((n, width)) for n in outs],
        pieces,
    )


def job_rows(refs, job):
    return jnp.concatenate([ref[job] for ref in refs], axis=0)


def back_body(count, up_ref, *refs):
    out = refs[count]
    for job in range(up_ref.shape[0]):
        held = job_rows(refs[:count], job)
        out[job] = (DELTA_MULTIPLIER * dot(held, up_ref[job], 1, 1)).astype(BF)


def back_project(line, up, rows):
    local, rank = up.shape[0], up.shape[1]
    shape = (local, sum(x.shape[1] for x in rows), rank)
    return line.call(
        functools.partial(back_body, len(rows)),
        [up, *rows],
        [whole(up.shape)] + [whole(x.shape) for x in rows],
        whole(shape),
        jax.ShapeDtypeStruct(shape, BF),
    )


def term_body(back_ref, down_ref, *outs):
    for job in range(down_ref.shape[0]):
        term = dot(back_ref[job], down_ref[job], 1, 1).astype(BF)
        at = 0
        for out in outs:
            out[job] = term[at : at + out.shape[1]]
            at += out.shape[1]


def adapter_terms(line, back_low, down, outs):
    local, width, rank = down.shape
    step = width // PIECES
    return line.call(
        term_body,
        [back_low, down],
        [whole(back_low.shape), pl.BlockSpec((local, step, rank), lambda i: (0, i, 0))],
        [pl.BlockSpec((local, n, step), lambda i: (0, 0, i)) for n in outs],
        [far((local, n, width)) for n in outs],
        PIECES,
    )


def owner_body(count, back_ref, down_ref, *refs):
    ins, (low_ref, grad_ref) = refs[:count], refs[count:]

    @pl.when(pl.program_id(0) == 0)
    def _():
        low_ref[...] = jnp.zeros_like(low_ref)

    for job in range(down_ref.shape[0]):
        held = job_rows(ins, job)
        low_ref[job] += dot(held, down_ref[job])
        grad_ref[job] = dot(held, back_ref[job], 0, 0).astype(BF)


def owner_step(line, back_low, down, rows):
    local, width, rank = down.shape
    step = width // PIECES
    part = pl.BlockSpec((local, step, rank), lambda i: (0, i, 0))
    low_shape = (local, back_low.shape[1], rank)
    return line.call(
        functools.partial(owner_body, len(rows)),
        [back_low, down, *rows],
        [whole(back_low.shape), part]
        + [pl.BlockSpec((local, x.shape[1], step), lambda i: (0, 0, i)) for x in rows],
        [whole(low_shape), part],
        [jax.ShapeDtypeStruct(low_shape, F32), jax.ShapeDtypeStruct(down.shape, BF)],
        PIECES,
    )


def up_body(count, low_ref, *refs):
    out = refs[count]
    for job in range(low_ref.shape[0]):
        low = low_ref[job].astype(BF)
        held = job_rows(refs[:count], job)
        out[job] = (DELTA_MULTIPLIER * dot(low, held, 0, 0)).astype(BF)


def up_gradient(line, low, rows):
    shape = (low.shape[0], low.shape[2], rows[0].shape[2])
    return line.call(
        functools.partial(up_body, len(rows)),
        [low, *rows],
        [whole(low.shape)] + [whole(x.shape) for x in rows],
        whole(shape),
        jax.ShapeDtypeStruct(shape, BF),
    )


def base_body(count, mine_ref, other_ref, *refs):
    ins, outs = refs[:count], refs[count:]
    lower = lax.axis_index("groups") == 0
    mine, other = mine_ref[0], other_ref[0]
    weight = jnp.concatenate(
        [jnp.where(lower, mine, other), jnp.where(lower, other, mine)], axis=0
    )
    for x, out in zip(ins, outs):
        out[...] = dot(weight, x[...], 1, 1).astype(BF)


def base_step(line, weight, rows):
    planes, share, deep = weight[0].shape
    step, tokens = 2 * share, rows[0].shape[0]
    half = pl.BlockSpec((1, share, deep), lambda i: (i, 0, 0))
    return line.call(
        functools.partial(base_body, len(rows)),
        [*weight, *rows],
        [half, half] + [whole(x.shape) for x in rows],
        [pl.BlockSpec((step, tokens), lambda i: (i, 0)) for _ in rows],
        [far((planes * step, tokens)) for _ in rows],
        planes,
    )


def final_body(count, rows_ref, came_ref, *refs):
    bases, out, held = refs[:count], refs[count], refs[count + 1]
    size = bases[0].shape[0]
    place = lax.rem(lax.axis_index("dp"), count)
    for s, ref in enumerate(bases):
        held[pl.ds(pl.multiple_of((place ^ s) * size, 16), size)] = ref[...]
    tokens = held.shape[1]
    one = (
        lax.broadcasted_iota(jnp.int32, (tokens, tokens), 0)
        == lax.broadcasted_iota(jnp.int32, (tokens, tokens), 1)
    ).astype(F32)
    base = dot(one.astype(BF), held[...], 1, 1)
    out[...] = (base + dot(rows_ref[...], came_ref[...])).astype(BF)


def final_step(line, rows, came, bases):
    tokens = rows.shape[0]
    step = came.shape[1] // PLANES
    size = step // len(bases)
    return line.call(
        functools.partial(final_body, len(bases)),
        [rows, came, *bases],
        [whole(rows.shape), pl.BlockSpec((came.shape[0], step), lambda i: (0, i))]
        + [pl.BlockSpec((size, tokens), lambda i: (i, 0)) for _ in bases],
        pl.BlockSpec((tokens, step), lambda i: (0, i)),
        jax.ShapeDtypeStruct((tokens, step * PLANES), BF),
        PLANES,
        [pltpu.VMEM((step, tokens), BF)],
    )


def shards(
    acts,
    cotan,
    frozen_key_weight,
    adapter_down_slots,
    adapter_up_slots,
    token_row_jobs,
    slot_owner_jobs,
    loss_token_count,
):
    devices = lax.axis_size("dp")
    parts = lax.axis_size("groups")
    tok_rows = acts.shape[0]
    local = adapter_down_slots.shape[0]
    jobs_all = slot_owner_jobs.shape[0]
    depth = 2 * tok_rows // (local * devices)
    column = devices // PLANES
    ring = column <= 4 and parts == 2
    most = local * column * depth
    segment = PLANES * depth
    me = lax.axis_index("dp")
    plane, place = me // column, me % column

    first = Line()
    stripes = [[p * column + c for p in range(PLANES)] for c in range(column)]
    ids = token_row_jobs[:, 0]
    lengths = loss_token_count.astype(F32)
    weights = jnp.mean(lengths) / lengths
    numbers = jnp.arange(jobs_all, dtype=jnp.int32)
    row_weight = jnp.sum(jnp.where(ids[:, None] == numbers[None, :], weights[None, :], 0.0), axis=1)
    row_slot = jnp.sum(
        jnp.where(ids[:, None] == slot_owner_jobs[None, :], numbers[None, :], 0), axis=1
    )
    scaled = (row_weight[:, None] * cotan.astype(F32)).astype(BF)

    planes = jnp.arange(PLANES, dtype=jnp.int32)
    need = jnp.max(
        jnp.sum((row_slot[:, None] // (local * column) == planes[None, :]).astype(jnp.int32), axis=0)
    )
    note = jnp.concatenate([row_slot, jnp.full((128,), need, jnp.int32)])
    share = frozen_key_weight.shape[0] // parts
    deep = frozen_key_weight.shape[1]
    own_share = lax.dynamic_slice_in_dim(
        frozen_key_weight, lax.axis_index("groups") * share, share, 0
    )
    if ring:
        shares = [own_share] + [
            lax.ppermute(
                own_share,
                "dp",
                [(d, ((d // column) ^ s) * column + d % column) for d in range(devices)],
            )
            for s in range(1, PLANES)
        ]
        first.last = [own_share]
        near_share, far_shares = shares[1:2], shares[2:]
        shares = jnp.stack(shares)
        turn = jnp.arange(PLANES, dtype=jnp.int32) ^ plane
        weight_z = shares[0][None]
        for s in range(1, PLANES):
            weight_z = jnp.where((turn == s)[:, None, None], shares[s][None], weight_z)
    earlier = jnp.arange(tok_rows)[None, :] < jnp.arange(tok_rows)[:, None]
    own_goal = row_slot // (local * column)
    own_order = jnp.sum(
        ((own_goal[:, None] == own_goal[None, :]) & earlier).astype(jnp.int32), axis=1
    )

    def across(bufs):
        return [bufs[0]] + [
            lax.ppermute(
                bufs[s],
                "dp",
                [(d, ((d // column) ^ s) * column + d % column) for d in range(devices)],
            )
            for s in range(1, PLANES)
        ]

    blocks = [[p * column + c for c in range(column)] for p in range(PLANES)]

    def within(x):
        return lax.all_to_all(
            x, "dp", split_axis=0, concat_axis=0, tiled=True, axis_index_groups=blocks
        )

    blocks_out = [local * segment] * column if ring else [column * local * segment]
    owner_outs = [segment] * column if ring else [column * segment]

    def near(bufs):
        if not ring:
            return [within(bufs[0])]
        return [bufs[0]] + [
            lax.ppermute(bufs[s], "dp", [(d, d ^ s) for d in range(devices)])
            for s in range(1, column)
        ]

    def at_owner(bufs):
        width = bufs[0].shape[1]
        if ring:
            return [x.reshape(local, segment, width) for x in bufs]
        x = bufs[0].reshape(column, local, segment, width).transpose(1, 0, 2, 3)
        return [x.reshape(local, column * segment, width)]

    def from_owner(bufs):
        width = bufs[0].shape[2]
        if ring:
            return [x.reshape(local * segment, width) for x in bufs]
        x = bufs[0].reshape(local, column, segment, width).transpose(1, 0, 2, 3)
        return [x.reshape(column * local * segment, width)]

    def planes_swap(x):
        return lax.all_to_all(
            x, "dp", split_axis=0, concat_axis=0, tiled=True, axis_index_groups=stripes
        )

    def gather_all(x, axis, groups=None):
        return lax.all_gather(x, axis, axis=0, tiled=True, axis_index_groups=groups)

    def outward(size, side):
        lanes = jnp.arange(PLANES * size, dtype=jnp.int32)
        code = side * size + own_order
        return (lanes[:, None] == code[None, :]).astype(BF), (
            code[:, None] == lanes[None, :]
        ).astype(BF)

    def inward(size, turned=False):
        kth = jnp.arange(size, dtype=jnp.int32)
        target = jnp.sum(
            jnp.where(
                (order[:, None, :] == kth[None, :, None]) & (spot[:, None, :] >= 0),
                spot[:, None, :] + 1,
                0,
            ),
            axis=2,
        )
        if turned:
            there = (planes ^ plane)[:, None, None] == planes[None, :, None]
            target = jnp.sum(jnp.where(there, target[None], 0), axis=1)
        target = target.reshape(PLANES * size) - 1
        spots = jnp.arange(PLANES * most, dtype=jnp.int32)
        return (spots[:, None] == target[None, :]).astype(BF), (
            target[:, None] == spots[None, :]
        ).astype(BF)

    rows_out = outward(most, own_goal ^ plane)[0]
    if ring:
        lanes = jnp.arange(tok_rows, dtype=jnp.int32)
        same_rows = (lanes[:, None] == lanes[None, :]).astype(BF)
        first.last += near_share
        early = route(first, same_rows, [scaled], [tok_rows])[0]
        mates = [
            early,
            *(lax.ppermute(early, "dp", [(d, d ^ s) for d in range(devices)]) for s in range(1, 3)),
        ]
        first.last += mates[1:2]
        late = route(first, same_rows, [scaled], [tok_rows])[0]
        mates += [
            lax.ppermute(late, "dp", [(d, d ^ s) for d in range(devices)])
            for s in range(3, column)
        ]
        mates = mates[:column]
        first.last += far_shares
    scaled_z = across(route(first, rows_out, [scaled], [most] * PLANES))
    if ring:
        note = note_step(first, note[None])[0]
    note = jnp.broadcast_to(note[None, None], (parts * devices, 1, tok_rows + 128))
    notes = lax.all_to_all(
        note,
        ("groups", "dp"),
        split_axis=0,
        concat_axis=0,
        tiled=True,
    )[:, 0]
    need_all = jnp.max(notes[:, tok_rows])
    mine = notes[:, :tok_rows].reshape(parts, PLANES, column, tok_rows)
    mine = lax.dynamic_index_in_dim(mine, lax.axis_index("groups"), 0, keepdims=False)
    mine = lax.dynamic_index_in_dim(mine, place, 1, keepdims=False)
    slots = mine
    goal = slots // (local * column)
    order = jnp.sum(
        ((goal[:, :, None] == goal[:, None, :]) & earlier[None]).astype(jnp.int32), axis=2
    )
    rank = jnp.sum(
        ((slots[:, :, None] == slots[:, None, :]) & earlier[None]).astype(jnp.int32), axis=2
    )
    owner = (slots // local) % column
    if ring:
        owner = owner ^ place
    spot = (
        owner * (local * segment)
        + (slots % local) * segment
        + planes[:, None] * depth
        + rank
    )
    spot = jnp.where(goal == plane, spot, -1)
    steps = [most * 11 // 16, most * 3 // 4, most * 13 // 16, most]
    total = PLANES * steps[0]
    usual = route(first, outward(steps[0], own_goal)[0], [acts], [total])[0]
    scaled_sent = route(first, inward(most, True)[0], scaled_z, blocks_out)

    def run(size):
        line = Line()
        total = PLANES * size
        out_rows, back_rows = outward(size, own_goal)
        spread, gather = inward(size)
        if ring:
            weight = weight_z, lax.ppermute(weight_z, "groups", [(0, 1), (1, 0)])
        else:
            weight = gather_all(frozen_key_weight, "dp")
        leaving = usual if size == steps[0] else route(line, out_rows, [acts], [total])[0]
        acts_z = planes_swap(leaving)
        got_scaled = at_owner(near(scaled_sent))
        back_low = back_project(line, adapter_up_slots, got_scaled)
        terms = adapter_terms(line, back_low, adapter_down_slots, owner_outs)
        terms = near(from_owner(terms))
        if ring:
            bases = near(base_step(line, weight, mates))
        else:
            bases = [dot(weight, scaled, 1, 1).astype(BF)]
        got = route(line, spread, [acts_z], blocks_out)
        came = planes_swap(route(line, gather, terms, [total])[0])
        got = at_owner(near(got))
        low, grad_a = owner_step(line, back_low, adapter_down_slots, got)
        grad_b = up_gradient(line, low, got_scaled)
        result = final_step(line, back_rows, came, bases)
        return result, grad_a, grad_b

    which = sum((need_all > s).astype(jnp.int32) for s in steps[:-1])
    return lax.switch(which, [functools.partial(run, s) for s in steps])


def solution(mesh):
    return jax.shard_map(
        shards,
        mesh=mesh,
        in_specs=(
            P(("groups", "dp"), None),
            P(("groups", "dp"), None),
            P("dp", None),
            P(("groups", "dp"), None, None),
            P(("groups", "dp"), None, None),
            P(("groups", "dp"), None),
            P("groups"),
            P("groups"),
        ),
        out_specs=(
            P(("groups", "dp"), None),
            P(("groups", "dp"), None, None),
            P(("groups", "dp"), None, None),
        ),
        check_vma=False,
    )
```
